32 devices in a mesh: seq: 16 (over z, y, x), blk: 2 (over core).
Axes of the slice: x: 2, y: 2, z: 4, core: 2. Of those that a mesh axis runs over, the one named last changes fastest.
Arguments:
- tokens: bfloat16 [16, 1024, 768], P('seq', 'blk'), may hold values from -6 to 6
- image_lengths: int32 [16, 6], P('seq'), may hold values from 0 to 960, as said below
- cotangent: bfloat16 [16, 1024, 768], P('seq', 'blk'), may hold values from -8 to 8
- ln1_gain: bfloat16 [768], replicated, may hold values from 0.5 to 2
- ln1_bias: bfloat16 [768], replicated, may hold values from -3 to 3
- w_query: bfloat16 [768, 768], replicated, may hold values from -0.21875 to 0.21875
- b_query: bfloat16 [768], replicated, may hold values from -3 to 3
- w_key: bfloat16 [768, 768], replicated, may hold values from -0.21875 to 0.21875
- w_value: bfloat16 [768, 768], replicated, may hold values from -0.21875 to 0.21875
- b_value: bfloat16 [768], replicated, may hold values from -3 to 3
- q_gain: bfloat16 [768], replicated, may hold values from 0.5 to 2
- k_gain: bfloat16 [768], replicated, may hold values from 0.5 to 2
- w_out: bfloat16 [768, 768], replicated, may hold values from -1.75 to 1.75
- b_out: bfloat16 [768], replicated, may hold values from -1.75 to 1.75
- ln2_gain: bfloat16 [768], replicated, may hold values from 0.5 to 2
- ln2_bias: bfloat16 [768], replicated, may hold values from -3 to 3
- w_up: bfloat16 [768, 3072], replicated, may hold values from -0.21875 to 0.21875
- b_up: bfloat16 [3072], replicated, may hold values from -3 to 3
- w_down: bfloat16 [3072, 768], replicated, may hold values from -0.109375 to 0.109375
- b_down: bfloat16 [768], replicated, may hold values from -1.75 to 1.75
Outputs:
- layer_out: bfloat16 [16, 1024, 768], P('seq', 'blk')
- grad_tokens: float32 [16, 1024, 768], P('seq', 'blk')
- grad_ln1_gain: float32 [768], P('seq')
- grad_ln1_bias: float32 [768], P('seq')
- grad_w_query: float32 [768, 768], P('seq')
- grad_b_query: float32 [768], P('seq')
- grad_w_key: float32 [768, 768], P('seq')
- grad_w_value: float32 [768, 768], P('seq')
- grad_b_value: float32 [768], P('seq')
- grad_q_gain: float32 [768], P('seq')
- grad_k_gain: float32 [768], P('seq')
- grad_w_out: float32 [768, 768], P('seq')
- grad_b_out: float32 [768], P('seq')
- grad_ln2_gain: float32 [768], P('seq')
- grad_ln2_bias: float32 [768], P('seq')
- grad_w_up: float32 [768, 3072], P('seq')
- grad_b_up: float32 [3072], P('seq')
- grad_w_down: float32 [3072, 768], P('seq')
- grad_b_down: float32 [768], P('seq')
The draws below stay inside these ranges and needn't reach their ends.
Inputs may be any that keep to these rules, and one draw needn't show every extreme that they name: `image_lengths`: images fill a sequence from its start in slot order, and the patches after their sum are padding. Among the 1 sequence of each index of seq, exactly one holds an image of at most 64 patches in slot 0, then one of 960 patches in slot 1, and zeros in the other slots; every other image has fewer than 256 patches.
All inputs are finite; a program needn't handle non-finite values.
Results may differ from the reference program's by a relative error of at most 0.02.
Values may be sent and summed in bfloat16 or wider, within the bound.
No kernel may reach another device: no remote copies, remote signals or barrier semaphores. Data moves between devices by JAX's collectives and lax.ppermute only.
A program may use at most 192 MiB of HBM per device.

```python
import math
import jax
import jax.numpy as jnp
from jax import lax

D = 768
H = 12
HD = 64
FF = 3072
LEN = 1024
NIMG = 6
SEQS = 1
NSEQ = 16
N_BLK = 2


def draw_image_lengths(key, part):
    key = jax.random.fold_in(key, 11)
    pick_key, size_key, lead_key = jax.random.split(key, 3)
    sizes = jax.random.randint(size_key, (NSEQ, NIMG), LEN // 16, LEN // 4, dtype=jnp.int32)
    image_ends = jnp.cumsum(sizes, axis=1)
    kept = jnp.where(image_ends <= LEN, sizes, 0)
    picks = jax.random.randint(pick_key, (NSEQ // SEQS,), 0, SEQS, dtype=jnp.int32)
    leads = jax.random.randint(lead_key, (NSEQ,), 1, LEN // 16 + 1, dtype=jnp.int32)
    row_ids = jnp.arange(NSEQ, dtype=jnp.int32)
    spanning = row_ids % SEQS == picks[row_ids // SEQS]
    slot_ids = jnp.arange(NIMG, dtype=jnp.int32)
    span_rows = jnp.where(slot_ids[None, :] == 0, leads[:, None], jnp.where(slot_ids[None, :] == 1, LEN - LEN // 16, 0))
    return jnp.where(spanning[:, None], span_rows, kept).astype(jnp.int32)


def with_spikes(values, stream_key, source, target, parts, factor):
    owner, partner = [(jnp.arange(values.shape[position]) // (values.shape[position] // parts)).reshape([-1 if axis == position else 1 for axis in range(values.ndim)]) for position in (source, target)]
    chosen = jax.random.permutation(stream_key, parts)[partner]
    strong = (owner == chosen) | (owner == (partner + parts // 2) % parts)
    return jnp.where(strong, factor * values, values)


def block_scale(key, shape, cuts, low, high):
    def one(dim, blocks):
        steps = jax.random.uniform(jax.random.fold_in(jax.random.fold_in(key, 6), dim), (blocks,), jnp.float32, low / len(cuts), high / len(cuts))
        return jnp.repeat(jnp.exp(steps), shape[dim] // blocks).reshape((-1,) + (1,) * (len(shape) - dim - 1))

    loudness = one(*cuts[0])
    for cut in cuts[1:]:
        loudness = loudness * one(*cut)
    return loudness


def normal_values(stream_key, extent, deviation, bound, cuts=(), held_as=jnp.bfloat16):
    factor_of = block_scale(stream_key, extent, cuts, -0.22, 0.18) if cuts else 1.0
    entries = jax.random.normal(stream_key, extent, jnp.float32) * deviation * factor_of
    return jnp.minimum(jnp.maximum(entries, -bound), bound).astype(held_as)


def gaussian_with(key, shape, spread, reach, cuts, heavy, kind=jnp.bfloat16):
    values = spread * jax.random.normal(key, shape, jnp.float32)
    if cuts:
        values = values * block_scale(key, shape, cuts, -0.22, 0.18)
    return jnp.clip(with_spikes(values, jax.random.fold_in(key, 3), *heavy), -reach, reach).astype(kind)


def setup_inputs(seed: int = 0) -> dict:
    arg_keys = jax.random.split(jax.random.key(seed), 21)
    return {
        "tokens": normal_values(arg_keys[0], (NSEQ, LEN, D), 1.0, 6.0, ((0, 16), (1, 2))),
        "image_lengths": draw_image_lengths(jax.random.fold_in(arg_keys[20], 71), 0),
        "cotangent": gaussian_with(arg_keys[2], (NSEQ, LEN, D), 1.0, 8.0, ((0, 16), (1, 2)), (0, 2, 16, 2.0)),
        "ln1_gain": jnp.clip(jnp.exp(jax.random.uniform(arg_keys[3], (D,), jnp.float32, math.log(0.5), math.log(2.0))), 0.5, 2.0).astype(jnp.bfloat16),
        "ln1_bias": normal_values(arg_keys[4], (D,), 0.5, 3.0),
        "w_query": normal_values(arg_keys[5], (D, D), D ** -0.5, 0.21875),
        "b_query": normal_values(arg_keys[6], (D,), 0.5, 3.0),
        "w_key": normal_values(arg_keys[7], (D, D), D ** -0.5, 0.21875),
        "w_value": normal_values(arg_keys[8], (D, D), D ** -0.5, 0.21875),
        "b_value": normal_values(arg_keys[9], (D,), 0.5, 3.0),
        "q_gain": jnp.clip(jnp.exp(jax.random.uniform(arg_keys[10], (D,), jnp.float32, math.log(0.5), math.log(2.0))), 0.5, 2.0).astype(jnp.bfloat16),
        "k_gain": jnp.clip(jnp.exp(jax.random.uniform(arg_keys[11], (D,), jnp.float32, math.log(0.5), math.log(2.0))), 0.5, 2.0).astype(jnp.bfloat16),
        "w_out": normal_values(arg_keys[12], (D, D), (max(D // 64, 1)) ** -0.5, 1.75),
        "b_out": normal_values(arg_keys[13], (D,), 0.3, 1.75),
        "ln2_gain": jnp.clip(jnp.exp(jax.random.uniform(arg_keys[14], (D,), jnp.float32, math.log(0.5), math.log(2.0))), 0.5, 2.0).astype(jnp.bfloat16),
        "ln2_bias": normal_values(arg_keys[15], (D,), 0.5, 3.0),
        "w_up": normal_values(arg_keys[16], (D, FF), D ** -0.5, 0.21875),
        "b_up": normal_values(arg_keys[17], (FF,), 0.5, 3.0),
        "w_down": normal_values(arg_keys[18], (FF, D), FF ** -0.5, 0.109375),
        "b_down": normal_values(arg_keys[19], (D,), 0.3, 1.75),
    }


@jax.custom_vjp
def low(v):
    return lax.optimization_barrier(v.astype(jnp.bfloat16)).astype(jnp.float32)

@jax.custom_vjp
def low_back(v):
    return v

def low_keep(v):
    return (low(v), None)

def low_pass(kept, grad):
    return (grad,)

def back_keep(v):
    return (v, None)

def back_low(kept, grad):
    return (low(grad),)
low.defvjp(low_keep, low_pass)
low_back.defvjp(back_keep, back_low)
EPSILON = 1e-06
NEGATIVE = -1e+30
PRECISE = lax.Precision.HIGHEST

def normalize(values):
    average = lax.optimization_barrier(jnp.mean(values, axis=-1, keepdims=True))
    centred = values - average
    variance = lax.optimization_barrier(jnp.mean(centred * centred, axis=-1, keepdims=True))
    return centred * lax.rsqrt(variance + EPSILON)

def head_norm(values):
    per_head = values.reshape(values.shape[:-1] + (H, HD))
    return normalize(per_head).reshape(values.shape)

def project(operand, weight):
    return jnp.einsum('gtd,de->gte', operand, weight, precision=PRECISE, preferred_element_type=jnp.float32)

def segment_ids(lengths, positions):
    image_ends = jnp.cumsum(lengths, axis=-1).astype(jnp.int32)
    inside = positions[None, :, None] >= image_ends[:, None, :]
    segments = lax.optimization_barrier(jnp.sum(inside.astype(jnp.int32), axis=-1)).astype(jnp.int32)
    return jnp.where(positions[None, :] < image_ends[:, -1:], segments, -1).astype(jnp.int32)

def attend(query_low, key_low, value_low, segments):
    span_len = LEN // N_BLK
    allowed = (segments[:, None] == segments[None, :]) & (segments[:, None] >= 0)
    allowed = allowed.reshape(N_BLK, 1, span_len, LEN)
    queries = query_low.reshape(N_BLK, span_len, H, HD)
    key_copies = low_back(jnp.broadcast_to(key_low[None], (N_BLK, LEN, D))).reshape(N_BLK, LEN, H, HD)
    value_copies = low_back(jnp.broadcast_to(value_low[None], (N_BLK, LEN, D))).reshape(N_BLK, LEN, H, HD)
    scores = low_back(jnp.einsum('cqhe,ckhe->chqk', queries, key_copies, precision=PRECISE) / math.sqrt(HD))
    masked = jnp.where(allowed, scores, NEGATIVE)
    row_top = lax.optimization_barrier(jnp.max(masked, axis=-1, keepdims=True))
    lifted = jnp.where(allowed, jnp.exp(masked - row_top), 0.0)
    row_total = lax.optimization_barrier(jnp.sum(lifted, axis=-1, keepdims=True))
    probs_low = low(lifted / jnp.maximum(row_total, 1.0))
    attended = jnp.einsum('chqk,ckhe->cqhe', probs_low, value_copies, precision=PRECISE)
    return attended.reshape(LEN, D)

def forward(params, inputs, segments):
    ln1_gain, ln1_bias, w_query, b_query, w_key, w_value, b_value, q_gain, k_gain, w_out, b_out, ln2_gain, ln2_bias, w_up, b_up, w_down, b_down = params
    act_one = low(normalize(inputs) * ln1_gain + ln1_bias)
    query_pre = low_back(project(act_one, w_query) + b_query)
    key_pre = low_back(project(act_one, w_key))
    value_low = low(low_back(project(act_one, w_value) + b_value))
    query_low = low(head_norm(query_pre) * q_gain)
    key_low = low(head_norm(key_pre) * k_gain)
    checked = jax.checkpoint(attend)
    attended = lax.map(lambda pieces: checked(*pieces), (query_low, key_low, value_low, segments))
    attended = low(low_back(attended))
    branch = low_back(project(attended, w_out) + b_out)
    resid = inputs + branch
    act_two = low(normalize(resid) * ln2_gain + ln2_bias)
    pre_up = low_back(project(act_two, w_up) + b_up)
    hidden = low(jax.nn.gelu(pre_up, approximate=False))
    return resid + project(hidden, w_down) + b_down

def reference(tokens, image_lengths, cotangent, ln1_gain, ln1_bias, w_query, b_query, w_key, w_value, b_value, q_gain, k_gain, w_out, b_out, ln2_gain, ln2_bias, w_up, b_up, w_down, b_down):
    params = tuple((param.astype(jnp.float32) for param in (ln1_gain, ln1_bias, w_query, b_query, w_key, w_value, b_value, q_gain, k_gain, w_out, b_out, ln2_gain, ln2_bias, w_up, b_up, w_down, b_down)))
    group_size = math.gcd(NSEQ, 4)
    group_count = NSEQ // group_size
    inputs_all = tokens.astype(jnp.float32).reshape(group_count, group_size, LEN, D)
    cot_all = cotangent.astype(jnp.float32).reshape(group_count, group_size, LEN, D)
    lengths_all = image_lengths.reshape(group_count, group_size, NIMG)
    positions = jnp.arange(LEN, dtype=jnp.int32)

    def one_group(totals, pieces):
        inputs_grp, cot_grp, lengths_grp = pieces
        segments = segment_ids(lengths_grp, positions)
        result, pullback = jax.vjp(lambda params_in, inputs_in: forward(params_in, inputs_in, segments), params, inputs_grp)
        grad_params, grad_inputs = pullback(cot_grp)
        totals = tuple((total + extra for total, extra in zip(totals, grad_params)))
        return (totals, (result.astype(jnp.bfloat16), grad_inputs))
    zero_grads = tuple((jnp.zeros(param.shape, jnp.float32) for param in params))
    totals, (outputs, grad_rows) = lax.scan(one_group, zero_grads, (inputs_all, cot_all, lengths_all))
    layer_out = outputs.reshape(NSEQ, LEN, D)
    grad_tokens = grad_rows.reshape(NSEQ, LEN, D)
    grad_ln1_gain, grad_ln1_bias, grad_w_query, grad_b_query, grad_w_key, grad_w_value, grad_b_value, grad_q_gain, grad_k_gain, grad_w_out, grad_b_out, grad_ln2_gain, grad_ln2_bias, grad_w_up, grad_b_up, grad_w_down, grad_b_down = totals
    return (layer_out, grad_tokens, grad_ln1_gain, grad_ln1_bias, grad_w_query, grad_b_query, grad_w_key, grad_w_value, grad_b_value, grad_q_gain, grad_k_gain, grad_w_out, grad_b_out, grad_ln2_gain, grad_ln2_bias, grad_w_up, grad_b_up, grad_w_down, grad_b_down)
```

```python
import math

import jax
import jax.numpy as jnp
from jax import lax
from jax.sharding import PartitionSpec as P

H = 12
HD = 64


EPSILON = 1e-06
NEGATIVE = -1e30


def normalize(values):
    average = jnp.mean(values, axis=-1, keepdims=True)
    centred = values - average
    variance = jnp.mean(centred * centred, axis=-1, keepdims=True)
    return centred * lax.rsqrt(variance + EPSILON)


def head_norm(values):
    per_head = values.reshape(values.shape[:-1] + (H, HD))
    return normalize(per_head).reshape(values.shape)


def gelu_exact(values):
    return jax.nn.gelu(values, approximate=False)


def split_heads(values):
    return values.reshape(values.shape[0], values.shape[1], H, HD)


def project(operand, weight):
    return jnp.einsum("scd,de->sce", operand, weight, preferred_element_type=jnp.float32)


def back_project(grads, weight):
    return jnp.einsum("sce,de->scd", grads, weight, preferred_element_type=jnp.float32)


def weight_grad(operand, grads):
    return jnp.einsum("scd,sce->de", operand, grads, preferred_element_type=jnp.float32)


def token_sum(values):
    return jnp.sum(values.astype(jnp.float32), axis=(0, 1))


def segment_ids(lengths, positions):
    image_ends = jnp.cumsum(lengths, axis=-1)
    inside = positions[None, :, None] >= image_ends[:, None, :]
    segments = jnp.sum(inside.astype(jnp.int32), axis=-1)
    return jnp.where(positions[None, :] < image_ends[:, -1:], segments, -1)


def score_rows(query_low, keys_all, allowed):
    scores = jnp.einsum(
        "sqhe,skhe->shqk",
        split_heads(query_low),
        split_heads(keys_all),
        preferred_element_type=jnp.float32,
    ) / math.sqrt(HD)
    return jnp.where(allowed, scores, NEGATIVE)


def attend_rows(query_low, keys_all, values_all, allowed):
    masked = score_rows(query_low, keys_all, allowed)
    row_top = jnp.max(masked, axis=-1, keepdims=True)
    lifted = jnp.where(allowed, jnp.exp(masked - row_top), 0.0)
    row_norm = jnp.maximum(jnp.sum(lifted, axis=-1, keepdims=True), 1.0)
    probs_low = (lifted / row_norm).astype(jnp.bfloat16)
    attended = jnp.einsum(
        "shqk,skhe->sqhe", probs_low, split_heads(values_all), preferred_element_type=jnp.float32
    )
    return (attended.reshape(query_low.shape), row_top, row_norm)


def attend_back(query_low, keys_all, values_all, allowed, row_top, row_norm, att_heads):
    masked_back = score_rows(query_low, keys_all, allowed)
    probs_full = jnp.where(allowed, jnp.exp(masked_back - row_top), 0.0) / row_norm
    probs_again = probs_full.astype(jnp.bfloat16)
    d_probs = jnp.einsum(
        "sqhe,skhe->shqk", att_heads, split_heads(values_all), preferred_element_type=jnp.float32
    )
    delta = jnp.sum(probs_full * d_probs, axis=-1, keepdims=True)
    d_scores = (probs_full * (d_probs - delta)).astype(jnp.bfloat16)
    d_query_low = jnp.einsum(
        "shqk,skhe->sqhe", d_scores, split_heads(keys_all), preferred_element_type=jnp.float32
    )
    d_query_low = d_query_low.reshape(query_low.shape) / math.sqrt(HD)
    key_term = jnp.einsum(
        "shqk,sqhe->skhe", d_scores, split_heads(query_low), preferred_element_type=jnp.float32
    )
    key_term = key_term.reshape(keys_all.shape) / math.sqrt(HD)
    value_term = jnp.einsum(
        "shqk,sqhe->skhe", probs_again, att_heads, preferred_element_type=jnp.float32
    )
    value_term = value_term.reshape(keys_all.shape)
    return (d_query_low, key_term, value_term)


def swap(values, axis, bit):
    count = lax.axis_size(axis)
    return lax.ppermute(values, axis, [(i, i ^ (1 << bit)) for i in range(count)])


def add_low(one, two):
    return (one.astype(jnp.float32) + two.astype(jnp.float32)).astype(jnp.bfloat16)


def owner_rows(grad, owners):
    return grad.astype(jnp.bfloat16).reshape(owners, grad.shape[0] // owners, grad.shape[1])


def reduce_rows(rows, first_bits):
    owners, height, width = rows.shape
    core = lax.axis_index("blk") & 1
    half = width // 2
    theirs = lax.dynamic_slice_in_dim(rows, (1 - core) * half, half, 2)
    mine = lax.dynamic_slice_in_dim(rows, core * half, half, 2)
    held = add_low(mine, swap(theirs, "blk", 0))
    bits = owners.bit_length() - 1
    order = list(first_bits) + [bit for bit in range(bits) if bit not in first_bits]
    held = held.reshape((2,) * bits + (height, half))
    left = list(reversed(range(bits)))
    me = lax.axis_index("seq")
    for bit in order:
        axis = left.index(bit)
        side = (me >> bit) & 1
        give = lax.dynamic_index_in_dim(held, 1 - side, axis, keepdims=False)
        keep = lax.dynamic_index_in_dim(held, side, axis, keepdims=False)
        held = add_low(keep, swap(give, "seq", bit))
        left.pop(axis)
    for bit in range(1, lax.axis_size("blk").bit_length() - 1):
        held = add_low(held, swap(held, "blk", bit))
    other = swap(held, "blk", 0)
    low = jnp.where(core == 0, held, other)
    high = jnp.where(core == 0, other, held)
    return jnp.concatenate([low, high], axis=1).astype(jnp.float32)


def sum_everywhere(values):
    held = values.astype(jnp.bfloat16)
    for axis in ("blk", "seq"):
        for bit in range(lax.axis_size(axis).bit_length() - 1):
            held = add_low(held, swap(held, axis, bit))
    return held.astype(jnp.float32)


def local(
    tokens,
    image_lengths,
    cotangent,
    ln1_gain,
    ln1_bias,
    w_query,
    b_query,
    w_key,
    w_value,
    b_value,
    q_gain,
    k_gain,
    w_out,
    b_out,
    ln2_gain,
    ln2_bias,
    w_up,
    b_up,
    w_down,
    b_down,
):
    seq_count, span_len, features = tokens.shape
    owners = lax.axis_size("seq")
    blocks = lax.axis_size("blk")
    length = span_len * blocks
    offset = lax.axis_index("blk") * span_len
    key_pos = jnp.arange(length, dtype=jnp.int32)
    key_seg = segment_ids(image_lengths, key_pos)
    query_seg = lax.dynamic_slice_in_dim(key_seg, offset, span_len, 1)
    allowed = (query_seg[:, :, None] == key_seg[:, None, :]) & (query_seg[:, :, None] >= 0)
    allowed = allowed[:, None]
    inputs = tokens.astype(jnp.float32)
    norm_one = normalize(inputs)
    act_one = (norm_one * ln1_gain + ln1_bias).astype(jnp.bfloat16)
    query_pre = project(act_one, w_query) + b_query
    key_pre = project(act_one, w_key)
    value_low = (project(act_one, w_value) + b_value).astype(jnp.bfloat16)
    query_unit = head_norm(query_pre)
    key_unit = head_norm(key_pre)
    query_low = (query_unit * q_gain).astype(jnp.bfloat16)
    key_low = (key_unit * k_gain).astype(jnp.bfloat16)
    keys_all, values_all = (
        lax.all_gather(key_low, "blk", axis=1, tiled=True),
        lax.all_gather(value_low, "blk", axis=1, tiled=True),
    )
    attended, row_top, row_norm = attend_rows(query_low, keys_all, values_all, allowed)
    attended = attended.astype(jnp.bfloat16)
    resid = inputs + project(attended, w_out) + b_out
    norm_two = normalize(resid)
    act_two = (norm_two * ln2_gain + ln2_bias).astype(jnp.bfloat16)
    pre_up = project(act_two, w_up) + b_up
    hidden = gelu_exact(pre_up).astype(jnp.bfloat16)
    layer_out = (resid + project(hidden, w_down) + b_down).astype(jnp.bfloat16)
    grad_out = cotangent.astype(jnp.float32)
    grad_w_down = weight_grad(hidden, cotangent)
    grad_b_down = token_sum(cotangent)
    d_hidden = back_project(cotangent, w_down)
    unused_up, gelu_back = jax.vjp(gelu_exact, pre_up)
    d_up = gelu_back(d_hidden)[0].astype(jnp.bfloat16)
    grad_w_up = weight_grad(act_two, d_up)
    grad_b_up = token_sum(d_up)
    d_act_two = back_project(d_up, w_up)
    grad_ln2_gain = jnp.sum(d_act_two * norm_two, axis=(0, 1))
    grad_ln2_bias = jnp.sum(d_act_two, axis=(0, 1))
    unused_two, norm_back_two = jax.vjp(normalize, resid)
    d_resid = grad_out + norm_back_two(d_act_two * ln2_gain)[0]
    d_branch = d_resid.astype(jnp.bfloat16)
    grad_w_out = weight_grad(attended, d_branch)
    grad_b_out = token_sum(d_branch)
    d_att = back_project(d_branch, w_out).astype(jnp.bfloat16)
    att_heads = split_heads(d_att)
    keys_back, values_back = (keys_all, values_all)
    d_query_low, key_term, value_term = attend_back(
        query_low, keys_back, values_back, allowed, row_top, row_norm, att_heads
    )
    terms = jnp.stack([key_term, value_term]).astype(jnp.bfloat16)
    kv_total = lax.psum_scatter(terms, "blk", scatter_dimension=2, tiled=True).astype(jnp.float32)
    d_key_low, d_value = (kv_total[0], kv_total[1])
    grad_q_gain = jnp.sum(d_query_low * query_unit, axis=(0, 1))
    grad_k_gain = jnp.sum(d_key_low * key_unit, axis=(0, 1))
    unused_query, query_back = jax.vjp(head_norm, query_pre)
    d_query = query_back(d_query_low * q_gain)[0].astype(jnp.bfloat16)
    unused_key, key_back = jax.vjp(head_norm, key_pre)
    d_key = key_back(d_key_low * k_gain)[0].astype(jnp.bfloat16)
    d_value_low = d_value.astype(jnp.bfloat16)
    grad_w_query = weight_grad(act_one, d_query)
    grad_b_query = token_sum(d_query)
    grad_w_key = weight_grad(act_one, d_key)
    grad_w_value = weight_grad(act_one, d_value_low)
    grad_b_value = token_sum(d_value_low)
    d_act_one = (
        back_project(d_query, w_query)
        + back_project(d_key, w_key)
        + back_project(d_value_low, w_value)
    )
    grad_ln1_gain = jnp.sum(d_act_one * norm_one, axis=(0, 1))
    grad_ln1_bias = jnp.sum(d_act_one, axis=(0, 1))
    unused_one, norm_back_one = jax.vjp(normalize, inputs)
    grad_tokens = d_resid + norm_back_one(d_act_one * ln1_gain)[0]
    big = (grad_w_query, grad_w_key, grad_w_value, grad_w_out)
    sum_out = reduce_rows(jnp.concatenate([owner_rows(part, owners) for part in big], axis=1), (1, 0))
    sum_down = reduce_rows(owner_rows(grad_w_down, owners), (0, 1))
    up_rows = owner_rows(grad_w_up, owners)
    sum_up = reduce_rows(up_rows, (1, 0))
    sum_query, sum_key, sum_value, sum_wout = jnp.split(sum_out, 4, axis=0)
    small = (
        grad_ln1_gain,
        grad_ln1_bias,
        grad_b_query,
        grad_b_value,
        grad_q_gain,
        grad_k_gain,
        grad_b_out,
        grad_ln2_gain,
        grad_ln2_bias,
        grad_b_down,
        grad_b_up,
    )
    total = sum_everywhere(jnp.concatenate(small).reshape(-1, 128))
    total = total.reshape(-1)
    me = lax.axis_index("seq")
    pieces, start = [], 0
    for part in small:
        share = part.shape[0] // owners
        pieces.append(lax.dynamic_slice_in_dim(total[start : start + part.shape[0]], me * share, share))
        start += part.shape[0]
    s_ln1g, s_ln1b, s_bq, s_bv, s_qg, s_kg, s_bo, s_ln2g, s_ln2b, s_bd, s_bu = pieces
    return (
        layer_out,
        grad_tokens,
        s_ln1g,
        s_ln1b,
        sum_query,
        s_bq,
        sum_key,
        sum_value,
        s_bv,
        s_qg,
        s_kg,
        sum_wout,
        s_bo,
        s_ln2g,
        s_ln2b,
        sum_up,
        s_bu,
        sum_down,
        s_bd,
    )


def solution(mesh):
    return jax.shard_map(
        local,
        mesh=mesh,
        in_specs=(
            P("seq", "blk", None),
            P("seq", None),
            P("seq", "blk", None),
            P(),
            P(),
            P(),
            P(),
            P(),
            P(),
            P(),
            P(),
            P(),
            P(),
            P(),
            P(),
            P(),
            P(),
            P(),
            P(),
            P(),
        ),
        out_specs=(
            P("seq", "blk", None),
            P("seq", "blk", None),
            P("seq"),
            P("seq"),
            P("seq", None),
            P("seq"),
            P("seq", None),
            P("seq", None),
            P("seq"),
            P("seq"),
            P("seq"),
            P("seq", None),
            P("seq"),
            P("seq"),
            P("seq"),
            P("seq", None),
            P("seq"),
            P("seq", None),
            P("seq"),
        ),
        check_vma=False,
    )
```

```python
import functools
import math

import jax
import jax.numpy as jnp
from jax import lax
from jax.experimental import pallas as pl
from jax.experimental.pallas import tpu as pltpu
from jax.sharding import PartitionSpec as P

H = 12
HD = 64
EPSILON = 1e-06
BLOCKED = -1024.0
MIB = 1 << 20
NT = (((1,), (1,)), ((), ()))
TN = (((0,), (0,)), ((), ()))
NN = (((1,), (0,)), ((), ()))


def dot(one, two, dims=NN):
    return lax.dot_general(one, two, dims, preferred_element_type=jnp.float32)


def low(values):
    return values.astype(jnp.bfloat16)


def wide(values):
    return values.astype(jnp.float32)


def row_stats(values):
    average = jnp.mean(values, axis=-1, keepdims=True)
    centred = values - average
    variance = jnp.mean(centred * centred, axis=-1, keepdims=True)
    scale = lax.rsqrt(variance + EPSILON)
    return centred * scale, scale


def norm_back(unit, scale, grads):
    return scale * (
        grads
        - jnp.mean(grads, axis=-1, keepdims=True)
        - unit * jnp.mean(grads * unit, axis=-1, keepdims=True)
    )


def head_mean(values):
    width = 2 * HD
    rows = lax.broadcasted_iota(jnp.int32, (width, width), 0) // HD
    columns = lax.broadcasted_iota(jnp.int32, (width, width), 1) // HD
    average = jnp.where(rows == columns, 1.0 / HD, 0.0).astype(jnp.bfloat16)
    parts = []
    for start in range(0, values.shape[1], width):
        part = values[:, start : start + width]
        upper = low(part)
        lower = low(part - wide(upper))
        parts.append(dot(upper, average) + dot(lower, average))
    return jnp.concatenate(parts, axis=1)


def head_stats(values):
    centred = values - head_mean(values)
    scale = lax.rsqrt(head_mean(centred * centred) + EPSILON)
    return centred * scale, scale


def head_norm_back(unit, scale, grads):
    return scale * (grads - head_mean(grads) - unit * head_mean(grads * unit))


def column_sum(values):
    return jnp.sum(values, axis=0, keepdims=True)


def call(body, grid, ins, outs, scratch=(), limit=48, name=None, flops=0):
    specs = [spec for _, spec in ins]
    return pl.pallas_call(
        body,
        grid=grid,
        in_specs=specs,
        out_specs=[spec for _, spec in outs],
        out_shape=[shape for shape, _ in outs],
        scratch_shapes=list(scratch),
        compiler_params=pltpu.CompilerParams(vmem_limit_bytes=limit * MIB),
        name=name,
        cost_estimate=pl.CostEstimate(flops=flops, bytes_accessed=10 * MIB, transcendentals=0),
    )(*[array for array, _ in ins])


def whole(array):
    rank = len(array.shape)
    return (array, pl.BlockSpec(array.shape, lambda *_: (0,) * rank))


def whole_out(shape, dtype):
    rank = len(shape)
    return (jax.ShapeDtypeStruct(shape, dtype), pl.BlockSpec(shape, lambda *_: (0,) * rank))


def scalars(array):
    return (array, pl.BlockSpec(memory_space=pltpu.SMEM))


def project_body(tok, gain, bias, wq, bq, wk, wv, bv, qg, kg, q8, k_low, v_low, act, q_pre, k_pre):
    unit, _ = row_stats(wide(tok[...]))
    act_one = low(unit * wide(gain[...]) + wide(bias[...]))
    act[...] = act_one
    v_low[...] = low(dot(act_one, wv[...]) + wide(bv[...]))
    key = dot(act_one, wk[...])
    k_pre[...] = key
    k_low[...] = low(head_stats(key)[0] * wide(kg[...]))
    query = dot(act_one, wq[...]) + wide(bq[...])
    q_pre[...] = query
    q8[...] = low(head_stats(query)[0] * wide(qg[...])) * (1.0 / math.sqrt(HD))


def projections(tok, gain, bias, wq, bq, wk, wv, bv, qg, kg):
    count, width = tok.shape
    tile = count // 2

    def rows(array):
        return (array, pl.BlockSpec((tile, width), lambda i: (i, 0)))

    def rows_out(dtype):
        return rows(jax.ShapeDtypeStruct((count, width), dtype))

    ins = [rows(tok)] + [whole(a) for a in (gain, bias, wq, bq, wk, wv, bv, qg, kg)]
    outs = [rows_out(jnp.bfloat16)] * 4 + [rows_out(jnp.float32)] * 2
    return call(project_body, (2,), ins, outs, name="projections", flops=6 * count * width * width)


def segment_column(positions, lengths, sequence, slots):
    end = lengths[sequence, 0]
    segment = (positions >= end).astype(jnp.int32)
    for slot in range(1, slots):
        end = end + lengths[sequence, slot]
        segment = segment + (positions >= end).astype(jnp.int32)
    return segment


def query_lanes(count, start, lengths, sequence, slots):
    positions = lax.broadcasted_iota(jnp.int32, (count, 2 * HD), 0) + start
    lane = lax.broadcasted_iota(jnp.int32, (count, 2 * HD), 1) & (HD - 1)
    segment = segment_column(positions, lengths, sequence, slots)
    return jnp.where(segment == lane, 1.0, 0.0).astype(jnp.bfloat16)


def key_lanes(count, start, lengths, sequence, slots):
    positions = lax.broadcasted_iota(jnp.int32, (count, 2 * HD), 0) + start
    lane = lax.broadcasted_iota(jnp.int32, (count, 2 * HD), 1) & (HD - 1)
    segment = segment_column(positions, lengths, sequence, slots)
    open_to = (segment == lane) & (lane < slots)
    return jnp.where(open_to, 0.0, BLOCKED).astype(jnp.bfloat16)


def pair_spec(array):
    return (array, pl.BlockSpec((1, array.shape[1], 2 * HD), lambda s, h: (s, 0, h)))


def low_half(count):
    return lax.broadcasted_iota(jnp.int32, (count, 2 * HD), 1) < HD


def attend_body(chunks, slots, lengths, starts, q8, *refs):
    keys, values = refs[:chunks], refs[chunks : 2 * chunks]
    att, inverse = refs[2 * chunks : 2 * chunks + 2]
    q_mask, *k_masks = refs[2 * chunks + 2 :]
    sequence = pl.program_id(0)
    span = q8.shape[1]

    @pl.when(pl.program_id(1) == 0)
    def _():
        q_mask[...] = query_lanes(span, starts[0], lengths, sequence, slots)
        for chunk in range(chunks):
            k_masks[chunk][...] = key_lanes(keys[chunk].shape[1], starts[1 + chunk], lengths, sequence, slots)

    first = low_half(span)
    query = q8[0]
    one = jnp.where(first, query, q_mask[...])
    two = jnp.where(first, q_mask[...], query)
    sums = [None, None]
    for chunk in range(chunks):
        key, value, mask = keys[chunk][0], values[chunk][0], k_masks[chunk][...]
        key_first = low_half(key.shape[0])
        ones = jnp.ones_like(value)
        for side, operand in enumerate((one, two)):
            pick = key_first if side == 0 else ~key_first
            lifted = low(jnp.exp(dot(operand, jnp.where(pick, key, mask), NT)))
            term = dot(lifted, jnp.where(pick, value, ones))
            sums[side] = term if sums[side] is None else sums[side] + term
    top = jnp.where(first, sums[0], sums[1])
    total = pltpu.roll(jnp.where(first, sums[1], sums[0]), HD, 1)
    inv = jnp.where(total > 0.0, 1.0 / total, 0.0)
    att[0] = low(top * inv)
    inverse[0] = inv


def attend(lengths, starts, q8, keys, values):
    count, span, width = q8.shape
    slots = lengths.shape[1]
    ins = [scalars(lengths), scalars(starts), pair_spec(q8)]
    ins += [pair_spec(a) for a in keys] + [pair_spec(a) for a in values]
    outs = [
        pair_spec(jax.ShapeDtypeStruct((count, span, width), jnp.bfloat16)),
        pair_spec(jax.ShapeDtypeStruct((count, span, width), jnp.float32)),
    ]
    scratch = [pltpu.VMEM((span, 2 * HD), jnp.bfloat16)]
    scratch += [pltpu.VMEM((a.shape[1], 2 * HD), jnp.bfloat16) for a in keys]
    body = functools.partial(attend_body, len(keys), slots)
    length = sum(a.shape[1] for a in keys)
    return call(body, (count, H // 2), ins, outs, scratch, name="attend", flops=16 * count * span * length * width)


def attend_back_body(chunks, slots, lengths, starts, q8, att, d_att, inverse, *refs):
    keys, values = refs[:chunks], refs[chunks : 2 * chunks]
    d_query = refs[2 * chunks]
    d_pairs = refs[2 * chunks + 1 : 3 * chunks + 1]
    q_mask, *k_masks = refs[3 * chunks + 1 :]
    sequence = pl.program_id(0)
    span = q8.shape[1]

    @pl.when(pl.program_id(1) == 0)
    def _():
        q_mask[...] = query_lanes(span, starts[0], lengths, sequence, slots)
        for chunk in range(chunks):
            k_masks[chunk][...] = key_lanes(keys[chunk].shape[1], starts[1 + chunk], lengths, sequence, slots)

    lane = lax.broadcasted_iota(jnp.int32, (span, 2 * HD), 1)
    first = lane < HD
    query = q8[0]
    queries = (jnp.where(first, query, q_mask[...]), jnp.where(first, q_mask[...], query))
    d_low = low(wide(d_att[0]) * inverse[0])
    product = wide(att[0]) * wide(d_low)
    d_values = []
    for side in range(2):
        pick = first if side == 0 else ~first
        delta = -jnp.sum(jnp.where(pick, product, 0.0), axis=1, keepdims=True)
        high = low(delta)
        middle = low(delta - wide(high))
        rest = low(delta - wide(high) - wide(middle))
        spot = lane & (HD - 1)
        zero = jnp.zeros((), jnp.bfloat16)
        extra = jnp.where(spot == 0, high, jnp.where(spot == 1, middle, jnp.where(spot == 2, rest, zero)))
        d_values.append(jnp.where(pick, d_low, extra))
    d_query_t = None
    for chunk in range(chunks):
        key, value, mask = keys[chunk][0], values[chunk][0], k_masks[chunk][...]
        key_first = low_half(key.shape[0])
        ones = jnp.ones_like(value)
        key_t = key.T
        key_terms, value_terms, query_terms = [], [], []
        for side in range(2):
            pick = key_first if side == 0 else ~key_first
            lifted = jnp.exp(dot(jnp.where(pick, key, mask), queries[side], NT))
            shifted = dot(jnp.where(pick, value, ones), d_values[side], NT)
            d_scores = low(lifted * shifted)
            value_terms.append(dot(low(lifted), d_low))
            key_terms.append(dot(d_scores, query))
            rows = slice(side * HD, (side + 1) * HD)
            query_terms.append(dot(key_t[rows], d_scores))
        d_pairs[chunk][0, 0] = low(jnp.where(key_first, key_terms[0], key_terms[1]))
        d_pairs[chunk][1, 0] = low(jnp.where(key_first, value_terms[0], value_terms[1]))
        term = jnp.concatenate(query_terms, axis=0)
        d_query_t = term if d_query_t is None else d_query_t + term
    d_query[0] = d_query_t.T * (1.0 / math.sqrt(HD))


def attend_back(lengths, starts, q8, att, d_att, inverse, keys, values):
    count, span, width = q8.shape
    slots = lengths.shape[1]
    ins = [scalars(lengths), scalars(starts)] + [pair_spec(a) for a in (q8, att, d_att, inverse)]
    ins += [pair_spec(a) for a in keys] + [pair_spec(a) for a in values]
    outs = [pair_spec(jax.ShapeDtypeStruct((count, span, width), jnp.float32))]
    for a in keys:
        outs.append(
            (
                jax.ShapeDtypeStruct((2,) + a.shape, jnp.bfloat16),
                pl.BlockSpec((2, 1, a.shape[1], 2 * HD), lambda s, h: (0, s, 0, h)),
            )
        )
    scratch = [pltpu.VMEM((span, 2 * HD), jnp.bfloat16)]
    scratch += [pltpu.VMEM((a.shape[1], 2 * HD), jnp.bfloat16) for a in keys]
    body = functools.partial(attend_back_body, len(keys), slots)
    length = sum(a.shape[1] for a in keys)
    return call(body, (count, H // 2), ins, outs, scratch, name="attend_back", flops=40 * count * span * length * width)


def gelu_pair(values):
    half = 0.5 + 0.5 * lax.erf(values * math.sqrt(0.5))
    slope = half + values * (math.sqrt(0.5 / math.pi) * jnp.exp(-0.5 * values * values))
    return values * half, slope


def mlp_body(
    core, att, tok, cot, w_out, b_out, gain, bias, w_up, b_up, w_down, b_down,
    out, resid, act, d_up, b_down_sum, mine, theirs, total,
):
    step = pl.program_id(0)
    half = cot.shape[1] // 2

    @pl.when(step == 0)
    def _():
        held = wide(tok[...]) + dot(att[...], w_out[...]) + wide(b_out[...])
        resid[...] = held
        act[...] = low(row_stats(held)[0] * wide(gain[...]) + wide(bias[...]))
        total[...] = held + wide(b_down[...])
        b_down_sum[...] = column_sum(wide(cot[...]))

    pre_up = dot(act[...], w_up[...]) + wide(b_up[...])
    hidden, slope = gelu_pair(pre_up)
    hidden = low(hidden)
    d_hidden = dot(cot[...], w_down[...], NT)
    d_up[...] = low(d_hidden * slope)
    total[...] += dot(hidden, w_down[...])
    own = pl.multiple_of(core[0] * half, 128)
    other = pl.multiple_of((1 - core[0]) * half, 128)
    theirs[...] = low(dot(hidden, cot[:, pl.ds(other, half)], TN))
    mine[...] = low(dot(hidden, cot[:, pl.ds(own, half)], TN))

    @pl.when(step == pl.num_programs(0) - 1)
    def _():
        out[...] = low(total[...])


def mlp(core, att, tok, cot, w_out, b_out, gain, bias, w_up, b_up, w_down, b_down):
    count, width = tok.shape
    hidden = w_up.shape[1]
    tile = 768
    grid = hidden // tile
    ins = [scalars(core)] + [whole(a) for a in (att, tok, cot, w_out, b_out, gain, bias)]
    ins += [
        (w_up, pl.BlockSpec((width, tile), lambda j: (0, j))),
        (b_up, pl.BlockSpec((1, tile), lambda j: (0, j))),
        (w_down, pl.BlockSpec((tile, width), lambda j: (j, 0))),
        whole(b_down),
    ]
    part = (
        jax.ShapeDtypeStruct((hidden, width // 2), jnp.bfloat16),
        pl.BlockSpec((tile, width // 2), lambda j: (j, 0)),
    )
    outs = [
        whole_out((count, width), jnp.bfloat16),
        whole_out((count, width), jnp.float32),
        whole_out((count, width), jnp.bfloat16),
        (
            jax.ShapeDtypeStruct((count, hidden), jnp.bfloat16),
            pl.BlockSpec((count, tile), lambda j: (0, j)),
        ),
        whole_out((1, width), jnp.float32),
        part,
        part,
    ]
    scratch = [pltpu.VMEM((count, width), jnp.float32)]
    return call(mlp_body, (grid,), ins, outs, scratch, name="mlp", flops=8 * count * width * hidden)


def mlp_back_body(
    blocks, core, d_up, act, w_up, resid, cot, gain, att, w_out,
    d_resid, d_att, b_up_sum, gain_sum, bias_sum, b_out_sum, mine, theirs, total,
):
    step = pl.program_id(0)
    half = cot.shape[1] // 2

    @pl.when(step == 0)
    def _():
        total[...] = jnp.zeros_like(total)

    @pl.when(step < 2 * blocks)
    def _():
        grads = d_up[...]
        total[...] += dot(grads, w_up[...], NT)
        b_up_sum[...] = column_sum(wide(grads))
        piece = low(dot(act[...], grads, TN))

        @pl.when(step < blocks)
        def _():
            theirs[...] = piece

        @pl.when(step >= blocks)
        def _():
            mine[...] = piece

    @pl.when(step == 2 * blocks)
    def _():
        grads = total[...]
        unit, scale = row_stats(resid[...])
        gain_sum[...] = column_sum(grads * unit)
        bias_sum[...] = column_sum(grads)
        back = wide(cot[...]) + norm_back(unit, scale, grads * wide(gain[...]))
        d_resid[...] = back
        branch = low(back)
        b_out_sum[...] = column_sum(wide(branch))
        d_att[...] = low(dot(branch, w_out[...], NT))
        product = low(dot(att[...], branch, TN))
        for side in range(2):

            @pl.when(core[0] == side)
            def _():
                mine[...] = product[:, side * half : (side + 1) * half]
                theirs[...] = product[:, (1 - side) * half : (2 - side) * half]


def mlp_back(core, d_up, act, w_up, resid, cot, gain, att, w_out):
    count, width = act.shape
    hidden = w_up.shape[1]
    tile = width // 2
    blocks = hidden // tile // 2

    def place(j, core):
        j = jnp.minimum(j, 2 * blocks - 1)
        return jnp.where(core[0] == 0, (j + blocks) % (2 * blocks), j)

    def spec(shape, index):
        return pl.BlockSpec(shape, index)

    def full(array):
        rank = len(array.shape)
        return spec(array.shape, lambda j, core: (0,) * rank)

    def out(shape, dtype):
        return jax.ShapeDtypeStruct(shape, dtype)

    columns = spec((width, tile), lambda j, core: (0, place(j, core)))
    part = out((width, (blocks + 1) * tile), jnp.bfloat16)
    row = out((1, width), jnp.float32)
    shapes = [
        out((count, width), jnp.float32),
        out((count, width), jnp.bfloat16),
        out((1, hidden), jnp.float32),
        row,
        row,
        row,
        part,
        part,
    ]
    out_specs = [
        full(shapes[0]),
        full(shapes[1]),
        spec((1, tile), lambda j, core: (0, place(j, core))),
        full(row),
        full(row),
        full(row),
        spec((width, tile), lambda j, core: (0, jnp.maximum(j - blocks, 0))),
        spec((width, tile), lambda j, core: (0, jnp.where(j == 2 * blocks, blocks, jnp.minimum(j, blocks - 1)))),
    ]
    grid_spec = pltpu.PrefetchScalarGridSpec(
        num_scalar_prefetch=1,
        grid=(2 * blocks + 1,),
        in_specs=[
            spec((count, tile), lambda j, core: (0, place(j, core))),
            full(act),
            columns,
            full(resid),
            full(cot),
            full(gain),
            full(att),
            full(w_out),
        ],
        out_specs=out_specs,
        scratch_shapes=[pltpu.VMEM((count, width), jnp.float32)],
    )
    return pl.pallas_call(
        functools.partial(mlp_back_body, blocks),
        grid_spec=grid_spec,
        out_shape=shapes,
        compiler_params=pltpu.CompilerParams(vmem_limit_bytes=48 * MIB),
        name="mlp_back",
        cost_estimate=pl.CostEstimate(flops=4 * count * width * hidden, bytes_accessed=16 * MIB, transcendentals=0),
    )(core, d_up, act, w_up, resid, cot, gain, att, w_out)


def project_back_body(
    core, dq, dk, dv, dk_in, dv_in, q_pre, k_pre, qg, kg, act, wq, wk, wv, tok, d_resid, gain,
    grad_tok, bq_sum, bv_sum, qg_sum, kg_sum, gain_sum, bias_sum, mine, theirs, total,
):
    step = pl.program_id(0)
    tile = q_pre.shape[1]
    query_unit, query_scale = head_stats(q_pre[...])
    d_low = dq[...]
    qg_sum[...] = column_sum(d_low * query_unit)
    d_query = low(head_norm_back(query_unit, query_scale, d_low * wide(qg[...])))
    key_unit, key_scale = head_stats(k_pre[...])
    d_key_low = wide(dk[...]) + wide(dk_in[...])
    kg_sum[...] = column_sum(d_key_low * key_unit)
    d_key = low(head_norm_back(key_unit, key_scale, d_key_low * wide(kg[...])))
    d_value = low(wide(dv[...]) + wide(dv_in[...]))
    bq_sum[...] = column_sum(wide(d_query))
    bv_sum[...] = column_sum(wide(d_value))
    for place, grads in enumerate((d_query, d_key, d_value)):
        piece = low(dot(act[...], grads, TN))
        columns = slice(place * tile, (place + 1) * tile)

        @pl.when(step == 0)
        def _():
            theirs[:, columns] = piece

        @pl.when(step == 1)
        def _():
            mine[:, columns] = piece

    back = dot(d_query, wq[...], NT) + dot(d_key, wk[...], NT) + dot(d_value, wv[...], NT)

    @pl.when(step == 0)
    def _():
        total[...] = back

    @pl.when(step == 1)
    def _():
        grads = total[...] + back
        unit, scale = row_stats(wide(tok[...]))
        gain_sum[...] = column_sum(grads * unit)
        bias_sum[...] = column_sum(grads)
        grad_tok[...] = d_resid[...] + norm_back(unit, scale, grads * wide(gain[...]))


def project_back(core, dq, dk, dv, dk_in, dv_in, q_pre, k_pre, qg, kg, act, wq, wk, wv, tok, d_resid, gain):
    count, width = act.shape
    tile = width // 2

    def half(array):
        return pl.BlockSpec((array.shape[0], tile), lambda j, core: (0, (1 - core[0] + j) % 2))

    def full(array):
        rank = len(array.shape)
        return pl.BlockSpec(array.shape, lambda j, core: (0,) * rank)

    def out(shape, dtype):
        return jax.ShapeDtypeStruct(shape, dtype)

    row = out((1, width), jnp.float32)
    part = out((width, 3 * tile), jnp.bfloat16)
    shapes = [out((count, width), jnp.float32)] + [row] * 6 + [part, part]
    out_specs = [full(shapes[0])] + [half(row)] * 4 + [full(row)] * 2 + [full(part)] * 2
    halves = (dq, dk, dv, dk_in, dv_in, q_pre, k_pre, qg, kg)
    grid_spec = pltpu.PrefetchScalarGridSpec(
        num_scalar_prefetch=1,
        grid=(2,),
        in_specs=[half(a) for a in halves]
        + [full(act)]
        + [half(a) for a in (wq, wk, wv)]
        + [full(a) for a in (tok, d_resid, gain)],
        out_specs=out_specs,
        scratch_shapes=[pltpu.VMEM((count, width), jnp.float32)],
    )
    return pl.pallas_call(
        project_back_body,
        grid_spec=grid_spec,
        out_shape=shapes,
        compiler_params=pltpu.CompilerParams(vmem_limit_bytes=48 * MIB),
        name="project_back",
        cost_estimate=pl.CostEstimate(flops=12 * count * width * width, bytes_accessed=16 * MIB, transcendentals=0),
    )(core, *halves, act, wq, wk, wv, tok, d_resid, gain)


def swap(values, axis, bit):
    count = lax.axis_size(axis)
    return lax.ppermute(values, axis, [(i, i ^ (1 << bit)) for i in range(count)])


def add_low(one, two):
    return low(wide(one) + wide(two))


def reduce_rows(mine, theirs, first_bits):
    owners = lax.axis_size("seq")
    height, half = mine.shape[0] // owners, mine.shape[1]
    held = add_low(mine, swap(theirs, "blk", 0))
    bits = owners.bit_length() - 1
    order = list(first_bits) + [bit for bit in range(bits) if bit not in first_bits]
    held = held.reshape((2,) * bits + (height, half))
    left = list(reversed(range(bits)))
    me = lax.axis_index("seq")
    for bit in order:
        axis = left.index(bit)
        side = (me >> bit) & 1
        give = lax.dynamic_index_in_dim(held, 1 - side, axis, keepdims=False)
        keep = lax.dynamic_index_in_dim(held, side, axis, keepdims=False)
        held = add_low(keep, swap(give, "seq", bit))
        left.pop(axis)
    for bit in range(1, lax.axis_size("blk").bit_length() - 1):
        held = add_low(held, swap(held, "blk", bit))
    return held


def both_halves(held):
    core = lax.axis_index("blk") & 1
    other = swap(held, "blk", 0)
    first = jnp.where(core == 0, held, other)
    second = jnp.where(core == 0, other, held)
    return wide(first), wide(second)


def sum_everywhere(values):
    held = low(values)
    for axis in ("blk", "seq"):
        for bit in range(lax.axis_size(axis).bit_length() - 1):
            held = add_low(held, swap(held, axis, bit))
    return wide(held)


def local(
    tokens,
    image_lengths,
    cotangent,
    ln1_gain,
    ln1_bias,
    w_query,
    b_query,
    w_key,
    w_value,
    b_value,
    q_gain,
    k_gain,
    w_out,
    b_out,
    ln2_gain,
    ln2_bias,
    w_up,
    b_up,
    w_down,
    b_down,
):
    sequences, span, width = tokens.shape
    owners = lax.axis_size("seq")
    blocks = lax.axis_size("blk")
    me = lax.axis_index("seq")
    place = lax.axis_index("blk")
    core = (place & 1).reshape(1)
    tok = tokens.reshape(-1, width)
    cot = cotangent.reshape(-1, width)

    def row(vector):
        return vector.reshape(1, -1)

    def split(array):
        return array.reshape(sequences, -1, width)

    def flat(array):
        return array.reshape(-1, width)

    q8, k_low, v_low, act_one, q_pre, k_pre = projections(
        tok, row(ln1_gain), row(ln1_bias), w_query, row(b_query), w_key, w_value, row(b_value), row(q_gain), row(k_gain)
    )
    k_low, v_low = split(k_low), split(v_low)
    if blocks == 2:
        keys = [k_low, swap(k_low, "blk", 0)]
        values = [v_low, swap(v_low, "blk", 0)]
        starts = jnp.stack([place * span, place * span, (1 - place) * span])
    else:
        keys = [lax.all_gather(k_low, "blk", axis=1, tiled=True)]
        values = [lax.all_gather(v_low, "blk", axis=1, tiled=True)]
        starts = jnp.stack([place * span, place * 0])
    starts = starts.astype(jnp.int32)
    att, inverse = attend(image_lengths, starts, split(q8), keys, values)
    out, resid, act_two, d_up, s_bd, down_mine, down_theirs = mlp(
        core, flat(att), tok, cot, w_out, row(b_out), row(ln2_gain), row(ln2_bias), w_up, row(b_up), w_down, row(b_down)
    )
    down = reduce_rows(down_mine, down_theirs, (0, 1))
    d_resid, d_att, s_bu, s_ln2g, s_ln2b, s_bo, up_mine, up_theirs = mlp_back(
        core, d_up, act_two, w_up, resid, cot, row(ln2_gain), flat(att), w_out
    )
    up = reduce_rows(up_mine, up_theirs, (1, 0))
    dq, *pairs = attend_back(image_lengths, starts, split(q8), att, split(d_att), inverse, keys, values)
    if blocks == 2:
        own, arrived = pairs[0], swap(pairs[1], "blk", 0)
    else:
        own = lax.psum_scatter(pairs[0], "blk", scatter_dimension=2, tiled=True)
        arrived = jnp.zeros_like(own)
    grad_tok, s_bq, s_bv, s_qg, s_kg, s_ln1g, s_ln1b, qkv_mine, qkv_theirs = project_back(
        core, flat(dq), flat(own[0]), flat(own[1]), flat(arrived[0]), flat(arrived[1]), q_pre, k_pre,
        row(q_gain), row(k_gain), act_one, w_query, w_key, w_value, tok, d_resid, row(ln1_gain),
    )
    qkv = reduce_rows(qkv_mine, qkv_theirs, (0, 1))
    small = (s_ln1g, s_ln1b, s_bq, s_bv, s_qg, s_kg, s_bo, s_ln2g, s_ln2b, s_bd, s_bu)
    total = sum_everywhere(jnp.concatenate([part.reshape(-1) for part in small]).reshape(-1, 128)).reshape(-1)
    pieces, start = [], 0
    for part in small:
        share = part.size // owners
        pieces.append(lax.dynamic_slice_in_dim(total[start : start + part.size], me * share, share))
        start += part.size
    t_ln1g, t_ln1b, t_bq, t_bv, t_qg, t_kg, t_bo, t_ln2g, t_ln2b, t_bd, t_bu = pieces
    half = width // 2

    def joined(first, second, start, stop):
        return jnp.concatenate([first[:, start:stop], second[:, start:stop]], axis=1)

    down = joined(*both_halves(down), 0, half)
    pair = both_halves(up)
    wide_up = w_up.shape[1] // 2
    grad_up = joined(*pair, 0, wide_up)
    grad_out = joined(*pair, wide_up, wide_up + half)
    pair = both_halves(qkv)
    grad_q, grad_k, grad_v = (joined(*pair, i * half, (i + 1) * half) for i in range(3))
    return (
        out.reshape(tokens.shape),
        grad_tok.reshape(tokens.shape),
        t_ln1g,
        t_ln1b,
        grad_q,
        t_bq,
        grad_k,
        grad_v,
        t_bv,
        t_qg,
        t_kg,
        grad_out,
        t_bo,
        t_ln2g,
        t_ln2b,
        grad_up,
        t_bu,
        down,
        t_bd,
    )


def solution(mesh):
    return jax.shard_map(
        local,
        mesh=mesh,
        in_specs=(
            P("seq", "blk", None),
            P("seq", None),
            P("seq", "blk", None),
            P(),
            P(),
            P(),
            P(),
            P(),
            P(),
            P(),
            P(),
            P(),
            P(),
            P(),
            P(),
            P(),
            P(),
            P(),
            P(),
            P(),
        ),
        out_specs=(
            P("seq", "blk", None),
            P("seq", "blk", None),
            P("seq"),
            P("seq"),
            P("seq", None),
            P("seq"),
            P("seq", None),
            P("seq", None),
            P("seq"),
            P("seq"),
            P("seq"),
            P("seq", None),
            P("seq"),
            P("seq"),
            P("seq"),
            P("seq", None),
            P("seq"),
            P("seq", None),
            P("seq"),
        ),
        check_vma=False,
    )
```

```python
import functools
import math

import jax
import jax.numpy as jnp
from jax import lax
from jax.experimental import pallas as pl
from jax.experimental.pallas import tpu as pltpu
from jax.sharding import PartitionSpec as P

H = 12
HD = 64
EPSILON = 1e-06
BLOCKED = -1024.0
MIB = 1 << 20
LONG = 10**12
SMALL = 10
NT = (((1,), (1,)), ((), ()))
TN = (((0,), (0,)), ((), ()))
NN = (((1,), (0,)), ((), ()))


def dot(one, two, dims=NN):
    return lax.dot_general(one, two, dims, preferred_element_type=jnp.float32)


def low(values):
    return values.astype(jnp.bfloat16)


def wide(values):
    return values.astype(jnp.float32)


def row_stats(values):
    average = jnp.mean(values, axis=-1, keepdims=True)
    centred = values - average
    variance = jnp.mean(centred * centred, axis=-1, keepdims=True)
    scale = lax.rsqrt(variance + EPSILON)
    return centred * scale, scale


def norm_back(unit, scale, grads):
    return scale * (
        grads
        - jnp.mean(grads, axis=-1, keepdims=True)
        - unit * jnp.mean(grads * unit, axis=-1, keepdims=True)
    )


def head_mean(values):
    width = 2 * HD
    rows = lax.broadcasted_iota(jnp.int32, (width, width), 0) // HD
    columns = lax.broadcasted_iota(jnp.int32, (width, width), 1) // HD
    average = jnp.where(rows == columns, 1.0 / HD, 0.0).astype(jnp.bfloat16)
    parts = []
    for start in range(0, values.shape[1], width):
        part = values[:, start : start + width]
        upper = low(part)
        lower = low(part - wide(upper))
        parts.append(dot(upper, average) + dot(lower, average))
    return jnp.concatenate(parts, axis=1)


def head_stats(values):
    centred = values - head_mean(values)
    scale = lax.rsqrt(head_mean(centred * centred) + EPSILON)
    return centred * scale, scale


def head_norm_back(unit, scale, grads):
    return scale * (grads - head_mean(grads) - unit * head_mean(grads * unit))


def vector(ref):
    return wide(ref[...]).reshape(1, -1)


def column_sum(values):
    return jnp.sum(values, axis=0, keepdims=True)


def call(body, grid, ins, outs, scratch=(), prefetch=None, after=(), limit=24, name=None, cost=1000):
    ins = list(ins) + [(array, pl.BlockSpec(memory_space=pl.ANY)) for array in after]
    lead = len(ins) - len(after) + (prefetch is not None)

    def kernel(*refs):
        body(*refs[:lead], *refs[lead + len(after) :])

    grid_spec = pltpu.PrefetchScalarGridSpec(
        num_scalar_prefetch=int(prefetch is not None),
        grid=grid,
        in_specs=[spec for _, spec in ins],
        out_specs=[spec for _, spec in outs],
        scratch_shapes=list(scratch),
    )
    arrays = [array for array, _ in ins]
    return pl.pallas_call(
        kernel,
        grid_spec=grid_spec,
        out_shape=[shape for shape, _ in outs],
        compiler_params=pltpu.CompilerParams(vmem_limit_bytes=limit * MIB),
        name=name,
        cost_estimate=pl.CostEstimate(flops=cost, bytes_accessed=1000, transcendentals=0),
    )(*([] if prefetch is None else [prefetch]), *arrays)


def whole(array):
    rank = len(array.shape)
    return (array, pl.BlockSpec(array.shape, lambda *_: (0,) * rank))


def whole_out(shape, dtype):
    rank = len(shape)
    return (jax.ShapeDtypeStruct(shape, dtype), pl.BlockSpec(shape, lambda *_: (0,) * rank))


def scalars(array):
    return (array, pl.BlockSpec(memory_space=pltpu.SMEM))


def project_body(tok, gain, bias, wq, bq, wk, wv, bv, qg, kg, q8, pair, act, q_pre, k_pre):
    unit, _ = row_stats(wide(tok[...]))
    act_one = low(unit * vector(gain) + vector(bias))
    act[...] = act_one
    pair[1] = low(dot(act_one, wv[...]) + vector(bv))
    key = dot(act_one, wk[...])
    k_pre[...] = key
    pair[0] = low(head_stats(key)[0] * vector(kg))
    query = dot(act_one, wq[...]) + vector(bq)
    q_pre[...] = query
    q8[...] = low(head_stats(query)[0] * vector(qg)) * (1.0 / math.sqrt(HD))


def projections(tok, gain, bias, wq, bq, wk, wv, bv, qg, kg):
    count, width = tok.shape
    tile = count // 2

    def rows(dtype):
        return (jax.ShapeDtypeStruct((count, width), dtype), pl.BlockSpec((tile, width), lambda i: (i, 0)))

    ins = [(tok, pl.BlockSpec((tile, width), lambda i: (i, 0)))]
    ins += [whole(a) for a in (gain, bias, wq, bq, wk, wv, bv, qg, kg)]
    pair = (
        jax.ShapeDtypeStruct((2, count, width), jnp.bfloat16),
        pl.BlockSpec((2, tile, width), lambda i: (0, i, 0)),
    )
    outs = [rows(jnp.bfloat16), pair, rows(jnp.bfloat16), rows(jnp.float32), rows(jnp.float32)]
    return call(project_body, (2,), ins, outs, limit=60, name="projections")


def segment_column(positions, lengths, sequence, slots):
    end = lengths[sequence, 0]
    segment = (positions >= end).astype(jnp.int32)
    for slot in range(1, slots):
        end = end + lengths[sequence, slot]
        segment = segment + (positions >= end).astype(jnp.int32)
    return segment


def query_lanes(count, start, lengths, sequence, slots):
    positions = lax.broadcasted_iota(jnp.int32, (count, 2 * HD), 0) + start
    lane = lax.broadcasted_iota(jnp.int32, (count, 2 * HD), 1) & (HD - 1)
    segment = segment_column(positions, lengths, sequence, slots)
    return jnp.where(segment == lane, 1.0, 0.0).astype(jnp.bfloat16)


def key_lanes(count, start, lengths, sequence, slots):
    positions = lax.broadcasted_iota(jnp.int32, (count, 2 * HD), 0) + start
    lane = lax.broadcasted_iota(jnp.int32, (count, 2 * HD), 1) & (HD - 1)
    segment = segment_column(positions, lengths, sequence, slots)
    open_to = (segment == lane) & (lane < slots)
    return jnp.where(open_to, 0.0, BLOCKED).astype(jnp.bfloat16)


def pair_spec(array):
    return (array, pl.BlockSpec((1, array.shape[1], 2 * HD), lambda s, h: (s, 0, h)))


def both_spec(array):
    return (array, pl.BlockSpec((2, 1, array.shape[2], 2 * HD), lambda s, h: (0, s, 0, h)))


def low_half(count):
    return lax.broadcasted_iota(jnp.int32, (count, 2 * HD), 1) < HD


def attend_body(chunks, slots, lengths, starts, q8, *refs):
    pairs = refs[:chunks]
    att, inverse = refs[chunks : chunks + 2]
    q_mask, *k_masks = refs[chunks + 2 :]
    sequence = pl.program_id(0)
    span = q8.shape[1]

    @pl.when(pl.program_id(1) == 0)
    def _():
        q_mask[...] = query_lanes(span, starts[0], lengths, sequence, slots)
        for chunk in range(chunks):
            k_masks[chunk][...] = key_lanes(pairs[chunk].shape[2], starts[1 + chunk], lengths, sequence, slots)

    first = low_half(span)
    query = q8[0]
    one = jnp.where(first, query, q_mask[...])
    two = jnp.where(first, q_mask[...], query)
    sums = [None, None]
    for chunk in range(chunks):
        key, value, mask = pairs[chunk][0, 0], pairs[chunk][1, 0], k_masks[chunk][...]
        key_first = low_half(key.shape[0])
        ones = jnp.ones_like(value)
        for side, operand in enumerate((one, two)):
            pick = key_first if side == 0 else ~key_first
            lifted = low(jnp.exp(dot(operand, jnp.where(pick, key, mask), NT)))
            term = dot(lifted, jnp.where(pick, value, ones))
            sums[side] = term if sums[side] is None else sums[side] + term
    top = jnp.where(first, sums[0], sums[1])
    total = pltpu.roll(jnp.where(first, sums[1], sums[0]), HD, 1)
    inv = jnp.where(total > 0.0, 1.0 / total, 0.0)
    att[0] = low(top * inv)
    inverse[0] = inv


def attend(lengths, starts, q8, pairs):
    count, span, width = q8.shape
    slots = lengths.shape[1]
    ins = [scalars(lengths), scalars(starts), pair_spec(q8)]
    ins += [both_spec(a) for a in pairs]
    outs = [
        pair_spec(jax.ShapeDtypeStruct((count, span, width), jnp.bfloat16)),
        pair_spec(jax.ShapeDtypeStruct((count, span, width), jnp.float32)),
    ]
    scratch = [pltpu.VMEM((span, 2 * HD), jnp.bfloat16)]
    scratch += [pltpu.VMEM((a.shape[2], 2 * HD), jnp.bfloat16) for a in pairs]
    body = functools.partial(attend_body, len(pairs), slots)
    return call(body, (count, H // 2), ins, outs, scratch, limit=32, name="attend")


def attend_back_body(chunks, slots, lengths, starts, q8, att, d_att, inverse, *refs):
    pairs = refs[:chunks]
    d_query = refs[chunks]
    d_keys, d_vals = refs[chunks + 1 : 2 * chunks + 1], refs[2 * chunks + 1 : 3 * chunks + 1]
    q_mask, *k_masks = refs[3 * chunks + 1 :]
    sequence = pl.program_id(0)
    span = q8.shape[1]

    @pl.when(pl.program_id(1) == 0)
    def _():
        q_mask[...] = query_lanes(span, starts[0], lengths, sequence, slots)
        for chunk in range(chunks):
            k_masks[chunk][...] = key_lanes(pairs[chunk].shape[2], starts[1 + chunk], lengths, sequence, slots)

    lane = lax.broadcasted_iota(jnp.int32, (span, 2 * HD), 1)
    first = lane < HD
    query = q8[0]
    queries = (jnp.where(first, query, q_mask[...]), jnp.where(first, q_mask[...], query))
    d_low = low(wide(d_att[0]) * inverse[0])
    product = wide(att[0]) * wide(d_low)
    d_values = []
    for side in range(2):
        pick = first if side == 0 else ~first
        delta = -jnp.sum(jnp.where(pick, product, 0.0), axis=1, keepdims=True)
        high = low(delta)
        middle = low(delta - wide(high))
        rest = low(delta - wide(high) - wide(middle))
        spot = lane & (HD - 1)
        zero = jnp.zeros((), jnp.bfloat16)
        extra = jnp.where(spot == 0, high, jnp.where(spot == 1, middle, jnp.where(spot == 2, rest, zero)))
        d_values.append(jnp.where(pick, d_low, extra))
    d_query_t = None
    for chunk in range(chunks):
        key, value, mask = pairs[chunk][0, 0], pairs[chunk][1, 0], k_masks[chunk][...]
        key_first = low_half(key.shape[0])
        ones = jnp.ones_like(value)
        key_t = key.T
        key_terms, value_terms, query_terms = [], [], []
        for side in range(2):
            pick = key_first if side == 0 else ~key_first
            lifted = jnp.exp(dot(jnp.where(pick, key, mask), queries[side], NT))
            shifted = dot(jnp.where(pick, value, ones), d_values[side], NT)
            d_scores = low(lifted * shifted)
            value_terms.append(dot(low(lifted), d_low))
            key_terms.append(dot(d_scores, query))
            rows = slice(side * HD, (side + 1) * HD)
            query_terms.append(dot(key_t[rows], d_scores))
        d_keys[chunk][0] = low(jnp.where(key_first, key_terms[0], key_terms[1]))
        d_vals[chunk][0] = low(jnp.where(key_first, value_terms[0], value_terms[1]))
        term = jnp.concatenate(query_terms, axis=0)
        d_query_t = term if d_query_t is None else d_query_t + term
    d_query[0] = d_query_t.T * (1.0 / math.sqrt(HD))


def attend_back(lengths, starts, q8, att, d_att, inverse, pairs, after):
    count, span, width = q8.shape
    slots = lengths.shape[1]
    ins = [scalars(lengths), scalars(starts)] + [pair_spec(a) for a in (q8, att, d_att, inverse)]
    ins += [both_spec(a) for a in pairs]
    outs = [pair_spec(jax.ShapeDtypeStruct((count, span, width), jnp.float32))]
    outs += [pair_spec(jax.ShapeDtypeStruct(a.shape[1:], jnp.bfloat16)) for a in pairs + pairs]
    scratch = [pltpu.VMEM((span, 2 * HD), jnp.bfloat16)]
    scratch += [pltpu.VMEM((a.shape[2], 2 * HD), jnp.bfloat16) for a in pairs]
    body = functools.partial(attend_back_body, len(pairs), slots)
    return call(body, (count, H // 2), ins, outs, scratch, after=after, limit=40, name="attend_back")


def gelu_pair(values):
    half = 0.5 + 0.5 * lax.erf(values * math.sqrt(0.5))
    slope = half + values * (math.sqrt(0.5 / math.pi) * jnp.exp(-0.5 * values * values))
    return values * half, slope


def fold_rows(piece, out, height):
    owners, width = out.shape[0] // height, piece.shape[1]
    folds = piece.shape[0] // out.shape[0]
    parts = piece.reshape(owners, folds, height, width)
    for fold in range(folds):
        out[:, fold * width : (fold + 1) * width] = parts[:, fold].reshape(out.shape[0], width)


def mlp_body(
    height, core, att, tok, cot, w_out, b_out, gain, bias, w_up, b_up, w_down, b_down,
    out, resid, act, hidden_out, d_up, theirs, total,
):
    step = pl.program_id(0)
    half = cot.shape[1] // 2
    tile = w_up.shape[1]

    @pl.when(step == 0)
    def _():
        held = wide(tok[...]) + dot(att[...], w_out[...]) + vector(b_out)
        resid[...] = held
        act[...] = low(row_stats(held)[0] * vector(gain) + vector(bias))
        total[...] = held + vector(b_down)

    pre_up = dot(act[...], w_up[...]) + wide(b_up[pl.ds(step * tile, tile)]).reshape(1, -1)
    hidden, slope = gelu_pair(pre_up)
    hidden = low(hidden)
    hidden_out[...] = hidden
    d_hidden = dot(cot[...], w_down[...], NT)
    d_up[...] = low(d_hidden * slope)
    total[...] += dot(hidden, w_down[...])
    other = pl.multiple_of((1 - core[0]) * half, 128)
    fold_rows(low(dot(hidden, cot[:, pl.ds(other, half)], TN)), theirs, height)

    @pl.when(step == pl.num_programs(0) - 1)
    def _():
        out[...] = low(total[...])


def folded(hidden, width, tile):
    folds = hidden // width
    return (
        jax.ShapeDtypeStruct((width, folds * (width // 2)), jnp.bfloat16),
        pl.BlockSpec((tile // folds, folds * (width // 2)), lambda j, *_: (j, 0)),
    )


def mlp(height, core, att, tok, cot, w_out, b_out, gain, bias, w_up, b_up, w_down, b_down):
    count, width = tok.shape
    hidden = w_up.shape[1]
    tile = width
    ins = [scalars(core)] + [whole(a) for a in (att, tok, cot, w_out, b_out, gain, bias)]
    ins += [
        (w_up, pl.BlockSpec((width, tile), lambda j: (0, j))),
        whole(b_up),
        (w_down, pl.BlockSpec((tile, width), lambda j: (j, 0))),
        whole(b_down),
    ]
    blocks = (
        jax.ShapeDtypeStruct((count, hidden), jnp.bfloat16),
        pl.BlockSpec((count, tile), lambda j: (0, j)),
    )
    outs = [
        whole_out((count, width), jnp.bfloat16),
        whole_out((count, width), jnp.float32),
        whole_out((count, width), jnp.bfloat16),
        blocks,
        blocks,
        folded(hidden, width, tile),
    ]
    scratch = [pltpu.VMEM((count, width), jnp.float32)]
    body = functools.partial(mlp_body, height)
    return call(body, (hidden // tile,), ins, outs, scratch, limit=48, name="mlp")


def down_mine_body(height, core, hidden, cot, mine):
    fold_rows(low(dot(hidden[...], cot[...], TN)), mine, height)


def down_mine(height, core, hidden, cot):
    count, width = cot.shape
    tile = width
    ins = [
        (hidden, pl.BlockSpec((count, tile), lambda j, core: (0, j))),
        (cot, pl.BlockSpec((count, width // 2), lambda j, core: (0, core[0]))),
    ]
    outs = [folded(hidden.shape[1], width, tile)]
    body = functools.partial(down_mine_body, height)
    return call(body, (hidden.shape[1] // tile,), ins, outs, prefetch=core, name="down_mine", cost=LONG)[0]


def mlp_back_body(
    core, d_up, act, w_up, resid, cot, gain, w_out, att,
    d_resid, branch_out, d_att, b_up_sum, rows, theirs, total,
):
    step = pl.program_id(0)
    last = pl.num_programs(0) - 1
    tile = d_up.shape[1]

    @pl.when(step == 0)
    def _():
        total[...] = jnp.zeros_like(total)

    grads = d_up[...]
    total[...] += dot(grads, w_up[...], NT)
    b_up_sum[...] = column_sum(wide(grads))

    @pl.when(step <= last // 2)
    def _():
        theirs[:, pl.ds(step * tile, tile)] = low(dot(act[...], grads, TN))

    @pl.when(step == last)
    def _():
        grads = total[...]
        unit, scale = row_stats(resid[...])
        rows[0:1, :] = column_sum(grads * unit)
        rows[1:2, :] = column_sum(grads)
        back = wide(cot[...]) + norm_back(unit, scale, grads * vector(gain))
        d_resid[...] = back
        branch = low(back)
        branch_out[...] = branch
        rows[2:3, :] = column_sum(wide(branch))
        rows[3:4, :] = column_sum(wide(cot[...]))
        d_att[...] = low(dot(branch, w_out[...], NT))
        half = branch.shape[1] // 2
        other = jnp.where(core[0] == 0, branch[:, half:], branch[:, :half])
        theirs[:, theirs.shape[1] - half :] = low(dot(att[...], other, TN))


def mlp_back(core, d_up, act, w_up, resid, cot, gain, w_out, att, after):
    count, width = act.shape
    hidden = w_up.shape[1]
    tile = width
    blocks = hidden // tile

    def place(j, core):
        return (j + (1 - core[0]) * (blocks // 2)) % blocks

    ins = [
        (d_up, pl.BlockSpec((count, tile), lambda j, core: (0, place(j, core)))),
        whole(act),
        (w_up, pl.BlockSpec((width, tile), lambda j, core: (0, place(j, core)))),
    ] + [whole(a) for a in (resid, cot, gain, w_out, att)]
    outs = [
        whole_out((count, width), jnp.float32),
        whole_out((count, width), jnp.bfloat16),
        whole_out((count, width), jnp.bfloat16),
        (
            jax.ShapeDtypeStruct((1, hidden), jnp.float32),
            pl.BlockSpec((1, tile), lambda j, core: (0, place(j, core))),
        ),
        whole_out((8, width), jnp.float32),
        whole_out((width, hidden // 2 + width // 2), jnp.bfloat16),
    ]
    scratch = [pltpu.VMEM((count, width), jnp.float32)]
    return call(mlp_back_body, (blocks,), ins, outs, scratch, prefetch=core, after=after, limit=40, name="mlp_back")


def up_mine_body(core, act, d_up, att, branch, mine):
    step = pl.program_id(0)
    tile = d_up.shape[1]
    mine[:, pl.ds(step * tile, tile)] = low(dot(act[...], d_up[...], TN))

    @pl.when(step == pl.num_programs(0) - 1)
    def _():
        mine[:, mine.shape[1] - branch.shape[1] :] = low(dot(att[...], branch[...], TN))


def up_mine(core, act, d_up, att, branch):
    count, width = act.shape
    tile = width
    blocks = d_up.shape[1] // tile // 2
    ins = [
        whole(act),
        (d_up, pl.BlockSpec((count, tile), lambda j, core: (0, core[0] * blocks + j))),
        whole(att),
        (branch, pl.BlockSpec((count, width // 2), lambda j, core: (0, core[0]))),
    ]
    outs = [whole_out((width, blocks * tile + width // 2), jnp.bfloat16)]
    return call(up_mine_body, (blocks,), ins, outs, prefetch=core, name="up_mine", cost=LONG)[0]


def project_back_body(
    first, owners, core, dq, dk, dv, dk_in, dv_in, q_pre, k_pre, wq, wk, wv, act, qg, kg, *refs
):
    if first:
        rows, one, two, back_out = refs
    else:
        tok, d_resid, gain, back_in, rows_in, up_sum, row_sums, grad_tok, one, two = refs
    tile = q_pre.shape[1]
    left = (core[0] == 0) != first

    def gain_half(ref):
        gains = vector(ref)
        return jnp.where(left, gains[:, :tile], gains[:, tile:])

    query_unit, query_scale = head_stats(q_pre[...])
    d_low = dq[...]
    qg_sum = column_sum(d_low * query_unit)
    d_query = low(head_norm_back(query_unit, query_scale, d_low * gain_half(qg)))
    key_unit, key_scale = head_stats(k_pre[...])
    d_key_low = wide(dk[...]) + wide(dk_in[...])
    kg_sum = column_sum(d_key_low * key_unit)
    d_key = low(head_norm_back(key_unit, key_scale, d_key_low * gain_half(kg)))
    d_value = low(wide(dv[...]) + wide(dv_in[...]))
    sums = (column_sum(wide(d_query)), column_sum(wide(d_value)), qg_sum, kg_sum)
    cut = one.shape[1] - tile
    one[:, :tile] = low(dot(act[...], d_query, TN))
    piece = low(dot(act[...], d_key, TN))
    one[:, tile:] = piece[:, :cut]
    two[:, : tile - cut] = piece[:, cut:]
    two[:, tile - cut : 2 * tile - cut] = low(dot(act[...], d_value, TN))
    back = dot(d_query, wq[...], NT) + dot(d_key, wk[...], NT) + dot(d_value, wv[...], NT)
    if first:
        for place, values in enumerate(sums):
            rows[place : place + 1, :] = values
        two[:, 2 * tile - cut :] = jnp.zeros((two.shape[0], 128), jnp.bfloat16)
        back_out[...] = back
        return
    grads = back_in[...] + back
    unit, scale = row_stats(wide(tok[...]))
    grad_tok[...] = d_resid[...] + norm_back(unit, scale, grads * vector(gain))
    full = [column_sum(grads * unit), column_sum(grads)]
    mine_first = core[0] == 0
    for place, values in enumerate(sums):
        other = rows_in[place : place + 1, :]
        ends = [jnp.where(mine_first, values, other), jnp.where(mine_first, other, values)]
        full.append(jnp.concatenate(ends, axis=1))
    width = back.shape[1]
    full = jnp.concatenate([row_sums[0:4, :]] + full, axis=0)
    full = jnp.concatenate([full, jnp.zeros((128 - full.shape[0], width), jnp.float32)], axis=0)
    columns = full.T
    lane = lax.broadcasted_iota(jnp.int32, columns.shape, 1)
    hidden = up_sum.shape[1]
    folds = hidden // width
    tall = jnp.broadcast_to(up_sum[...], (128, hidden)).T.reshape(owners, folds, width // owners, 128)
    for fold in range(folds):
        piece = tall[:, fold].reshape(width, 128)
        columns = jnp.where(lane == SMALL + fold, piece, columns)
    two[:, 2 * tile - cut :] = low(columns)


def project_back(first, owners, core, halves, wholes, after):
    count, width = halves[0].shape
    tile = width // 2

    def columns(array):
        return pl.BlockSpec((array.shape[0], tile), lambda j, core: (0, 1 - core[0] if first else core[0]))

    ins = [(a, columns(a)) for a in halves] + [whole(a) for a in wholes]
    grads = [whole_out((width, (3 * tile + 128) // 2), jnp.bfloat16)] * 2
    total = whole_out((count, width), jnp.float32)
    outs = [whole_out((8, tile), jnp.float32), *grads, total] if first else [total, *grads]
    name = "project_back_theirs" if first else "project_back_mine"
    body = functools.partial(project_back_body, first, owners)
    cost = 1000 if first else LONG
    return call(body, (1,), ins, outs, prefetch=core, after=after, limit=48, name=name, cost=cost)


def swap(values, axis, bit):
    count = lax.axis_size(axis)
    return lax.ppermute(values, axis, [(i, i ^ (1 << bit)) for i in range(count)])


def add_low(one, two):
    return low(wide(one) + wide(two))


def split_body(parts, side, *refs):
    mine, other = side[0], 1 - side[0]
    give, keep = refs[2 * parts :]
    start = 0
    for kept, coming in zip(refs[:parts], refs[parts : 2 * parts]):
        columns = slice(start, start + kept.shape[3])
        give[:, :, columns] = low(wide(kept[:, other]) + wide(coming[:, other]))
        keep[:, :, columns] = low(wide(kept[:, mine]) + wide(coming[:, mine]))
        start += kept.shape[3]


def merge_body(kept, coming, out):
    out[...] = low(wide(kept[...]) + wide(coming[...]))


class RowSum:
    def __init__(self, height, left, parts):
        self.height, self.left, self.parts = height, left, parts

    def send(self, bit, after=()):
        axis = self.left.index(bit)
        before, behind = 1 << axis, 1 << (len(self.left) - axis - 1)
        side = ((lax.axis_index("seq") >> bit) & 1).reshape(1)

        def view(array):
            return whole(array.reshape(before, 2, behind * self.height, array.shape[-1]))

        ins = [scalars(side)] + [view(kept) for kept, _ in self.parts] + [view(coming) for _, coming in self.parts]
        width = sum(kept.shape[-1] for kept, _ in self.parts)
        outs = [whole_out((before, behind * self.height, width), jnp.bfloat16)] * 2
        body = functools.partial(split_body, len(self.parts))
        given, kept = call(body, (1,), ins, outs, after=after, name="split")
        self.parts = [(kept, swap(given, "seq", bit))]
        self.left = [other for other in self.left if other != bit]
        return given

    def join(self, other):
        assert self.left == other.left
        return RowSum(self.height, self.left, self.parts + other.parts)

    def finish(self, after=()):
        for bit in list(reversed(self.left)):
            self.send(bit, after)
        kept, coming = self.parts[0]
        shape = (self.height, kept.shape[-1])
        ins = [whole(kept.reshape(shape)), whole(coming.reshape(shape))]
        held = call(merge_body, (1,), ins, [whole_out(shape, jnp.bfloat16)], after=after, name="merge")[0]
        for bit in range(1, lax.axis_size("blk").bit_length() - 1):
            held = add_low(held, swap(held, "blk", bit))
        return held, swap(held, "blk", 0)


def place_halves(core, held, other, out, rows, start, half):
    columns = slice(start, start + half)
    own, far = wide(held[:, columns]), wide(other[:, columns])
    first = core[0] == 0
    out[rows, :half] = jnp.where(first, own, far)
    out[rows, half:] = jnp.where(first, far, own)


def finish_ff_body(core, held, other, grad_down, grad_up, grad_out):
    height = held.shape[0]
    every = slice(0, height)
    half = grad_down.shape[1] // 2
    folds = grad_down.shape[0] // height
    for fold in range(folds):
        place_halves(core, held, other, grad_down, slice(fold * height, (fold + 1) * height), fold * half, half)
    place_halves(core, held, other, grad_up, every, folds * half, folds * half)
    place_halves(core, held, other, grad_out, every, 2 * folds * half, half)


def finish_ff(core, held, other, width, folds):
    height = held.shape[0]
    ins = [scalars(core), whole(held), whole(other)]
    shapes = ((folds * height, width), (height, folds * width), (height, width))
    outs = [whole_out(shape, jnp.float32) for shape in shapes]
    return call(finish_ff_body, (1,), ins, outs, name="finish_ff")


def finish_attention_body(core, held, other, *outs):
    half = outs[0].shape[1] // 2
    for place, out in enumerate(outs[:3]):
        place_halves(core, held, other, out, slice(0, held.shape[0]), place * half, half)
    sums = (wide(held[:, 3 * half :]) + wide(other[:, 3 * half :])).T
    for place, out in enumerate(outs[3:-1]):
        out[...] = sums[place : place + 1]
    folds = outs[-1].shape[0]
    outs[-1][...] = sums[SMALL : SMALL + folds]


def finish_attention(core, held, other, width, folds):
    ins = [scalars(core), whole(held), whole(other)]
    height = held.shape[0]
    outs = [whole_out((height, width), jnp.float32)] * 3
    outs += [whole_out((1, height), jnp.float32)] * SMALL + [whole_out((folds, height), jnp.float32)]
    return call(finish_attention_body, (1,), ins, outs, name="finish_attention")


def local(
    tokens,
    image_lengths,
    cotangent,
    ln1_gain,
    ln1_bias,
    w_query,
    b_query,
    w_key,
    w_value,
    b_value,
    q_gain,
    k_gain,
    w_out,
    b_out,
    ln2_gain,
    ln2_bias,
    w_up,
    b_up,
    w_down,
    b_down,
):
    sequences, span, width = tokens.shape
    owners = lax.axis_size("seq")
    blocks = lax.axis_size("blk")
    place = lax.axis_index("blk")
    core = (place & 1).reshape(1)
    tok = tokens.reshape(-1, width)
    cot = cotangent.reshape(-1, width)

    def split(array):
        return array.reshape(array.shape[:-2] + (sequences, -1, width))

    def flat(array):
        return array.reshape(array.shape[:-3] + (-1, width))

    q8, pair, act_one, q_pre, k_pre = projections(
        tok, ln1_gain, ln1_bias, w_query, b_query, w_key, w_value, b_value, q_gain, k_gain
    )
    q8, pair = split(q8), split(pair)
    if blocks == 2:
        pairs = [pair, swap(pair, "blk", 0)]
        starts = jnp.stack([place * span, place * span, (1 - place) * span])
    else:
        pairs = [lax.all_gather(pair, "blk", axis=2, tiled=True)]
        starts = jnp.stack([place * span, place * 0])
    starts = starts.astype(jnp.int32)
    att, inverse = attend(image_lengths, starts, q8, pairs)
    height = width // owners
    folds = w_up.shape[1] // width
    bits = list(reversed(range(owners.bit_length() - 1)))
    out, resid, act_two, hidden, d_up, theirs = mlp(
        height, core, flat(att), tok, cot, w_out, b_out, ln2_gain, ln2_bias, w_up, b_up, w_down, b_down
    )
    arrived = swap(theirs, "blk", 0)
    down = RowSum(height, bits, [(down_mine(height, core, hidden, cot), arrived)])
    given = down.send(0)
    d_resid, branch, d_att, up_sum, row_sums, theirs = mlp_back(
        core, d_up, act_two, w_up, resid, cot, ln2_gain, w_out, flat(att), [given]
    )
    arrived = swap(theirs, "blk", 0)
    up = RowSum(height, bits, [(up_mine(core, act_two, d_up, flat(att), branch), arrived)])
    given = up.send(1)
    dq, *d_pairs = attend_back(image_lengths, starts, q8, att, split(d_att), inverse, pairs, [given])
    if blocks == 2:
        dk, dk_far, dv, dv_far = d_pairs
        dk_far, dv_far = swap(dk_far, "blk", 0), swap(dv_far, "blk", 0)
    else:
        dk, dv = (lax.psum_scatter(part, "blk", scatter_dimension=1, tiled=True) for part in d_pairs)
        dk_far, dv_far = jnp.zeros_like(dk), jnp.zeros_like(dv)
    given = down.send(1, [dq])
    halves = [flat(a) for a in (dq, dk, dv, dk_far, dv_far)] + [q_pre, k_pre, w_query, w_key, w_value]
    wholes = [act_one, q_gain, k_gain]
    rows, theirs_one, theirs_two, back = project_back(True, owners, core, halves, wholes, [given])
    arrived_one, arrived_two = swap(theirs_one, "blk", 0), swap(theirs_two, "blk", 0)
    given = up.send(0, [rows])
    wholes += [tok, d_resid, ln1_gain, back, rows, up_sum, row_sums]
    grad_tok, mine_one, mine_two = project_back(False, owners, core, halves, wholes, [given])
    one = RowSum(height, bits, [(mine_one, arrived_one)])
    two = RowSum(height, bits, [(mine_two, arrived_two)])
    given = [one.send(0), two.send(1)]
    ff = down.join(up)
    given = [ff.send(2, given)]
    given = [one.send(1, given), two.send(0, given)]
    given = [ff.send(3, given)]
    rest = one.join(two)
    given = [rest.send(2, given)]
    grad_down, grad_up, grad_out = finish_ff(core, *ff.finish(given), width, folds)
    grad_q, grad_k, grad_v, *vectors = finish_attention(core, *rest.finish(given), width, folds)
    t_ln2g, t_ln2b, t_bo, t_bd, t_ln1g, t_ln1b, t_bq, t_bv, t_qg, t_kg, t_bu = (v.reshape(-1) for v in vectors)
    return (
        out.reshape(tokens.shape),
        grad_tok.reshape(tokens.shape),
        t_ln1g,
        t_ln1b,
        grad_q,
        t_bq,
        grad_k,
        grad_v,
        t_bv,
        t_qg,
        t_kg,
        grad_out,
        t_bo,
        t_ln2g,
        t_ln2b,
        grad_up,
        t_bu,
        grad_down,
        t_bd,
    )


def solution(mesh):
    return jax.shard_map(
        local,
        mesh=mesh,
        in_specs=(
            P("seq", "blk", None),
            P("seq", None),
            P("seq", "blk", None),
            P(),
            P(),
            P(),
            P(),
            P(),
            P(),
            P(),
            P(),
            P(),
            P(),
            P(),
            P(),
            P(),
            P(),
            P(),
            P(),
            P(),
        ),
        out_specs=(
            P("seq", "blk", None),
            P("seq", "blk", None),
            P("seq"),
            P("seq"),
            P("seq", None),
            P("seq"),
            P("seq", None),
            P("seq", None),
            P("seq"),
            P("seq"),
            P("seq"),
            P("seq", None),
            P("seq"),
            P("seq"),
            P("seq"),
            P("seq", None),
            P("seq"),
            P("seq", None),
            P("seq"),
        ),
        check_vma=False,
    )
```

```python
import functools
import math

import jax
import jax.numpy as jnp
from jax import lax
from jax.experimental import pallas as pl
from jax.experimental.pallas import tpu as pltpu
from jax.sharding import PartitionSpec as P

H = 12
HD = 64
EPSILON = 1e-06
BLOCKED = -1024.0
MIB = 1 << 20
LONG = 10**12
SMALL = 10
NT = (((1,), (1,)), ((), ()))
TN = (((0,), (0,)), ((), ()))
NN = (((1,), (0,)), ((), ()))


def dot(one, two, dims=NN):
    return lax.dot_general(one, two, dims, preferred_element_type=jnp.float32)


def low(values):
    return values.astype(jnp.bfloat16)


def wide(values):
    return values.astype(jnp.float32)


def row_stats(values):
    average = jnp.mean(values, axis=-1, keepdims=True)
    centred = values - average
    variance = jnp.mean(centred * centred, axis=-1, keepdims=True)
    scale = lax.rsqrt(variance + EPSILON)
    return centred * scale, scale


def norm_back(unit, scale, grads):
    return scale * (
        grads
        - jnp.mean(grads, axis=-1, keepdims=True)
        - unit * jnp.mean(grads * unit, axis=-1, keepdims=True)
    )


def head_mean(values, exact=False):
    parts = []
    for start in range(0, values.shape[1], 4 * HD):
        part = values[:, start : start + 4 * HD]
        width = part.shape[1]
        rows = lax.broadcasted_iota(jnp.int32, (width, width), 0) // HD
        columns = lax.broadcasted_iota(jnp.int32, (width, width), 1) // HD
        average = jnp.where(rows == columns, 1.0 / HD, 0.0).astype(jnp.bfloat16)
        upper = low(part)
        total = dot(upper, average)
        if exact:
            total = total + dot(low(part - wide(upper)), average)
        parts.append(total)
    return jnp.concatenate(parts, axis=1)


def head_stats(values):
    centred = values - head_mean(values, exact=True)
    scale = lax.rsqrt(head_mean(centred * centred) + EPSILON)
    return centred * scale, scale


def head_norm_back(unit, scale, grads):
    return scale * (grads - head_mean(grads) - unit * head_mean(grads * unit))


def vector(ref):
    return wide(ref[...]).reshape(1, -1)


def column_sum(values):
    return jnp.sum(values, axis=0, keepdims=True)


def call(body, grid, ins, outs, scratch=(), prefetch=None, after=(), limit=24, name=None, cost=1000):
    ins = list(ins) + [(array, pl.BlockSpec(memory_space=pl.ANY)) for array in after]
    lead = len(ins) - len(after) + (prefetch is not None)

    def kernel(*refs):
        body(*refs[:lead], *refs[lead + len(after) :])

    grid_spec = pltpu.PrefetchScalarGridSpec(
        num_scalar_prefetch=int(prefetch is not None),
        grid=grid,
        in_specs=[spec for _, spec in ins],
        out_specs=[spec for _, spec in outs],
        scratch_shapes=list(scratch),
    )
    arrays = [array for array, _ in ins]
    return pl.pallas_call(
        kernel,
        grid_spec=grid_spec,
        out_shape=[shape for shape, _ in outs],
        compiler_params=pltpu.CompilerParams(vmem_limit_bytes=limit * MIB),
        name=name,
        cost_estimate=pl.CostEstimate(flops=cost, bytes_accessed=1000, transcendentals=0),
    )(*([] if prefetch is None else [prefetch]), *arrays)


def whole(array):
    rank = len(array.shape)
    return (array, pl.BlockSpec(array.shape, lambda *_: (0,) * rank))


def whole_out(shape, dtype):
    rank = len(shape)
    return (jax.ShapeDtypeStruct(shape, dtype), pl.BlockSpec(shape, lambda *_: (0,) * rank))


def scalars(array):
    return (array, pl.BlockSpec(memory_space=pltpu.SMEM))


def project_body(gain, bias, bq, bv, qg, kg, *refs):
    sources, refs = refs[:4], refs[4:]
    act_hbm, pair_hbm, k_hbm, q_hbm, q8_hbm = refs[:5]
    targets, refs = refs[5:9], refs[9:]
    act, pair, k_pre, q_pre, q8, got, put = refs
    loads = [pltpu.make_async_copy(a, b, got.at[i]) for i, (a, b) in enumerate(zip(sources, targets))]
    for load in loads:
        load.start()
    sends = []

    def send(source, target):
        copy = pltpu.make_async_copy(source, target, put.at[len(sends)])
        copy.start()
        sends.append(copy)

    tok, wv, wk, wq = targets
    loads[0].wait()
    unit, _ = row_stats(wide(tok[...]))
    act_one = low(unit * vector(gain) + vector(bias))
    act[...] = act_one
    send(act, act_hbm)
    loads[1].wait()
    pair[1] = low(dot(act_one, wv[...]) + vector(bv))
    send(pair.at[1], pair_hbm.at[1])
    loads[2].wait()
    key_unit, key_scale = head_stats(dot(act_one, wk[...]))
    pair[0] = low(key_unit * vector(kg))
    send(pair.at[0], pair_hbm.at[0])
    k_pre[0] = low(key_unit)
    k_pre[1] = low(key_scale)
    send(k_pre, k_hbm)
    loads[3].wait()
    query_unit, query_scale = head_stats(dot(act_one, wq[...]) + vector(bq))
    q8[...] = low(query_unit * vector(qg)) * (1.0 / math.sqrt(HD))
    send(q8, q8_hbm)
    q_pre[0] = low(query_unit)
    q_pre[1] = low(query_scale)
    send(q_pre, q_hbm)
    for copy in sends:
        copy.wait()


def projections(tok, gain, bias, wq, bq, wk, wv, bv, qg, kg):
    count, width = tok.shape
    anywhere = pl.BlockSpec(memory_space=pl.ANY)
    sources = (tok, wv, wk, wq)
    ins = [whole(a) for a in (gain, bias, bq, bv, qg, kg)] + [(a, anywhere) for a in sources]

    def rows(dtype):
        return jax.ShapeDtypeStruct((count, width), dtype)

    pair = jax.ShapeDtypeStruct((2, count, width), jnp.bfloat16)
    results = (rows(jnp.bfloat16), pair, pair, pair, rows(jnp.bfloat16))
    outs = [(a, anywhere) for a in results]
    scratch = [pltpu.VMEM(a.shape, a.dtype) for a in sources + results]
    scratch += [pltpu.SemaphoreType.DMA((4,)), pltpu.SemaphoreType.DMA((6,))]
    return call(project_body, (1,), ins, outs, scratch, limit=60, name="projections")


def segment_column(positions, lengths, sequence, slots):
    end = lengths[sequence, 0]
    segment = (positions >= end).astype(jnp.int32)
    for slot in range(1, slots):
        end = end + lengths[sequence, slot]
        segment = segment + (positions >= end).astype(jnp.int32)
    return segment


def query_lanes(count, start, lengths, sequence, slots):
    positions = lax.broadcasted_iota(jnp.int32, (count, 2 * HD), 0) + start
    lane = lax.broadcasted_iota(jnp.int32, (count, 2 * HD), 1) & (HD - 1)
    segment = segment_column(positions, lengths, sequence, slots)
    return jnp.where(segment == lane, 1.0, 0.0).astype(jnp.bfloat16)


def key_lanes(count, start, lengths, sequence, slots):
    positions = lax.broadcasted_iota(jnp.int32, (count, 2 * HD), 0) + start
    lane = lax.broadcasted_iota(jnp.int32, (count, 2 * HD), 1) & (HD - 1)
    segment = segment_column(positions, lengths, sequence, slots)
    open_to = (segment == lane) & (lane < slots)
    return jnp.where(open_to, 0.0, BLOCKED).astype(jnp.bfloat16)


def pair_spec(array):
    return (array, pl.BlockSpec((1, array.shape[1], 2 * HD), lambda s, h: (s, 0, h)))


def low_half(count):
    return lax.broadcasted_iota(jnp.int32, (count, 2 * HD), 1) < HD


def attend_pair(slots, lengths, starts, q8, pairs, q_mask, k_masks, sequence, place):
    span = q8.shape[1]

    @pl.when(place == 0)
    def _():
        q_mask[...] = query_lanes(span, starts[0], lengths, sequence, slots)
        for chunk, mask in enumerate(k_masks):
            mask[...] = key_lanes(mask.shape[0], starts[1 + chunk], lengths, sequence, slots)

    first = low_half(span)
    query = q8[0]
    one = jnp.where(first, query, q_mask[...])
    two = jnp.where(first, q_mask[...], query)
    sums = [None, None]
    for pair, k_mask in zip(pairs, k_masks):
        key, value, mask = pair[0, 0], pair[1, 0], k_mask[...]
        key_first = low_half(key.shape[0])
        ones = jnp.ones_like(value)
        for side, operand in enumerate((one, two)):
            pick = key_first if side == 0 else ~key_first
            lifted = low(jnp.exp(dot(operand, jnp.where(pick, key, mask), NT)))
            term = dot(lifted, jnp.where(pick, value, ones))
            sums[side] = term if sums[side] is None else sums[side] + term
    top = jnp.where(first, sums[0], sums[1])
    total = pltpu.roll(jnp.where(first, sums[1], sums[0]), HD, 1)
    inverse = jnp.where(total > 0.0, 1.0 / total, 0.0)
    return low(top * inverse), inverse


def attend_back_pair(query, queries, d_low, d_values, pairs, k_masks):
    key_grads, value_grads, d_query_t = [], [], None
    for pair, k_mask in zip(pairs, k_masks):
        key, value, mask = pair[0, 0], pair[1, 0], k_mask[...]
        key_first = low_half(key.shape[0])
        ones = jnp.ones_like(value)
        key_t = key.T
        key_terms, value_terms, query_terms = [], [], []
        for side in range(2):
            pick = key_first if side == 0 else ~key_first
            lifted = jnp.exp(dot(jnp.where(pick, key, mask), queries[side], NT))
            shifted = dot(jnp.where(pick, value, ones), d_values[side], NT)
            d_scores = low(lifted * shifted)
            value_terms.append(dot(low(lifted), d_low))
            key_terms.append(dot(d_scores, query))
            query_terms.append(dot(key_t[side * HD : (side + 1) * HD], d_scores))
        key_grads.append(low(jnp.where(key_first, key_terms[0], key_terms[1])))
        value_grads.append(low(jnp.where(key_first, value_terms[0], value_terms[1])))
        term = jnp.concatenate(query_terms, axis=0)
        d_query_t = term if d_query_t is None else d_query_t + term
    return d_query_t.T * (1.0 / math.sqrt(HD)), key_grads, value_grads


def delta_lanes(att, d_low, pick):
    lane = lax.broadcasted_iota(jnp.int32, att.shape, 1) & (HD - 1)
    delta = -jnp.sum(jnp.where(pick, wide(att) * wide(d_low), 0.0), axis=1, keepdims=True)
    high = low(delta)
    middle = low(delta - wide(high))
    rest = low(delta - wide(high) - wide(middle))
    zero = jnp.zeros((), jnp.bfloat16)
    extra = jnp.where(lane == 0, high, jnp.where(lane == 1, middle, jnp.where(lane == 2, rest, zero)))
    return jnp.where(pick, d_low, extra)


def attend_back_body(slots, chunks, core, lengths, starts, gain, q8, inverse, *refs):
    pairs, refs = refs[:chunks], refs[chunks:]
    sources, refs = refs[:6], refs[6:]
    d_query, refs = refs[0], refs[1:]
    d_keys, d_vals, refs = refs[:chunks], refs[chunks : 2 * chunks], refs[2 * chunks :]
    rows, d_resid_hbm, grad_mine, grad_theirs = refs[:4]
    q_mask, refs = refs[4], refs[5:]
    k_masks, targets, refs = refs[:chunks], refs[chunks : chunks + 6], refs[chunks + 6 :]
    d_own, d_far, resid, cot, w_out, att = targets
    d_att, back, got, put = refs
    span, width = q8.shape[1], resid.shape[1]
    heads = H // 2
    step = pl.program_id(0)
    sequence, place = step // heads, step % heads

    def fetch(number):
        return pltpu.make_async_copy(sources[number], targets[number], got.at[number])

    def send_back():
        return pltpu.make_async_copy(back, d_resid_hbm, put.at[0])

    @pl.when(step == 0)
    def _():
        for number in range(6):
            fetch(number).start()
        for number in range(6):
            fetch(number).wait()
        grads = wide(d_own[...]) + wide(d_far[...])
        unit, scale = row_stats(resid[...])
        rows[0:1, :] = column_sum(grads * unit)
        rows[1:2, :] = column_sum(grads)
        total = wide(cot[...]) + norm_back(unit, scale, grads * vector(gain))
        back[...] = total
        send_back().start()
        branch = low(total)
        rows[2:3, :] = column_sum(wide(branch))
        rows[3:4, :] = column_sum(wide(cot[...]))
        d_att[...] = low(dot(branch, w_out[...], NT))
        product = low(dot(att[...], branch, TN))
        half = width // 2
        for side in range(2):

            @pl.when(core[0] == side)
            def _():
                grad_mine[...] = product[:, side * half : (side + 1) * half]
                grad_theirs[...] = product[:, (1 - side) * half : (2 - side) * half]

    @pl.when(place == 0)
    def _():
        q_mask[...] = query_lanes(span, starts[0], lengths, sequence, slots)
        for chunk, mask in enumerate(k_masks):
            mask[...] = key_lanes(mask.shape[0], starts[1 + chunk], lengths, sequence, slots)

    block = (pl.ds(sequence * span, span), pl.ds(pl.multiple_of(place * 128, 128), 128))
    first = low_half(span)
    query = q8[0]
    queries = (jnp.where(first, query, q_mask[...]), jnp.where(first, q_mask[...], query))
    d_low = low(wide(d_att[block]) * wide(inverse[0]))
    held = att[block]
    d_values = [delta_lanes(held, d_low, first), delta_lanes(held, d_low, ~first)]
    grads, key_grads, value_grads = attend_back_pair(query, queries, d_low, d_values, pairs, k_masks)
    d_query[0] = low(grads)
    for chunk in range(chunks):
        d_keys[chunk][0] = key_grads[chunk]
        d_vals[chunk][0] = value_grads[chunk]

    @pl.when(step == pl.num_programs(0) - 1)
    def _():
        send_back().wait()


def pair_block(array, lead, steps):
    heads = H // 2

    def index(i, *_):
        i = jnp.minimum(i, steps - 1)
        return (i // heads, 0, i % heads)

    shape = (1, array.shape[-2], 2 * HD)
    if lead:
        return (array, pl.BlockSpec((2,) + shape, lambda i, *_: (0,) + index(i)))
    return (array, pl.BlockSpec(shape, index))


def attend_back(core, lengths, starts, gain, q8, inverse, pairs, sources, after):
    count, span, width = q8.shape
    steps = count * H // 2
    tokens = count * span
    anywhere = pl.BlockSpec(memory_space=pl.ANY)

    def shape(sizes, dtype):
        return jax.ShapeDtypeStruct(sizes, dtype)

    ins = [scalars(core), scalars(lengths), scalars(starts), whole(gain)]
    ins += [pair_block(q8, False, steps), pair_block(inverse, False, steps)]
    ins += [pair_block(a, True, steps) for a in pairs] + [(a, anywhere) for a in sources]
    outs = [pair_block(shape((count, span, width), jnp.bfloat16), False, steps)]
    outs += [pair_block(shape(a.shape[1:], jnp.bfloat16), False, steps) for a in pairs + pairs]
    outs += [
        whole_out((8, width), jnp.float32),
        (shape((tokens, width), jnp.float32), anywhere),
        whole_out((width, width // 2), jnp.bfloat16),
        whole_out((width, width // 2), jnp.bfloat16),
    ]
    scratch = [pltpu.VMEM((a.shape[-2], 2 * HD), jnp.bfloat16) for a in [q8] + list(pairs)]
    scratch += [pltpu.VMEM(a.shape, a.dtype) for a in sources]
    scratch += [pltpu.VMEM((tokens, width), d) for d in (jnp.bfloat16, jnp.float32)]
    scratch += [pltpu.SemaphoreType.DMA((6,)), pltpu.SemaphoreType.DMA((1,))]
    body = functools.partial(attend_back_body, lengths.shape[1], len(pairs))
    return call(body, (steps,), ins, outs, scratch, after=after, limit=60, name="attend_back")


def gelu_pair(values):
    half = 0.5 + 0.5 * lax.erf(values * math.sqrt(0.5))
    slope = half + values * (math.sqrt(0.5 / math.pi) * jnp.exp(-0.5 * values * values))
    return values * half, slope


def layer_body(resid, own, far, bias, out):
    out[...] = low(resid[...] + wide(own[...]) + wide(far[...]) + vector(bias))


def layer(resid, own, far, bias, after):
    count, width = resid.shape
    spec = pl.BlockSpec((count // 2, width), lambda i: (i, 0))
    ins = [(resid, spec), (own, spec), (far, spec), whole(bias)]
    outs = [(jax.ShapeDtypeStruct((count, width), jnp.bfloat16), spec)]
    return call(layer_body, (2,), ins, outs, after=after, limit=60, name="layer", cost=LONG)[0]


def attend_body(slots, chunks, lengths, starts, b_out, gain, bias, q8, *refs):
    pairs, refs = refs[:chunks], refs[chunks:]
    sources, refs = refs[:2], refs[2:]
    att, inverse, resid, act, q_mask = refs[:5]
    k_masks, refs = refs[5 : 5 + chunks], refs[5 + chunks :]
    tok, w_out, held, got = refs
    span = q8.shape[1]
    heads = H // 2
    step = pl.program_id(0)
    last = pl.num_programs(0) - 1
    targets = (tok, w_out)

    def fetch(number):
        return pltpu.make_async_copy(sources[number], targets[number], got.at[number])

    @pl.when(step == 0)
    def _():
        fetch(0).start()
        fetch(1).start()

    @pl.when(step < last)
    def _():
        sequence, place = step // heads, step % heads
        values, inv = attend_pair(slots, lengths, starts, q8, pairs, q_mask, k_masks, sequence, place)
        att[0] = values
        inverse[0] = low(inv)
        held[pl.ds(sequence * span, span), pl.ds(pl.multiple_of(place * 128, 128), 128)] = values

    @pl.when(step == last)
    def _():
        fetch(0).wait()
        fetch(1).wait()
        total = wide(tok[...]) + dot(held[...], w_out[...]) + vector(b_out)
        resid[...] = total
        act[...] = low(row_stats(total)[0] * vector(gain) + vector(bias))


def attend(lengths, starts, b_out, gain, bias, q8, pairs, tok, w_out):
    count, span, width = q8.shape
    steps = count * H // 2
    tokens = count * span
    anywhere = pl.BlockSpec(memory_space=pl.ANY)

    def shape(dtype):
        return jax.ShapeDtypeStruct((count, span, width), dtype)

    ins = [scalars(lengths), scalars(starts)] + [whole(a) for a in (b_out, gain, bias)]
    ins += [pair_block(q8, False, steps)] + [pair_block(a, True, steps) for a in pairs]
    ins += [(tok, anywhere), (w_out, anywhere)]
    outs = [
        pair_block(shape(jnp.bfloat16), False, steps),
        pair_block(shape(jnp.bfloat16), False, steps),
        whole_out((tokens, width), jnp.float32),
        whole_out((tokens, width), jnp.bfloat16),
    ]
    scratch = [pltpu.VMEM((a.shape[-2], 2 * HD), jnp.bfloat16) for a in [q8] + list(pairs)]
    scratch += [pltpu.VMEM(tok.shape, jnp.bfloat16), pltpu.VMEM(w_out.shape, jnp.bfloat16)]
    scratch += [pltpu.VMEM(tok.shape, jnp.bfloat16), pltpu.SemaphoreType.DMA((2,))]
    body = functools.partial(attend_body, lengths.shape[1], len(pairs))
    return call(body, (steps + 1,), ins, outs, scratch, limit=60, name="attend")


def feed_body(
    height, core, spot, act, act_far, cot, cot_far, w_up, w_down, b_up,
    up_sum, out_own, out_far, d_own, d_far, hbm_0, hbm_1, hbm_2, hbm_3, own_out, own_d, far_out, far_d, grads, put,
):
    step = pl.program_id(0)
    width, tile = w_up.shape
    steps = pl.num_programs(0)
    start = (core[0] * steps + step) * tile
    bias = wide(b_up[pl.ds(pl.multiple_of(start, tile), tile)]).reshape(1, -1)
    @pl.when(step == 0)
    def _():
        for ref in (own_out, own_d, far_out, far_d):
            ref[...] = jnp.zeros_like(ref)

    down_grads = up_grads = sums = None
    for values, upper, out_sum, d_sum in ((act, cot, own_out, own_d), (act_far, cot_far, far_out, far_d)):
        hidden, slope = gelu_pair(dot(values[...], w_up[...]) + bias)
        hidden = low(hidden)
        d_up = low(dot(upper[...], w_down[...], NT) * slope)
        out_sum[...] += dot(hidden, w_down[...])
        d_sum[...] += dot(d_up, w_up[...], NT)
        down_term = dot(hidden, upper[...], TN)
        up_term = dot(values[...], d_up, TN)
        sum_term = column_sum(wide(d_up))
        down_grads = down_term if down_grads is None else down_grads + down_term
        up_grads = up_term if up_grads is None else up_grads + up_term
        sums = sum_term if sums is None else sums + sum_term
    up_sum[...] = sums
    owners = width // height
    rows = grads.shape[1]
    folds = grads.shape[2] // width // 2
    here = tile // (folds * height)
    tall = down_grads.reshape(here // 4, 4, folds, height, width)
    broad = up_grads.reshape(2, owners // 8, 4, height, tile)
    lines = pl.ds(pl.multiple_of(step * (here // 4 * height), 16), here // 4 * height)
    for place in range(4):
        which = place ^ spot[0]
        for fold in range(folds):
            piece = low(tall[:, place, fold].reshape(here // 4 * height, width))
            grads[which, lines, fold * width : (fold + 1) * width] = piece
        for top in range(2):
            columns = pl.ds(pl.multiple_of(folds * width + (2 * step + top) * tile, tile), tile)
            grads[which, :, columns] = low(broad[top, :, place].reshape(rows, tile))

    @pl.when(step == steps - 1)
    def _():
        sends = [
            pltpu.make_async_copy(grads.at[place], target, put.at[place])
            for place, target in enumerate((hbm_0, hbm_1, hbm_2, hbm_3))
        ]
        for send in sends:
            send.start()
        d_far[...] = low(far_d[...])
        d_own[...] = low(own_d[...])
        out_far[...] = low(far_out[...])
        out_own[...] = low(own_out[...])
        for send in sends:
            send.wait()


def feed(height, core, spot, act, act_far, cot, cot_far, w_up, w_down, b_up):
    count, width = act.shape
    hidden = w_up.shape[1]
    steps = hidden // width // 2
    ins = [scalars(spot)] + [whole(a) for a in (act, act_far, cot, cot_far)]
    ins += [
        (w_up, pl.BlockSpec((width, width), lambda j, core: (0, core[0] * steps + j))),
        (w_down, pl.BlockSpec((width, width), lambda j, core: (core[0] * steps + j, 0))),
        whole(b_up),
    ]
    up_sum = (
        jax.ShapeDtypeStruct((1, hidden // 2), jnp.float32),
        pl.BlockSpec((1, width), lambda j, core: (0, j)),
    )
    half_sum = whole_out((count, width), jnp.bfloat16)
    part = jax.ShapeDtypeStruct((width // 8, 2 * hidden), jnp.bfloat16)
    outs = [up_sum] + [half_sum] * 4 + [(part, pl.BlockSpec(memory_space=pl.ANY))] * 4
    scratch = [pltpu.VMEM((count, width), jnp.float32)] * 4 + [pltpu.VMEM((4,) + part.shape, jnp.bfloat16)]
    scratch += [pltpu.SemaphoreType.DMA((4,))]
    body = functools.partial(feed_body, height)
    return call(body, (steps,), ins, outs, scratch, prefetch=core, limit=60, name="feed")


def project_back_body(owners, parts, core, qg, kg, gain, up_sum, row_sums, *refs):
    sources, refs = refs[:parts], refs[parts:]
    grad_hbm, mine_q, mine_k, mine_two, theirs_q, theirs_k, theirs_two = refs[:7]
    targets, refs = refs[7 : 7 + parts], refs[7 + parts :]
    grad, one, two, got, put = refs
    copies = [pltpu.make_async_copy(a, b, got.at[i]) for i, (a, b) in enumerate(zip(sources, targets))]
    for copy in copies:
        copy.start()
    waited = set()

    def use(*places):
        for place in places:
            if place not in waited:
                copies[place].wait()
                waited.add(place)
        return [targets[place] for place in places]

    def joined(*places):
        return jnp.concatenate([wide(ref[...]) for ref in use(*places)], axis=1)

    act, wv, wk, wq = 0, 3, 7, 10
    half = one.shape[2] // 2

    side_one = core[0] == 0

    def place_pieces(piece, spots):
        left, right = piece[:, :half], piece[:, half:]
        own, far = jnp.where(side_one, left, right), jnp.where(side_one, right, left)
        for target, start, first, last in spots:
            columns = slice(start, start + last - first)
            target[0, :, columns] = own[:, first:last]
            target[1, :, columns] = far[:, first:last]

    d_value = low(joined(1) + joined(2))
    (act_ref,) = use(act)
    place_pieces(low(dot(act_ref[...], d_value, TN)), ((two, 0, 0, half),))
    bv_sum = column_sum(wide(d_value))
    (w_ref,) = use(wv)
    back = dot(d_value, w_ref[...], NT)
    d_key_low = joined(4) + joined(5)
    (pre,) = use(6)
    unit, scale = wide(pre[0]), wide(pre[1])
    kg_sum = column_sum(d_key_low * unit)
    d_key = low(head_norm_back(unit, scale, d_key_low * vector(kg)))
    place_pieces(low(dot(act_ref[...], d_key, TN)), ((one, half, 0, half),))
    sends = []

    def send(source, target):
        copy = pltpu.make_async_copy(source, target, put.at[len(sends)])
        copy.start()
        sends.append(copy)

    send(two.at[0, :, :half], mine_two.at[:, :half])
    two[1, :, half:] = jnp.zeros((two.shape[1], 128), jnp.bfloat16)
    send(two.at[1], theirs_two)
    send(one.at[1, :, half:], theirs_k)
    send(one.at[0, :, half:], mine_k)
    (w_ref,) = use(wk)
    back = back + dot(d_key, w_ref[...], NT)
    d_low = joined(8)
    (pre,) = use(9)
    unit, scale = wide(pre[0]), wide(pre[1])
    qg_sum = column_sum(d_low * unit)
    d_query = low(head_norm_back(unit, scale, d_low * vector(qg)))
    bq_sum = column_sum(wide(d_query))
    place_pieces(low(dot(act_ref[...], d_query, TN)), ((one, 0, 0, half),))
    send(one.at[0, :, :half], mine_q)
    send(one.at[1, :, :half], theirs_q)
    (w_ref,) = use(wq)
    grads = back + dot(d_query, w_ref[...], NT)
    tok, d_resid = use(11, 12)
    unit, scale = row_stats(wide(tok[...]))
    grad[...] = d_resid[...] + norm_back(unit, scale, grads * vector(gain))
    send(grad, grad_hbm)
    full = [row_sums[0:4, :], column_sum(grads * unit), column_sum(grads), bq_sum, bv_sum, qg_sum, kg_sum]
    full = jnp.concatenate(full, axis=0)
    width = full.shape[1]
    full = jnp.concatenate([full, jnp.zeros((128 - full.shape[0], width), jnp.float32)], axis=0)
    columns = full.T
    lane = lax.broadcasted_iota(jnp.int32, columns.shape, 1)
    hidden = 2 * up_sum.shape[1]
    folds = hidden // width
    first = core[0] == 0
    halves = [jnp.where(first, up_sum[...], 0.0), jnp.where(first, 0.0, up_sum[...])]
    tall = jnp.broadcast_to(jnp.concatenate(halves, axis=1), (128, hidden)).T.reshape(owners, folds, width // owners, 128)
    for fold in range(folds):
        piece = tall[:, fold].reshape(width, 128)
        columns = jnp.where(lane == SMALL + fold, piece, columns)
    end = slice(half, half + 128)
    two[0, :, end] = low(columns)
    send(two.at[0, :, end], mine_two.at[:, end])
    for copy in sends:
        copy.wait()


def project_back(owners, core, vectors, sources, after):
    act = sources[0]
    count, width = act.shape
    anywhere = pl.BlockSpec(memory_space=pl.ANY)
    ins = [scalars(core)] + [whole(a) for a in vectors] + [(a, anywhere) for a in sources]
    one = jax.ShapeDtypeStruct((width, width), jnp.bfloat16)
    two = jax.ShapeDtypeStruct((width, width // 2 + 128), jnp.bfloat16)
    total = jax.ShapeDtypeStruct((count, width), jnp.float32)
    piece = jax.ShapeDtypeStruct((width, width // 2), jnp.bfloat16)
    outs = [(a, anywhere) for a in (total, piece, piece, two, piece, piece, two)]
    scratch = [pltpu.VMEM(a.shape, a.dtype) for a in sources]
    scratch += [pltpu.VMEM(total.shape, total.dtype)] + [pltpu.VMEM((2,) + a.shape, a.dtype) for a in (one, two)]
    scratch += [pltpu.SemaphoreType.DMA((len(sources),)), pltpu.SemaphoreType.DMA((8,))]
    body = functools.partial(project_back_body, owners, len(sources))
    return call(body, (1,), ins, outs, scratch, after=after, limit=60, name="project_back", cost=1000)


def swap(values, axis, bit):
    count = lax.axis_size(axis)
    return lax.ppermute(values, axis, [(i, i ^ (1 << bit)) for i in range(count)])


def add_low(one, two):
    return low(wide(one) + wide(two))


def split_body(counts, side, *refs):
    total = sum(sum(count) for count in counts)
    inputs, outs = refs[:total], refs[total:]
    place = 0
    for group, count in enumerate(counts):
        give, keep = outs[2 * group : 2 * group + 2]
        mine = side[group]
        start = 0
        for terms in count:
            columns = slice(start, start + inputs[place].shape[3])
            for half, out in ((1 - mine, give), (mine, keep)):
                held = wide(inputs[place][:, half])
                for other in range(place + 1, place + terms):
                    held = held + wide(inputs[other][:, half])
                out[:, :, columns] = low(held)
            start += inputs[place].shape[3]
            place += terms


def merge_body(parts, *refs):
    out = refs[-1]
    start = 0
    for kept, coming in zip(refs[:parts], refs[parts : 2 * parts]):
        columns = slice(start, start + kept.shape[1])
        out[:, columns] = low(wide(kept[...]) + wide(coming[...]))
        start += kept.shape[1]


def merge(parts, after):
    height, width = parts[0][0].shape[0], sum(kept.shape[1] for kept, _ in parts)
    ins = [whole(kept) for kept, _ in parts] + [whole(coming) for _, coming in parts]
    outs = [whole_out((height, width), jnp.bfloat16)]
    held = call(functools.partial(merge_body, len(parts)), (1,), ins, outs, after=after, name="merge")[0]
    for bit in range(1, lax.axis_size("blk").bit_length() - 1):
        held = add_low(held, swap(held, "blk", bit))
    return held, swap(held, "blk", 0)


def top_body(tile, side, kept, coming, down, give, keep):
    total = wide(kept[...]) + wide(coming[...])
    width = down.shape[1]
    down[...] = low(total[:, :width])
    for block in range(give.shape[1] // tile):
        columns = slice(block * tile, (block + 1) * tile)
        for top in range(2):
            start = width + (2 * block + top) * tile
            piece = low(total[:, start : start + tile])

            @pl.when(side[0] == top)
            def _():
                keep[:, columns] = piece

            @pl.when(side[0] != top)
            def _():
                give[:, columns] = piece


def send_top(ff, tile, folds, after):
    owners, blocks = lax.axis_size("seq"), lax.axis_size("blk")
    top = owners.bit_length() - 2
    side = ((lax.axis_index("seq") >> top) & 1).reshape(1)
    kept, coming = (a.reshape(ff.height, -1) for a in ff.parts[0])
    ins = [scalars(side), whole(kept), whole(coming)]
    outs = [whole_out((ff.height, size), jnp.bfloat16) for size in (folds * tile, folds // 2 * tile, folds // 2 * tile)]
    down, give, keep = call(functools.partial(top_body, tile), (1,), ins, outs, after=after, name="top")
    moves = [
        (s * blocks + b, (s ^ (1 << top)) * blocks + b) for s in range(owners) for b in range(blocks) if (s >> top) != b % 2
    ]
    return [(down, lax.ppermute(down, ("seq", "blk"), moves)), (keep, swap(give, "seq", top))], [down, give]


def send_all(sums, bits, after=(), cost=1000):
    me = lax.axis_index("seq")
    side = jnp.stack([(me >> bit) & 1 for bit in bits])
    terms, outs = [], []
    for one, bit in zip(sums, bits):
        axis = one.left.index(bit)
        before, rows = 1 << axis, one.height << (len(one.left) - axis - 1)
        for part in one.parts:
            terms += [whole(a.reshape(before, 2, rows, a.shape[-1])) for a in part]
        width = sum(part[0].shape[-1] for part in one.parts)
        outs += [whole_out((before, rows, width), jnp.bfloat16)] * 2
    body = functools.partial(split_body, [[len(part) for part in one.parts] for one in sums])
    results = call(body, (1,), [scalars(side)] + terms, outs, after=after, name="split", cost=cost)
    return [one.sent(bit, *results[2 * i : 2 * i + 2]) for i, (one, bit) in enumerate(zip(sums, bits))]


class RowSum:
    def __init__(self, height, left, parts):
        self.height, self.left, self.parts = height, left, parts

    def sent(self, bit, given, kept):
        self.parts = [(kept, swap(given, "seq", bit))]
        self.left = [other for other in self.left if other != bit]
        return given

    def join(self, *others):
        assert all(self.left == other.left for other in others)
        return RowSum(self.height, self.left, sum((other.parts for other in others), self.parts))

    def last(self):
        return [(a.reshape(self.height, -1), b.reshape(self.height, -1)) for a, b in self.parts]


def place_halves(core, held, other, out, rows, start, half):
    columns = slice(start, start + half)
    own, far = wide(held[:, columns]), wide(other[:, columns])
    first = core[0] == 0
    out[rows, :half] = jnp.where(first, own, far)
    out[rows, half:] = jnp.where(first, far, own)


def finish_ff_body(core, holder, held, other, grad_down, grad_up):
    height, width = held.shape[0], grad_down.shape[1]
    folds = grad_down.shape[0] // height
    for fold in range(folds):
        columns = slice(fold * width, (fold + 1) * width)
        own, far = wide(held[:, columns]), wide(other[:, columns])
        grad_down[fold * height : (fold + 1) * height, :] = jnp.where(holder[0] == 1, own, far)
    place_halves(core, held, other, grad_up, slice(0, height), folds * width, folds * width // 2)


def finish_ff(core, holder, held, other, width, folds):
    height = held.shape[0]
    ins = [scalars(core), scalars(holder), whole(held), whole(other)]
    shapes = ((folds * height, width), (height, folds * width))
    outs = [whole_out(shape, jnp.float32) for shape in shapes]
    return call(finish_ff_body, (1,), ins, outs, name="finish_ff")


def finish_attention_body(core, held, other, *outs):
    half = outs[0].shape[1] // 2
    starts = (0, half, 2 * half, 3 * half + 128)
    for start, out in zip(starts, outs[:4]):
        place_halves(core, held, other, out, slice(0, held.shape[0]), start, half)
    lanes = slice(3 * half, 3 * half + 128)
    sums = (wide(held[:, lanes]) + wide(other[:, lanes])).T
    for place, out in enumerate(outs[4:-1]):
        out[...] = sums[place : place + 1]
    folds = outs[-1].shape[0]
    outs[-1][...] = sums[SMALL : SMALL + folds]


def finish_attention(core, held, other, width, folds):
    ins = [scalars(core), whole(held), whole(other)]
    height = held.shape[0]
    outs = [whole_out((height, width), jnp.float32)] * 4
    outs += [whole_out((1, height), jnp.float32)] * SMALL + [whole_out((folds, height), jnp.float32)]
    return call(finish_attention_body, (1,), ins, outs, name="finish_attention")


def local(
    tokens,
    image_lengths,
    cotangent,
    ln1_gain,
    ln1_bias,
    w_query,
    b_query,
    w_key,
    w_value,
    b_value,
    q_gain,
    k_gain,
    w_out,
    b_out,
    ln2_gain,
    ln2_bias,
    w_up,
    b_up,
    w_down,
    b_down,
):
    sequences, span, width = tokens.shape
    owners = lax.axis_size("seq")
    blocks = lax.axis_size("blk")
    place = lax.axis_index("blk")
    core = (place & 1).reshape(1)
    tok = tokens.reshape(-1, width)
    cot = cotangent.reshape(-1, width)

    def split(array):
        return array.reshape(array.shape[:-2] + (sequences, -1, width))

    def flat(array):
        return array.reshape(array.shape[:-3] + (-1, width))

    act_one, pair, key_norm, query_norm, q8 = projections(
        tok, ln1_gain, ln1_bias, w_query, b_query, w_key, w_value, b_value, q_gain, k_gain
    )
    q8, pair = split(q8), split(pair)
    if blocks == 2:
        pairs = [pair, swap(pair, "blk", 0)]
        starts = jnp.stack([place * span, place * span, (1 - place) * span])
    else:
        pairs = [lax.all_gather(pair, "blk", axis=2, tiled=True)]
        starts = jnp.stack([place * span, place * 0])
    starts = starts.astype(jnp.int32)
    height = width // owners
    folds = w_up.shape[1] // width
    top = owners.bit_length() - 2
    me = lax.axis_index("seq")
    holder = (((me >> top) & 1) == (place & 1)).astype(jnp.int32).reshape(1)
    cot_far = swap(cot, "blk", 0)
    att, inverse, resid, act_two = attend(
        image_lengths, starts, b_out, ln2_gain, ln2_bias, q8, pairs, tok, w_out
    )
    act_far = swap(act_two, "blk", 0)
    spot = (me & 3).reshape(1)
    up_sum, out_own, out_far, d_own, d_far, kept, *given = feed(
        height, core, spot, act_two, act_far, cot, cot_far, w_up, w_down, b_up
    )
    d_far = swap(d_far, "blk", 0)
    moved = [lax.ppermute(a, "seq", [(i, i ^ r) for i in range(owners)]) for r, a in enumerate(given, 1)]
    ff = RowSum(height, list(reversed(range(2, top))), [(kept, *moved)])
    dq, *rest = attend_back(
        core,
        image_lengths,
        starts,
        ln2_gain,
        q8,
        inverse,
        pairs,
        (d_own, d_far, resid, cot, w_out, flat(att)),
        given,
    )
    *rest, row_sums, d_resid, out_mine, out_theirs = rest
    if blocks == 2:
        dk, dk_far, dv, dv_far = rest
        dk_far, dv_far = swap(dk_far, "blk", 0), swap(dv_far, "blk", 0)
    else:
        dk, dv = (lax.psum_scatter(a, "blk", scatter_dimension=1, tiled=True) for a in rest)
        dk_far, dv_far = jnp.zeros_like(dk), jnp.zeros_like(dv)
    dq, dk, dk_far, dv, dv_far = (flat(a) for a in (dq, dk, dk_far, dv, dv_far))
    out_arrived = swap(out_theirs, "blk", 0)
    out_far = swap(out_far, "blk", 0)
    out = layer(resid, out_own, out_far, b_down, [dq])
    sources = (act_one, dv, dv_far, w_value, dk, dk_far, key_norm, w_key, dq, query_norm, w_query, tok, d_resid)
    grad_tok, mine_q, mine_k, mine_two, *theirs = project_back(
        owners, core, (q_gain, k_gain, ln1_gain, up_sum, row_sums), sources, [out]
    )
    arrived_q, arrived_k, arrived_two = (swap(a, "blk", 0) for a in theirs)
    bits = list(reversed(range(top + 1)))
    one = RowSum(height, bits, [(mine_q, arrived_q), (mine_k, arrived_k)])
    two = RowSum(height, bits, [(mine_two, arrived_two), (out_mine, out_arrived)])
    given = [grad_tok]
    for bit in range(2, top):
        given = send_all((ff,), (bit,), given, LONG)
    given = send_all((one, two), (0, 1), given)
    given = send_all((one, two), (1, 0), given)
    ff_parts, given = send_top(ff, width, folds, given)
    rest = one.join(two)
    given = send_all((rest,), (2,), given)
    ff_held = merge(ff_parts, given)
    given = [ff_held[0]]
    for bit in range(3, top + 1):
        given = send_all((rest,), (bit,), given)
    grad_down, grad_up = finish_ff(core, holder, *ff_held, width, folds)
    rest_held = merge(rest.last(), given)
    grad_q, grad_k, grad_v, grad_out, *vectors = finish_attention(core, *rest_held, width, folds)
    t_ln2g, t_ln2b, t_bo, t_bd, t_ln1g, t_ln1b, t_bq, t_bv, t_qg, t_kg, t_bu = (v.reshape(-1) for v in vectors)
    return (
        out.reshape(tokens.shape),
        grad_tok.reshape(tokens.shape),
        t_ln1g,
        t_ln1b,
        grad_q,
        t_bq,
        grad_k,
        grad_v,
        t_bv,
        t_qg,
        t_kg,
        grad_out,
        t_bo,
        t_ln2g,
        t_ln2b,
        grad_up,
        t_bu,
        grad_down,
        t_bd,
    )


def solution(mesh):
    return jax.shard_map(
        local,
        mesh=mesh,
        in_specs=(
            P("seq", "blk", None),
            P("seq", None),
            P("seq", "blk", None),
            P(),
            P(),
            P(),
            P(),
            P(),
            P(),
            P(),
            P(),
            P(),
            P(),
            P(),
            P(),
            P(),
            P(),
            P(),
            P(),
            P(),
        ),
        out_specs=(
            P("seq", "blk", None),
            P("seq", "blk", None),
            P("seq"),
            P("seq"),
            P("seq", None),
            P("seq"),
            P("seq", None),
            P("seq", None),
            P("seq"),
            P("seq"),
            P("seq"),
            P("seq", None),
            P("seq"),
            P("seq"),
            P("seq"),
            P("seq", None),
            P("seq"),
            P("seq", None),
            P("seq"),
        ),
        check_vma=False,
    )
```

```python
import functools
import math

import jax
import jax.numpy as jnp
from jax import lax
from jax.experimental import pallas as pl
from jax.experimental.pallas import tpu as pltpu
from jax.sharding import PartitionSpec as P

H = 12
HD = 64
EPSILON = 1e-06
BLOCKED = -1024.0
MIB = 1 << 20
LONG = 10**12
BIG = 63
GROUP = 2
CORE, QUERY_START, KEY_START, SIDES = 0, 1, 2, 4
SMALL = 10
NT = (((1,), (1,)), ((), ()))
TN = (((0,), (0,)), ((), ()))
NN = (((1,), (0,)), ((), ()))


def dot(one, two, dims=NN):
    return lax.dot_general(one, two, dims, preferred_element_type=jnp.float32)


def low(values):
    return values.astype(jnp.bfloat16)


def wide(values):
    return values.astype(jnp.float32)


def row_stats(values):
    average = jnp.mean(values, axis=-1, keepdims=True)
    centred = values - average
    variance = jnp.mean(centred * centred, axis=-1, keepdims=True)
    scale = lax.rsqrt(variance + EPSILON)
    return centred * scale, scale


def norm_back(unit, scale, grads):
    return scale * (
        grads
        - jnp.mean(grads, axis=-1, keepdims=True)
        - unit * jnp.mean(grads * unit, axis=-1, keepdims=True)
    )


def head_mean(values, exact=False):
    parts = []
    for start in range(0, values.shape[1], 4 * HD):
        part = values[:, start : start + 4 * HD]
        width = part.shape[1]
        rows = lax.broadcasted_iota(jnp.int32, (width, width), 0) // HD
        columns = lax.broadcasted_iota(jnp.int32, (width, width), 1) // HD
        average = jnp.where(rows == columns, 1.0 / HD, 0.0).astype(jnp.bfloat16)
        upper = low(part)
        total = dot(upper, average)
        if exact:
            total = total + dot(low(part - wide(upper)), average)
        parts.append(total)
    return jnp.concatenate(parts, axis=1)


def head_stats(values):
    centred = values - head_mean(values, exact=True)
    scale = lax.rsqrt(head_mean(centred * centred) + EPSILON)
    return centred * scale, scale


def head_norm_back(unit, scale, grads):
    return scale * (grads - head_mean(grads) - unit * head_mean(grads * unit))


def vector(ref):
    return wide(ref[...]).reshape(1, -1)


def column_sum(values):
    return jnp.sum(values, axis=0, keepdims=True)


def call(body, grid, ins, outs, scratch=(), prefetch=None, after=(), limit=24, name=None, cost=1000):
    ins = list(ins) + [(a, pl.BlockSpec(memory_space=pltpu.SMEM if a.size == 1 else pl.ANY)) for a in after]
    lead = len(ins) - len(after) + (prefetch is not None)

    def kernel(*refs):
        body(*refs[:lead], *refs[lead + len(after) :])

    grid_spec = pltpu.PrefetchScalarGridSpec(
        num_scalar_prefetch=int(prefetch is not None),
        grid=grid,
        in_specs=[spec for _, spec in ins],
        out_specs=[spec for _, spec in outs],
        scratch_shapes=list(scratch),
    )
    arrays = [array for array, _ in ins]
    return pl.pallas_call(
        kernel,
        grid_spec=grid_spec,
        out_shape=[shape for shape, _ in outs],
        compiler_params=pltpu.CompilerParams(vmem_limit_bytes=limit * MIB),
        name=name,
        cost_estimate=pl.CostEstimate(flops=cost, bytes_accessed=1000, transcendentals=0),
    )(*([] if prefetch is None else [prefetch]), *arrays)


def whole(array):
    rank = len(array.shape)
    return (array, pl.BlockSpec(array.shape, lambda *_: (0,) * rank))


def whole_out(shape, dtype):
    rank = len(shape)
    return (jax.ShapeDtypeStruct(shape, dtype), pl.BlockSpec(shape, lambda *_: (0,) * rank))


def scalars(array):
    return (array, pl.BlockSpec(memory_space=pltpu.SMEM))


def project_body(gain, bias, bv, kg, *refs):
    sources, refs = refs[:3], refs[3:]
    act_hbm, pair_hbm, k_hbm = refs[:3]
    targets, refs = refs[3:6], refs[6:]
    act, pair, k_pre, got, put = refs
    loads = [pltpu.make_async_copy(a, b, got.at[i]) for i, (a, b) in enumerate(zip(sources, targets))]
    for load in loads:
        load.start()
    sends = []

    def send(source, target):
        copy = pltpu.make_async_copy(source, target, put.at[len(sends)])
        copy.start()
        sends.append(copy)

    tok, wv, wk = targets
    loads[0].wait()
    unit, _ = row_stats(wide(tok[...]))
    act_one = low(unit * vector(gain) + vector(bias))
    act[...] = act_one
    send(act, act_hbm)
    loads[1].wait()
    pair[1] = low(dot(act_one, wv[...]) + vector(bv))
    send(pair.at[1], pair_hbm.at[1])
    loads[2].wait()
    key_unit, key_scale = head_stats(dot(act_one, wk[...]))
    pair[0] = low(key_unit * vector(kg))
    send(pair.at[0], pair_hbm.at[0])
    k_pre[0] = low(key_unit)
    k_pre[1] = low(key_scale)
    send(k_pre, k_hbm)
    for copy in sends:
        copy.wait()


def projections(tok, gain, bias, wk, wv, bv, kg):
    count, width = tok.shape
    anywhere = pl.BlockSpec(memory_space=pl.ANY)
    sources = (tok, wv, wk)
    ins = [whole(a) for a in (gain, bias, bv, kg)] + [(a, anywhere) for a in sources]

    def rows(dtype):
        return jax.ShapeDtypeStruct((count, width), dtype)

    pair = jax.ShapeDtypeStruct((2, count, width), jnp.bfloat16)
    results = (rows(jnp.bfloat16), pair, pair)
    outs = [(a, anywhere) for a in results]
    scratch = [pltpu.VMEM(a.shape, a.dtype) for a in sources + results]
    scratch += [pltpu.SemaphoreType.DMA((3,)), pltpu.SemaphoreType.DMA((4,))]
    return call(project_body, (1,), ins, outs, scratch, limit=BIG, name="projections")


def query_body(bias, gain, act, w_query, q8, norm):
    unit, scale = head_stats(dot(act[...], w_query[...]) + vector(bias))
    q8[...] = low(unit * vector(gain)) * (1.0 / math.sqrt(HD))
    norm[0] = low(unit)
    norm[1] = low(scale)


def queries(act, w_query, bias, gain):
    ins = [whole(a) for a in (bias, gain, act, w_query)]
    outs = [whole_out(act.shape, jnp.bfloat16), whole_out((2,) + act.shape, jnp.bfloat16)]
    return call(query_body, (1,), ins, outs, limit=BIG, name="queries", cost=LONG)


def segment_column(positions, lengths, sequence, slots):
    end = lengths[sequence, 0]
    segment = (positions >= end).astype(jnp.int32)
    for slot in range(1, slots):
        end = end + lengths[sequence, slot]
        segment = segment + (positions >= end).astype(jnp.int32)
    return segment


def query_lanes(count, start, lengths, sequence, slots):
    positions = lax.broadcasted_iota(jnp.int32, (count, 2 * HD), 0) + start
    lane = lax.broadcasted_iota(jnp.int32, (count, 2 * HD), 1) & (HD - 1)
    segment = segment_column(positions, lengths, sequence, slots)
    return jnp.where(segment == lane, 1.0, 0.0).astype(jnp.bfloat16)


def key_lanes(count, start, lengths, sequence, slots):
    positions = lax.broadcasted_iota(jnp.int32, (count, 2 * HD), 0) + start
    lane = lax.broadcasted_iota(jnp.int32, (count, 2 * HD), 1) & (HD - 1)
    segment = segment_column(positions, lengths, sequence, slots)
    open_to = (segment == lane) & (lane < slots)
    return jnp.where(open_to, 0.0, BLOCKED).astype(jnp.bfloat16)


def pair_spec(array):
    return (array, pl.BlockSpec((1, array.shape[1], 2 * HD), lambda s, h: (s, 0, h)))


def low_half(count):
    return lax.broadcasted_iota(jnp.int32, (count, 2 * HD), 1) < HD


def attend_masks(slots, lengths, facts, q_mask, k_masks, sequence, place):
    span = q_mask.shape[0]

    @pl.when(place == 0)
    def _():
        q_mask[...] = query_lanes(span, facts[QUERY_START], lengths, sequence, slots)
        for chunk, mask in enumerate(k_masks):
            mask[...] = key_lanes(mask.shape[0], facts[KEY_START + chunk], lengths, sequence, slots)


def attend_pair(q8, pairs, q_mask, k_masks, lanes):
    first = low_half(q8.shape[1])
    query = q8[0, :, lanes]
    one = jnp.where(first, query, q_mask[...])
    two = jnp.where(first, q_mask[...], query)
    sums = [None, None]
    for pair, k_mask in zip(pairs, k_masks):
        key, value, mask = pair[0, 0, :, lanes], pair[1, 0, :, lanes], k_mask[...]
        key_first = low_half(key.shape[0])
        ones = jnp.ones_like(value)
        for side, operand in enumerate((one, two)):
            pick = key_first if side == 0 else ~key_first
            lifted = low(jnp.exp(dot(operand, jnp.where(pick, key, mask), NT)))
            term = dot(lifted, jnp.where(pick, value, ones))
            sums[side] = term if sums[side] is None else sums[side] + term
    top = jnp.where(first, sums[0], sums[1])
    total = pltpu.roll(jnp.where(first, sums[1], sums[0]), HD, 1)
    inverse = jnp.where(total > 0.0, 1.0 / total, 0.0)
    return low(top * inverse), inverse


def attend_back_pair(query, queries, d_low, d_values, pairs, k_masks):
    key_grads, value_grads, d_query_t = [], [], None
    for pair, k_mask in zip(pairs, k_masks):
        key, value, mask = pair[0, 0], pair[1, 0], k_mask[...]
        key_first = low_half(key.shape[0])
        ones = jnp.ones_like(value)
        key_t = key.T
        key_terms, value_terms, query_terms = [], [], []
        for side in range(2):
            pick = key_first if side == 0 else ~key_first
            lifted = jnp.exp(dot(jnp.where(pick, key, mask), queries[side], NT))
            shifted = dot(jnp.where(pick, value, ones), d_values[side], NT)
            d_scores = low(lifted * shifted)
            value_terms.append(dot(low(lifted), d_low))
            key_terms.append(dot(d_scores, query))
            query_terms.append(dot(key_t[side * HD : (side + 1) * HD], d_scores))
        key_grads.append(low(jnp.where(key_first, key_terms[0], key_terms[1])))
        value_grads.append(low(jnp.where(key_first, value_terms[0], value_terms[1])))
        term = jnp.concatenate(query_terms, axis=0)
        d_query_t = term if d_query_t is None else d_query_t + term
    return d_query_t.T * (1.0 / math.sqrt(HD)), key_grads, value_grads


def delta_lanes(att, d_low, pick):
    lane = lax.broadcasted_iota(jnp.int32, att.shape, 1) & (HD - 1)
    delta = -jnp.sum(jnp.where(pick, wide(att) * wide(d_low), 0.0), axis=1, keepdims=True)
    high = low(delta)
    middle = low(delta - wide(high))
    rest = low(delta - wide(high) - wide(middle))
    zero = jnp.zeros((), jnp.bfloat16)
    extra = jnp.where(lane == 0, high, jnp.where(lane == 1, middle, jnp.where(lane == 2, rest, zero)))
    return jnp.where(pick, d_low, extra)


def attend_back_body(slots, chunks, facts, lengths, gain, q8, inverse, *refs):
    pairs, refs = refs[:chunks], refs[chunks:]
    sources, refs = refs[:6], refs[6:]
    d_query, refs = refs[0], refs[1:]
    d_keys, d_vals, refs = refs[:chunks], refs[chunks : 2 * chunks], refs[2 * chunks :]
    rows, d_resid_hbm, grad_mine, grad_theirs, mark = refs[:5]
    q_mask, refs = refs[5], refs[6:]
    mark[0] = 0
    k_masks, targets, refs = refs[:chunks], refs[chunks : chunks + 6], refs[chunks + 6 :]
    d_own, d_far, resid, cot, w_out, att = targets
    d_att, back, got, put = refs
    span, width = q8.shape[1], resid.shape[1]
    heads = H // 2
    step = pl.program_id(0)
    sequence, place = step // heads, step % heads

    def fetch(number):
        return pltpu.make_async_copy(sources[number], targets[number], got.at[number])

    def send_back():
        return pltpu.make_async_copy(back, d_resid_hbm, put.at[0])

    @pl.when(step == 0)
    def _():
        for number in range(6):
            fetch(number).start()
        for number in range(6):
            fetch(number).wait()
        grads = wide(d_own[...]) + wide(d_far[...])
        unit, scale = row_stats(resid[...])
        rows[0:1, :] = column_sum(grads * unit)
        rows[1:2, :] = column_sum(grads)
        total = wide(cot[...]) + norm_back(unit, scale, grads * vector(gain))
        back[...] = total
        send_back().start()
        branch = low(total)
        rows[2:3, :] = column_sum(wide(branch))
        rows[3:4, :] = column_sum(wide(cot[...]))
        d_att[...] = low(dot(branch, w_out[...], NT))
        product = low(dot(att[...], branch, TN))
        half = width // 2
        for side in range(2):

            @pl.when(facts[CORE] == side)
            def _():
                grad_mine[...] = product[:, side * half : (side + 1) * half]
                grad_theirs[...] = product[:, (1 - side) * half : (2 - side) * half]

    @pl.when(place == 0)
    def _():
        q_mask[...] = query_lanes(span, facts[QUERY_START], lengths, sequence, slots)
        for chunk, mask in enumerate(k_masks):
            mask[...] = key_lanes(mask.shape[0], facts[KEY_START + chunk], lengths, sequence, slots)

    block = (pl.ds(sequence * span, span), pl.ds(pl.multiple_of(place * 128, 128), 128))
    first = low_half(span)
    query = q8[0]
    queries = (jnp.where(first, query, q_mask[...]), jnp.where(first, q_mask[...], query))
    d_low = low(wide(d_att[block]) * wide(inverse[0]))
    held = att[block]
    d_values = [delta_lanes(held, d_low, first), delta_lanes(held, d_low, ~first)]
    grads, key_grads, value_grads = attend_back_pair(query, queries, d_low, d_values, pairs, k_masks)
    d_query[0] = low(grads)
    for chunk in range(chunks):
        d_keys[chunk][0] = key_grads[chunk]
        d_vals[chunk][0] = value_grads[chunk]

    @pl.when(step == pl.num_programs(0) - 1)
    def _():
        send_back().wait()


def pair_block(array, lead, steps, group=1):
    heads = H // 2 // group

    def index(i, *_):
        i = jnp.minimum(i, steps - 1)
        return (i // heads, 0, i % heads)

    shape = (1, array.shape[-2], 2 * HD * group)
    if lead:
        return (array, pl.BlockSpec((2,) + shape, lambda i, *_: (0,) + index(i)))
    return (array, pl.BlockSpec(shape, index))


def attend_back(facts, lengths, gain, q8, inverse, pairs, sources, after):
    count, span, width = q8.shape
    steps = count * H // 2
    tokens = count * span
    anywhere = pl.BlockSpec(memory_space=pl.ANY)

    def shape(sizes, dtype):
        return jax.ShapeDtypeStruct(sizes, dtype)

    ins = [scalars(facts), scalars(lengths), whole(gain)]
    ins += [pair_block(q8, False, steps), pair_block(inverse, False, steps)]
    ins += [pair_block(a, True, steps) for a in pairs] + [(a, anywhere) for a in sources]
    outs = [pair_block(shape((count, span, width), jnp.bfloat16), False, steps)]
    outs += [pair_block(shape(a.shape[1:], jnp.bfloat16), False, steps) for a in pairs + pairs]
    outs += [
        whole_out((8, width), jnp.float32),
        (shape((tokens, width), jnp.float32), anywhere),
        whole_out((width, width // 2), jnp.bfloat16),
        whole_out((width, width // 2), jnp.bfloat16),
        (jax.ShapeDtypeStruct((1,), jnp.int32), pl.BlockSpec(memory_space=pltpu.SMEM)),
    ]
    scratch = [pltpu.VMEM((a.shape[-2], 2 * HD), jnp.bfloat16) for a in [q8] + list(pairs)]
    scratch += [pltpu.VMEM(a.shape, a.dtype) for a in sources]
    scratch += [pltpu.VMEM((tokens, width), d) for d in (jnp.bfloat16, jnp.float32)]
    scratch += [pltpu.SemaphoreType.DMA((6,)), pltpu.SemaphoreType.DMA((1,))]
    body = functools.partial(attend_back_body, lengths.shape[1], len(pairs))
    return call(body, (steps,), ins, outs, scratch, after=after, limit=BIG, name="attend_back")


def gelu_pair(values):
    half = 0.5 + 0.5 * lax.erf(values * math.sqrt(0.5))
    slope = half + values * (math.sqrt(0.5 / math.pi) * jnp.exp(-0.5 * values * values))
    return values * half, slope


def layer_body(resid, own, far, bias, out):
    out[...] = low(resid[...] + wide(own[...]) + wide(far[...]) + vector(bias))


def layer(resid, own, far, bias, after):
    count, width = resid.shape
    spec = pl.BlockSpec((count // 2, width), lambda i: (i, 0))
    ins = [(resid, spec), (own, spec), (far, spec), whole(bias)]
    outs = [(jax.ShapeDtypeStruct((count, width), jnp.bfloat16), spec)]
    return call(layer_body, (2,), ins, outs, after=after, limit=BIG, name="layer", cost=LONG)[0]


def attend_body(slots, chunks, lengths, facts, b_out, gain, bias, q8, *refs):
    pairs, refs = refs[:chunks], refs[chunks:]
    sources, refs = refs[:2], refs[2:]
    att, inverse, resid, act, q_mask = refs[:5]
    k_masks, refs = refs[5 : 5 + chunks], refs[5 + chunks :]
    tok, w_out, held, got = refs
    span = q8.shape[1]
    heads = H // 2 // GROUP
    step = pl.program_id(0)
    last = pl.num_programs(0) - 1
    targets = (tok, w_out)

    def fetch(number):
        return pltpu.make_async_copy(sources[number], targets[number], got.at[number])

    @pl.when(step == 0)
    def _():
        fetch(0).start()
        fetch(1).start()

    @pl.when(step < last)
    def _():
        sequence, place = step // heads, step % heads
        attend_masks(slots, lengths, facts, q_mask, k_masks, sequence, place)
        for member in range(GROUP):
            lanes = slice(member * 128, (member + 1) * 128)
            values, inv = attend_pair(q8, pairs, q_mask, k_masks, lanes)
            att[0, :, lanes] = values
            inverse[0, :, lanes] = low(inv)
            start = pl.multiple_of((place * GROUP + member) * 128, 128)
            held[pl.ds(sequence * span, span), pl.ds(start, 128)] = values

    @pl.when(step == last)
    def _():
        fetch(0).wait()
        fetch(1).wait()
        total = wide(tok[...]) + dot(held[...], w_out[...]) + vector(b_out)
        resid[...] = total
        act[...] = low(row_stats(total)[0] * vector(gain) + vector(bias))


def attend(lengths, facts, b_out, gain, bias, q8, pairs, tok, w_out):
    count, span, width = q8.shape
    steps = count * (H // 2 // GROUP)
    tokens = count * span
    anywhere = pl.BlockSpec(memory_space=pl.ANY)

    def shape(dtype):
        return jax.ShapeDtypeStruct((count, span, width), dtype)

    ins = [scalars(lengths), scalars(facts)] + [whole(a) for a in (b_out, gain, bias)]
    ins += [pair_block(q8, False, steps, GROUP)] + [pair_block(a, True, steps, GROUP) for a in pairs]
    ins += [(tok, anywhere), (w_out, anywhere)]
    outs = [
        pair_block(shape(jnp.bfloat16), False, steps, GROUP),
        pair_block(shape(jnp.bfloat16), False, steps, GROUP),
        whole_out((tokens, width), jnp.float32),
        whole_out((tokens, width), jnp.bfloat16),
    ]
    scratch = [pltpu.VMEM((a.shape[-2], 2 * HD), jnp.bfloat16) for a in [q8] + list(pairs)]
    scratch += [pltpu.VMEM(tok.shape, jnp.bfloat16), pltpu.VMEM(w_out.shape, jnp.bfloat16)]
    scratch += [pltpu.VMEM(tok.shape, jnp.bfloat16), pltpu.SemaphoreType.DMA((2,))]
    body = functools.partial(attend_body, lengths.shape[1], len(pairs))
    return call(body, (steps + 1,), ins, outs, scratch, limit=BIG, name="attend")


def feed_body(
    height, facts, act, act_far, cot, cot_far, w_up, w_down, b_up,
    up_sum, out_own, out_far, d_own, d_far, hbm_0, hbm_1, hbm_2, hbm_3,
    own_out, own_d, far_out, far_d, grads, put,
):
    step = pl.program_id(0)
    width, tile = w_up.shape
    steps = pl.num_programs(0)
    start = (facts[CORE] * steps + step) * tile
    bias = wide(b_up[pl.ds(pl.multiple_of(start, tile), tile)]).reshape(1, -1)
    @pl.when(step == 0)
    def _():
        for ref in (own_out, own_d, far_out, far_d):
            ref[...] = jnp.zeros_like(ref)

    down_grads = up_grads = sums = None
    for values, upper, out_sum, d_sum in ((act, cot, own_out, own_d), (act_far, cot_far, far_out, far_d)):
        hidden, slope = gelu_pair(dot(values[...], w_up[...]) + bias)
        hidden = low(hidden)
        d_up = low(dot(upper[...], w_down[...], NT) * slope)
        out_sum[...] += dot(hidden, w_down[...])
        d_sum[...] += dot(d_up, w_up[...], NT)
        down_term = dot(hidden, upper[...], TN)
        up_term = dot(values[...], d_up, TN)
        sum_term = column_sum(wide(d_up))
        down_grads = down_term if down_grads is None else down_grads + down_term
        up_grads = up_term if up_grads is None else up_grads + up_term
        sums = sum_term if sums is None else sums + sum_term
    up_sum[...] = sums
    folds = grads.shape[2] // width // 2
    here = tile // (folds * height)
    tall = down_grads.reshape(here // 4, 4, folds, height, width)
    broad = up_grads.reshape(2, width // (8 * height), 4, height, tile)
    spot = facts[SIDES] + 2 * facts[SIDES + 1]
    rows = here // 4 * height
    lines = pl.ds(pl.multiple_of(step * rows, 16), rows)
    for place in range(4):
        which = place ^ spot
        for fold in range(folds):
            columns = slice(fold * width, (fold + 1) * width)
            grads[which, lines, columns] = low(tall[:, place, fold].reshape(rows, width))
        for top in range(2):
            columns = pl.ds(pl.multiple_of(folds * width + (2 * step + top) * tile, tile), tile)
            grads[which, :, columns] = low(broad[top, :, place].reshape(grads.shape[1], tile))

    def copies(at):
        line = pl.ds(pl.multiple_of(at * rows, 16), rows)
        columns = pl.ds(pl.multiple_of((folds + 2 * at) * tile, tile), 2 * tile)
        for place, target in enumerate((hbm_0, hbm_1, hbm_2, hbm_3)):
            left = slice(0, folds * width)
            yield pltpu.make_async_copy(grads.at[place, line, left], target.at[line, left], put.at[at, 2 * place])
            yield pltpu.make_async_copy(
                grads.at[place, :, columns], target.at[:, columns], put.at[at, 2 * place + 1]
            )

    for copy in copies(step):
        copy.start()

    @pl.when(step == steps - 1)
    def _():
        d_far[...] = low(far_d[...])
        d_own[...] = low(own_d[...])
        out_far[...] = low(far_out[...])
        out_own[...] = low(own_out[...])
        for at in range(folds // 2):
            for copy in copies(at):
                copy.wait()


def feed(height, facts, act, act_far, cot, cot_far, w_up, w_down, b_up):
    count, width = act.shape
    hidden = w_up.shape[1]
    steps = hidden // width // 2
    ins = [whole(a) for a in (act, act_far, cot, cot_far)]
    ins += [
        (w_up, pl.BlockSpec((width, width), lambda j, facts: (0, facts[CORE] * steps + j))),
        (w_down, pl.BlockSpec((width, width), lambda j, facts: (facts[CORE] * steps + j, 0))),
        whole(b_up),
    ]
    up_sum = (
        jax.ShapeDtypeStruct((1, hidden // 2), jnp.float32),
        pl.BlockSpec((1, width), lambda j, facts: (0, j)),
    )
    half_sum = whole_out((count, width), jnp.bfloat16)
    part = jax.ShapeDtypeStruct((width // 8, 2 * hidden), jnp.bfloat16)
    outs = [up_sum] + [half_sum] * 4 + [(part, pl.BlockSpec(memory_space=pl.ANY))] * 4
    scratch = [pltpu.VMEM((count, width), jnp.float32)] * 4 + [pltpu.VMEM((4,) + part.shape, jnp.bfloat16)]
    scratch += [pltpu.SemaphoreType.DMA((steps, 8))]
    body = functools.partial(feed_body, height)
    return call(body, (steps,), ins, outs, scratch, prefetch=facts, limit=BIG, name="feed")


def project_back_body(owners, parts, core, qg, kg, gain, up_sum, row_sums, *refs):
    sources, refs = refs[:parts], refs[parts:]
    grad_hbm, mine_q, mine_k, mine_two, theirs_q, theirs_k, theirs_two, mark = refs[:8]
    targets, refs = refs[8 : 8 + parts], refs[8 + parts :]
    mark[0] = 0
    grad, one, two, got, put = refs
    copies = [pltpu.make_async_copy(a, b, got.at[i]) for i, (a, b) in enumerate(zip(sources, targets))]
    for copy in copies:
        copy.start()
    waited = set()

    def use(*places):
        for place in places:
            if place not in waited:
                copies[place].wait()
                waited.add(place)
        return [targets[place] for place in places]

    def joined(*places):
        return jnp.concatenate([wide(ref[...]) for ref in use(*places)], axis=1)

    act, wv, wk, wq = 0, 3, 7, 10
    half = one.shape[2] // 2

    side_one = core[0] == 0

    def place_pieces(piece, spots):
        left, right = piece[:, :half], piece[:, half:]
        own, far = jnp.where(side_one, left, right), jnp.where(side_one, right, left)
        for target, start, first, last in spots:
            columns = slice(start, start + last - first)
            target[0, :, columns] = own[:, first:last]
            target[1, :, columns] = far[:, first:last]

    d_value = low(joined(1) + joined(2))
    (act_ref,) = use(act)
    place_pieces(low(dot(act_ref[...], d_value, TN)), ((two, 0, 0, half),))
    bv_sum = column_sum(wide(d_value))
    (w_ref,) = use(wv)
    back = dot(d_value, w_ref[...], NT)
    d_key_low = joined(4) + joined(5)
    (pre,) = use(6)
    unit, scale = wide(pre[0]), wide(pre[1])
    kg_sum = column_sum(d_key_low * unit)
    d_key = low(head_norm_back(unit, scale, d_key_low * vector(kg)))
    place_pieces(low(dot(act_ref[...], d_key, TN)), ((one, half, 0, half),))
    sends = []

    def send(source, target):
        copy = pltpu.make_async_copy(source, target, put.at[len(sends)])
        copy.start()
        sends.append(copy)

    send(two.at[0, :, :half], mine_two.at[:, :half])
    two[1, :, half:] = jnp.zeros((two.shape[1], 128), jnp.bfloat16)
    send(two.at[1], theirs_two)
    send(one.at[1, :, half:], theirs_k)
    send(one.at[0, :, half:], mine_k)
    (w_ref,) = use(wk)
    back = back + dot(d_key, w_ref[...], NT)
    d_low = joined(8)
    (pre,) = use(9)
    unit, scale = wide(pre[0]), wide(pre[1])
    qg_sum = column_sum(d_low * unit)
    d_query = low(head_norm_back(unit, scale, d_low * vector(qg)))
    bq_sum = column_sum(wide(d_query))
    place_pieces(low(dot(act_ref[...], d_query, TN)), ((one, 0, 0, half),))
    send(one.at[0, :, :half], mine_q)
    send(one.at[1, :, :half], theirs_q)
    (w_ref,) = use(wq)
    grads = back + dot(d_query, w_ref[...], NT)
    tok, d_resid = use(11, 12)
    unit, scale = row_stats(wide(tok[...]))
    grad[...] = d_resid[...] + norm_back(unit, scale, grads * vector(gain))
    send(grad, grad_hbm)
    full = [row_sums[0:4, :], column_sum(grads * unit), column_sum(grads), bq_sum, bv_sum, qg_sum, kg_sum]
    full = jnp.concatenate(full, axis=0)
    width = full.shape[1]
    full = jnp.concatenate([full, jnp.zeros((128 - full.shape[0], width), jnp.float32)], axis=0)
    columns = full.T
    lane = lax.broadcasted_iota(jnp.int32, columns.shape, 1)
    hidden = 2 * up_sum.shape[1]
    folds = hidden // width
    first = core[0] == 0
    halves = [jnp.where(first, up_sum[...], 0.0), jnp.where(first, 0.0, up_sum[...])]
    tall = jnp.broadcast_to(jnp.concatenate(halves, axis=1), (128, hidden)).T.reshape(owners, folds, width // owners, 128)
    for fold in range(folds):
        piece = tall[:, fold].reshape(width, 128)
        columns = jnp.where(lane == SMALL + fold, piece, columns)
    end = slice(half, half + 128)
    two[0, :, end] = low(columns)
    send(two.at[0, :, end], mine_two.at[:, end])
    for copy in sends:
        copy.wait()


def project_back(owners, core, vectors, sources, after):
    act = sources[0]
    count, width = act.shape
    anywhere = pl.BlockSpec(memory_space=pl.ANY)
    ins = [scalars(core)] + [whole(a) for a in vectors] + [(a, anywhere) for a in sources]
    one = jax.ShapeDtypeStruct((width, width), jnp.bfloat16)
    two = jax.ShapeDtypeStruct((width, width // 2 + 128), jnp.bfloat16)
    total = jax.ShapeDtypeStruct((count, width), jnp.float32)
    piece = jax.ShapeDtypeStruct((width, width // 2), jnp.bfloat16)
    outs = [(a, anywhere) for a in (total, piece, piece, two, piece, piece, two)]
    outs.append((jax.ShapeDtypeStruct((1,), jnp.int32), pl.BlockSpec(memory_space=pltpu.SMEM)))
    scratch = [pltpu.VMEM(a.shape, a.dtype) for a in sources]
    scratch += [pltpu.VMEM(total.shape, total.dtype)] + [pltpu.VMEM((2,) + a.shape, a.dtype) for a in (one, two)]
    scratch += [pltpu.SemaphoreType.DMA((len(sources),)), pltpu.SemaphoreType.DMA((8,))]
    body = functools.partial(project_back_body, owners, len(sources))
    return call(body, (1,), ins, outs, scratch, after=after, limit=BIG, name="project_back", cost=1000)


def swap(values, axis, bit):
    count = lax.axis_size(axis)
    return lax.ppermute(values, axis, [(i, i ^ (1 << bit)) for i in range(count)])


def add_low(one, two):
    return low(wide(one) + wide(two))


def split_body(counts, bits, facts, *refs):
    total = sum(sum(count) for count in counts)
    inputs, outs = refs[:total], refs[total:]
    place = 0
    for group, count in enumerate(counts):
        give, keep = outs[2 * group : 2 * group + 2]
        mine = facts[SIDES + bits[group]]
        start = 0
        for terms in count:
            columns = slice(start, start + inputs[place].shape[3])
            for half, out in ((1 - mine, give), (mine, keep)):
                held = wide(inputs[place][:, half])
                for other in range(place + 1, place + terms):
                    held = held + wide(inputs[other][:, half])
                out[:, :, columns] = low(held)
            start += inputs[place].shape[3]
            place += terms


def merge_body(parts, *refs):
    out = refs[-1]
    start = 0
    for kept, coming in zip(refs[:parts], refs[parts : 2 * parts]):
        columns = slice(start, start + kept.shape[1])
        out[:, columns] = low(wide(kept[...]) + wide(coming[...]))
        start += kept.shape[1]


def merge(parts, after):
    height, width = parts[0][0].shape[0], sum(kept.shape[1] for kept, _ in parts)
    ins = [whole(kept) for kept, _ in parts] + [whole(coming) for _, coming in parts]
    outs = [whole_out((height, width), jnp.bfloat16)]
    held = call(functools.partial(merge_body, len(parts)), (1,), ins, outs, after=after, name="merge")[0]
    for bit in range(1, lax.axis_size("blk").bit_length() - 1):
        held = add_low(held, swap(held, "blk", bit))
    return held, swap(held, "blk", 0)


def top_body(tile, place, facts, *refs):
    terms, (down, give, keep) = refs[:-3], refs[-3:]
    sums = [wide(kept[...]) + wide(coming[...]) for kept, coming in zip(terms[::2], terms[1::2])]
    width = down.shape[1]
    lower, upper = sums if len(sums) == 2 else (sums[0][:, :width], sums[0][:, width:])
    down[...] = low(lower)
    for block in range(give.shape[1] // tile):
        columns = slice(block * tile, (block + 1) * tile)
        for top in range(2):
            start = (2 * block + top) * tile
            piece = low(upper[:, start : start + tile])

            @pl.when(facts[SIDES + place] == top)
            def _():
                keep[:, columns] = piece

            @pl.when(facts[SIDES + place] != top)
            def _():
                give[:, columns] = piece


def send_top(facts, ff, tile, folds, after):
    owners, blocks = lax.axis_size("seq"), lax.axis_size("blk")
    top = owners.bit_length() - 2
    ins = [scalars(facts)] + [whole(a.reshape(ff.height, -1)) for part in ff.parts for a in part]
    outs = [whole_out((ff.height, size), jnp.bfloat16) for size in (folds * tile, folds // 2 * tile, folds // 2 * tile)]
    down, give, keep = call(functools.partial(top_body, tile, top), (1,), ins, outs, after=after, name="top")
    moves = [
        (s * blocks + b, (s ^ (1 << top)) * blocks + b) for s in range(owners) for b in range(blocks) if (s >> top) != b % 2
    ]
    return [(down, lax.ppermute(down, ("seq", "blk"), moves)), (keep, swap(give, "seq", top))], [down, give]


def send_all(facts, sums, bits, after=(), cost=1000, limit=24):
    terms, outs = [], []
    for one, bit in zip(sums, bits):
        axis = one.left.index(bit)
        before, rows = 1 << axis, one.height << (len(one.left) - axis - 1)
        for part in one.parts:
            terms += [whole(a.reshape(before, 2, rows, a.shape[-1])) for a in part]
        width = sum(part[0].shape[-1] for part in one.parts)
        outs += [whole_out((before, rows, width), jnp.bfloat16)] * 2
    body = functools.partial(split_body, [[len(part) for part in one.parts] for one in sums], bits)
    results = call(body, (1,), [scalars(facts)] + terms, outs, after=after, limit=limit, name="split", cost=cost)
    return [one.sent(bit, *results[2 * i : 2 * i + 2]) for i, (one, bit) in enumerate(zip(sums, bits))]


class RowSum:
    def __init__(self, height, left, parts):
        self.height, self.left, self.parts = height, left, parts

    def sent(self, bit, given, kept):
        self.parts = [(kept, swap(given, "seq", bit))]
        self.left = [other for other in self.left if other != bit]
        return given

    def join(self, *others):
        assert all(self.left == other.left for other in others)
        return RowSum(self.height, self.left, sum((other.parts for other in others), self.parts))

    def last(self):
        return [(a.reshape(self.height, -1), b.reshape(self.height, -1)) for a, b in self.parts]


def place_halves(core, held, other, out, rows, start, half):
    columns = slice(start, start + half)
    own, far = wide(held[:, columns]), wide(other[:, columns])
    first = core[0] == 0
    out[rows, :half] = jnp.where(first, own, far)
    out[rows, half:] = jnp.where(first, far, own)


def finish_ff_body(place, core, held, other, grad_down, grad_up):
    height, width = held.shape[0], grad_down.shape[1]
    folds = grad_down.shape[0] // height
    for fold in range(folds):
        columns = slice(fold * width, (fold + 1) * width)
        own, far = wide(held[:, columns]), wide(other[:, columns])
        grad_down[fold * height : (fold + 1) * height, :] = jnp.where(core[SIDES + place] == core[CORE], own, far)
    place_halves(core, held, other, grad_up, slice(0, height), folds * width, folds * width // 2)


def finish_attention_body(core, kept, coming, far_kept, far_coming, *outs):
    half = outs[0].shape[1] // 2
    held = wide(kept[...]) + wide(coming[...])
    other = wide(far_kept[...]) + wide(far_coming[...])
    first = core[CORE] == 0
    left, right = jnp.where(first, held, other), jnp.where(first, other, held)
    starts = (0, half, 2 * half, 3 * half + 128)
    for start, out in zip(starts, outs[:4]):
        out[:, :half] = left[:, start : start + half]
        out[:, half:] = right[:, start : start + half]
    lanes = slice(3 * half, 3 * half + 128)
    sums = (held[:, lanes] + other[:, lanes]).T
    for place, out in enumerate(outs[4:-1]):
        out[...] = sums[place : place + 1]
    height = held.shape[0]
    for fold in range(outs[-1].shape[1] // height):
        outs[-1][:, fold * height : (fold + 1) * height] = sums[SMALL + fold : SMALL + fold + 1]


def finish_body(place, core, held, other, *refs):
    finish_ff_body(place, core, held, other, *refs[4:6])
    finish_attention_body(core, *refs[:4], *refs[6:])


def finish(core, ff, terms, width, folds):
    height = terms[0].shape[0]
    ins = [scalars(core)] + [whole(a) for a in (*ff, *terms)]
    shapes = [(folds * height, width), (height, folds * width)] + [(height, width)] * 4
    shapes += [(1, height)] * SMALL + [(1, folds * height)]
    outs = [whole_out(shape, jnp.float32) for shape in shapes]
    place = lax.axis_size("seq").bit_length() - 2
    return call(functools.partial(finish_body, place), (1,), ins, outs, name="finish")


def local(
    tokens,
    image_lengths,
    cotangent,
    ln1_gain,
    ln1_bias,
    w_query,
    b_query,
    w_key,
    w_value,
    b_value,
    q_gain,
    k_gain,
    w_out,
    b_out,
    ln2_gain,
    ln2_bias,
    w_up,
    b_up,
    w_down,
    b_down,
):
    sequences, span, width = tokens.shape
    owners = lax.axis_size("seq")
    blocks = lax.axis_size("blk")
    place = lax.axis_index("blk")
    me = lax.axis_index("seq")
    first_key, second_key = (place * span, (1 - place) * span) if blocks == 2 else (place * 0, place * 0)
    bits = list(reversed(range(owners.bit_length() - 1)))
    numbers = [place & 1, place * span, first_key, second_key] + [(me >> bit) & 1 for bit in reversed(bits)]
    facts = jnp.stack(numbers).astype(jnp.int32)
    tok = tokens.reshape(-1, width)
    cot = cotangent.reshape(-1, width)

    def split(array):
        return array.reshape(array.shape[:-2] + (sequences, -1, width))

    def flat(array):
        return array.reshape(array.shape[:-3] + (-1, width))

    act_one, pair, key_norm = projections(tok, ln1_gain, ln1_bias, w_key, w_value, b_value, k_gain)
    q8, query_norm = queries(act_one, w_query, b_query, q_gain)
    q8, pair = split(q8), split(pair)
    if blocks == 2:
        pairs = [pair, swap(pair, "blk", 0)]
    else:
        pairs = [lax.all_gather(pair, "blk", axis=2, tiled=True)]
    height = width // owners
    folds = w_up.shape[1] // width
    top = owners.bit_length() - 2
    cot_far = swap(cot, "blk", 0)
    att, inverse, resid, act_two = attend(
        image_lengths, facts, b_out, ln2_gain, ln2_bias, q8, pairs, tok, w_out
    )
    act_far = swap(act_two, "blk", 0)
    up_sum, out_own, out_far, d_own, d_far, kept, *given = feed(
        height, facts, act_two, act_far, cot, cot_far, w_up, w_down, b_up
    )
    d_far = swap(d_far, "blk", 0)
    moved = [lax.ppermute(a, "seq", [(i, i ^ r) for i in range(owners)]) for r, a in enumerate(given, 1)]
    ff = RowSum(height, list(reversed(range(2, top))), [(kept, *moved)])
    dq, *rest = attend_back(
        facts,
        image_lengths,
        ln2_gain,
        q8,
        inverse,
        pairs,
        (d_own, d_far, resid, cot, w_out, flat(att)),
        given,
    )
    *rest, row_sums, d_resid, out_mine, out_theirs, mark = rest
    if blocks == 2:
        dk, dk_far, dv, dv_far = rest
        dk_far, dv_far = swap(dk_far, "blk", 0), swap(dv_far, "blk", 0)
    else:
        dk, dv = (lax.psum_scatter(a, "blk", scatter_dimension=1, tiled=True) for a in rest)
        dk_far, dv_far = jnp.zeros_like(dk), jnp.zeros_like(dv)
    dq, dk, dk_far, dv, dv_far = (flat(a) for a in (dq, dk, dk_far, dv, dv_far))
    out_arrived = swap(out_theirs, "blk", 0)
    out_far = swap(out_far, "blk", 0)
    out = layer(resid, out_own, out_far, b_down, [mark])
    sources = (act_one, dv, dv_far, w_value, dk, dk_far, key_norm, w_key, dq, query_norm, w_query, tok, d_resid)
    grad_tok, mine_q, mine_k, mine_two, *theirs, mark = project_back(
        owners, facts, (q_gain, k_gain, ln1_gain, up_sum, row_sums), sources, [out]
    )
    arrived_q, arrived_k, arrived_two = (swap(a, "blk", 0) for a in theirs)
    one = RowSum(height, bits, [(mine_q, arrived_q), (mine_k, arrived_k)])
    two = RowSum(height, bits, [(mine_two, arrived_two), (out_mine, out_arrived)])
    one = RowSum(height, bits, [(mine_q, arrived_q), (mine_k, arrived_k)])
    two = RowSum(height, bits, [(mine_two, arrived_two), (out_mine, out_arrived)])
    given = [mark]
    for bit in range(2, top):
        given = send_all(facts, (ff,), (bit,), given, LONG)
    given = send_all(facts, (one, two), (0, 1), given)
    given = send_all(facts, (one, two), (1, 0), given)
    ff_parts, given = send_top(facts, ff, width, folds, given)
    rest = one.join(two)
    given = send_all(facts, (rest,), (2,), given)
    ff_held = merge(ff_parts, given)
    given = [ff_held[0]]
    for bit in range(3, top + 1):
        given = send_all(facts, (rest,), (bit,), given)
    terms = [a.reshape(height, -1) for a in rest.parts[0]]
    for bit in range(1, blocks.bit_length() - 1):
        terms = [add_low(a, swap(a, "blk", bit)) for a in terms]
    terms += [swap(a, "blk", 0) for a in terms]
    grad_down, grad_up, grad_q, grad_k, grad_v, grad_out, *vectors = finish(facts, ff_held, terms, width, folds)
    t_ln2g, t_ln2b, t_bo, t_bd, t_ln1g, t_ln1b, t_bq, t_bv, t_qg, t_kg, t_bu = (v.reshape(-1) for v in vectors)
    return (
        out.reshape(tokens.shape),
        grad_tok.reshape(tokens.shape),
        t_ln1g,
        t_ln1b,
        grad_q,
        t_bq,
        grad_k,
        grad_v,
        t_bv,
        t_qg,
        t_kg,
        grad_out,
        t_bo,
        t_ln2g,
        t_ln2b,
        grad_up,
        t_bu,
        grad_down,
        t_bd,
    )


def solution(mesh):
    return jax.shard_map(
        local,
        mesh=mesh,
        in_specs=(
            P("seq", "blk", None),
            P("seq", None),
            P("seq", "blk", None),
            P(),
            P(),
            P(),
            P(),
            P(),
            P(),
            P(),
            P(),
            P(),
            P(),
            P(),
            P(),
            P(),
            P(),
            P(),
            P(),
            P(),
        ),
        out_specs=(
            P("seq", "blk", None),
            P("seq", "blk", None),
            P("seq"),
            P("seq"),
            P("seq", None),
            P("seq"),
            P("seq", None),
            P("seq", None),
            P("seq"),
            P("seq"),
            P("seq"),
            P("seq", None),
            P("seq"),
            P("seq"),
            P("seq"),
            P("seq", None),
            P("seq"),
            P("seq", None),
            P("seq"),
        ),
        check_vma=False,
    )
```

```python
import functools
import math

import jax
import jax.numpy as jnp
from jax import lax
from jax.experimental import pallas as pl
from jax.experimental.pallas import tpu as pltpu
from jax.sharding import PartitionSpec as P

H = 12
HD = 64
EPSILON = 1e-06
BLOCKED = -1024.0
MIB = 1 << 20
LONG = 10**12
BIG = 63
GROUP = 2
CORE, QUERY_START, KEY_START, SIDES = 0, 1, 2, 4
SMALL = 10
NT = (((1,), (1,)), ((), ()))
TN = (((0,), (0,)), ((), ()))
NN = (((1,), (0,)), ((), ()))


def dot(one, two, dims=NN):
    return lax.dot_general(one, two, dims, preferred_element_type=jnp.float32)


def low(values):
    return values.astype(jnp.bfloat16)


def wide(values):
    return values.astype(jnp.float32)


def row_stats(values):
    average = jnp.mean(values, axis=-1, keepdims=True)
    centred = values - average
    variance = jnp.mean(centred * centred, axis=-1, keepdims=True)
    scale = lax.rsqrt(variance + EPSILON)
    return centred * scale, scale


def norm_back(unit, scale, grads):
    return scale * (
        grads
        - jnp.mean(grads, axis=-1, keepdims=True)
        - unit * jnp.mean(grads * unit, axis=-1, keepdims=True)
    )


def head_mean(values, exact=False):
    parts = []
    for start in range(0, values.shape[1], 4 * HD):
        part = values[:, start : start + 4 * HD]
        width = part.shape[1]
        rows = lax.broadcasted_iota(jnp.int32, (width, width), 0) // HD
        columns = lax.broadcasted_iota(jnp.int32, (width, width), 1) // HD
        average = jnp.where(rows == columns, 1.0 / HD, 0.0).astype(jnp.bfloat16)
        upper = low(part)
        total = dot(upper, average)
        if exact:
            total = total + dot(low(part - wide(upper)), average)
        parts.append(total)
    return jnp.concatenate(parts, axis=1)


def head_stats(values):
    centred = values - head_mean(values, exact=True)
    scale = lax.rsqrt(head_mean(centred * centred) + EPSILON)
    return centred * scale, scale


def head_norm_back(unit, scale, grads):
    return scale * (grads - head_mean(grads) - unit * head_mean(grads * unit))


def vector(ref):
    return wide(ref[...]).reshape(1, -1)


def column_sum(values):
    return jnp.sum(values, axis=0, keepdims=True)


def call(body, grid, ins, outs, scratch=(), prefetch=None, after=(), limit=24, name=None, cost=1000):
    ins = list(ins) + [(a, pl.BlockSpec(memory_space=pltpu.SMEM if a.size == 1 else pl.ANY)) for a in after]
    lead = len(ins) - len(after) + (prefetch is not None)

    def kernel(*refs):
        body(*refs[:lead], *refs[lead + len(after) :])

    grid_spec = pltpu.PrefetchScalarGridSpec(
        num_scalar_prefetch=int(prefetch is not None),
        grid=grid,
        in_specs=[spec for _, spec in ins],
        out_specs=[spec for _, spec in outs],
        scratch_shapes=list(scratch),
    )
    arrays = [array for array, _ in ins]
    return pl.pallas_call(
        kernel,
        grid_spec=grid_spec,
        out_shape=[shape for shape, _ in outs],
        compiler_params=pltpu.CompilerParams(vmem_limit_bytes=limit * MIB),
        name=name,
        cost_estimate=pl.CostEstimate(flops=cost, bytes_accessed=1000, transcendentals=0),
    )(*([] if prefetch is None else [prefetch]), *arrays)


def whole(array):
    rank = len(array.shape)
    return (array, pl.BlockSpec(array.shape, lambda *_: (0,) * rank))


def whole_out(shape, dtype):
    rank = len(shape)
    return (jax.ShapeDtypeStruct(shape, dtype), pl.BlockSpec(shape, lambda *_: (0,) * rank))


def scalars(array):
    return (array, pl.BlockSpec(memory_space=pltpu.SMEM))


def project_body(gain, bias, bv, kg, *refs):
    sources, refs = refs[:3], refs[3:]
    act_hbm, pair_hbm, k_hbm = refs[:3]
    targets, refs = refs[3:6], refs[6:]
    act, pair, k_pre, got, put = refs
    loads = [pltpu.make_async_copy(a, b, got.at[i]) for i, (a, b) in enumerate(zip(sources, targets))]
    for load in loads:
        load.start()
    sends = []

    def send(source, target):
        copy = pltpu.make_async_copy(source, target, put.at[len(sends)])
        copy.start()
        sends.append(copy)

    tok, wv, wk = targets
    loads[0].wait()
    unit, _ = row_stats(wide(tok[...]))
    act_one = low(unit * vector(gain) + vector(bias))
    act[...] = act_one
    send(act, act_hbm)
    loads[1].wait()
    pair[1] = low(dot(act_one, wv[...]) + vector(bv))
    send(pair.at[1], pair_hbm.at[1])
    loads[2].wait()
    key_unit, key_scale = head_stats(dot(act_one, wk[...]))
    pair[0] = low(key_unit * vector(kg))
    send(pair.at[0], pair_hbm.at[0])
    k_pre[0] = low(key_unit)
    k_pre[1] = low(key_scale)
    send(k_pre, k_hbm)
    for copy in sends:
        copy.wait()


def projections(tok, gain, bias, wk, wv, bv, kg):
    count, width = tok.shape
    anywhere = pl.BlockSpec(memory_space=pl.ANY)
    sources = (tok, wv, wk)
    ins = [whole(a) for a in (gain, bias, bv, kg)] + [(a, anywhere) for a in sources]

    def rows(dtype):
        return jax.ShapeDtypeStruct((count, width), dtype)

    pair = jax.ShapeDtypeStruct((2, count, width), jnp.bfloat16)
    results = (rows(jnp.bfloat16), pair, pair)
    outs = [(a, anywhere) for a in results]
    scratch = [pltpu.VMEM(a.shape, a.dtype) for a in sources + results]
    scratch += [pltpu.SemaphoreType.DMA((3,)), pltpu.SemaphoreType.DMA((4,))]
    return call(project_body, (1,), ins, outs, scratch, limit=BIG, name="projections")


def query_body(bias, gain, act, w_query, q8, norm):
    unit, scale = head_stats(dot(act[...], w_query[...]) + vector(bias))
    q8[...] = low(unit * vector(gain)) * (1.0 / math.sqrt(HD))
    norm[0] = low(unit)
    norm[1] = low(scale)


def queries(act, w_query, bias, gain):
    ins = [whole(a) for a in (bias, gain, act, w_query)]
    outs = [whole_out(act.shape, jnp.bfloat16), whole_out((2,) + act.shape, jnp.bfloat16)]
    return call(query_body, (1,), ins, outs, limit=BIG, name="queries", cost=LONG)


def segment_column(positions, lengths, sequence, slots):
    end = lengths[sequence, 0]
    segment = (positions >= end).astype(jnp.int32)
    for slot in range(1, slots):
        end = end + lengths[sequence, slot]
        segment = segment + (positions >= end).astype(jnp.int32)
    return segment


def query_lanes(count, start, lengths, sequence, slots):
    positions = lax.broadcasted_iota(jnp.int32, (count, 2 * HD), 0) + start
    lane = lax.broadcasted_iota(jnp.int32, (count, 2 * HD), 1) & (HD - 1)
    segment = segment_column(positions, lengths, sequence, slots)
    return jnp.where(segment == lane, 1.0, 0.0).astype(jnp.bfloat16)


def key_lanes(count, start, lengths, sequence, slots):
    positions = lax.broadcasted_iota(jnp.int32, (count, 2 * HD), 0) + start
    lane = lax.broadcasted_iota(jnp.int32, (count, 2 * HD), 1) & (HD - 1)
    segment = segment_column(positions, lengths, sequence, slots)
    open_to = (segment == lane) & (lane < slots)
    return jnp.where(open_to, 0.0, BLOCKED).astype(jnp.bfloat16)


def pair_spec(array):
    return (array, pl.BlockSpec((1, array.shape[1], 2 * HD), lambda s, h: (s, 0, h)))


def low_half(count):
    return lax.broadcasted_iota(jnp.int32, (count, 2 * HD), 1) < HD


def attend_masks(slots, lengths, facts, q_mask, k_masks, sequence, place):
    span = q_mask.shape[0]

    @pl.when(place == 0)
    def _():
        q_mask[...] = query_lanes(span, facts[QUERY_START], lengths, sequence, slots)
        for chunk, mask in enumerate(k_masks):
            mask[...] = key_lanes(mask.shape[0], facts[KEY_START + chunk], lengths, sequence, slots)


def attend_pair(q8, pairs, q_mask, k_masks, lanes):
    first = low_half(q8.shape[1])
    query = q8[0, :, lanes]
    one = jnp.where(first, query, q_mask[...])
    two = jnp.where(first, q_mask[...], query)
    sums = [None, None]
    for pair, k_mask in zip(pairs, k_masks):
        key, value, mask = pair[0, 0, :, lanes], pair[1, 0, :, lanes], k_mask[...]
        key_first = low_half(key.shape[0])
        ones = jnp.ones_like(value)
        for side, operand in enumerate((one, two)):
            pick = key_first if side == 0 else ~key_first
            lifted = low(jnp.exp(dot(operand, jnp.where(pick, key, mask), NT)))
            term = dot(lifted, jnp.where(pick, value, ones))
            sums[side] = term if sums[side] is None else sums[side] + term
    top = jnp.where(first, sums[0], sums[1])
    total = pltpu.roll(jnp.where(first, sums[1], sums[0]), HD, 1)
    inverse = jnp.where(total > 0.0, 1.0 / total, 0.0)
    return low(top * inverse), inverse


def attend_back_pair(query, queries, d_low, d_values, pairs, k_masks):
    key_grads, value_grads, d_query_t = [], [], None
    for pair, k_mask in zip(pairs, k_masks):
        key, value, mask = pair[0, 0], pair[1, 0], k_mask[...]
        key_first = low_half(key.shape[0])
        ones = jnp.ones_like(value)
        key_t = key.T
        key_terms, value_terms, query_terms = [], [], []
        for side in range(2):
            pick = key_first if side == 0 else ~key_first
            lifted = jnp.exp(dot(jnp.where(pick, key, mask), queries[side], NT))
            shifted = dot(jnp.where(pick, value, ones), d_values[side], NT)
            d_scores = low(lifted * shifted)
            value_terms.append(dot(low(lifted), d_low))
            key_terms.append(dot(d_scores, query))
            query_terms.append(dot(key_t[side * HD : (side + 1) * HD], d_scores))
        key_grads.append(low(jnp.where(key_first, key_terms[0], key_terms[1])))
        value_grads.append(low(jnp.where(key_first, value_terms[0], value_terms[1])))
        term = jnp.concatenate(query_terms, axis=0)
        d_query_t = term if d_query_t is None else d_query_t + term
    return d_query_t.T * (1.0 / math.sqrt(HD)), key_grads, value_grads


def delta_lanes(att, d_low, pick):
    lane = lax.broadcasted_iota(jnp.int32, att.shape, 1) & (HD - 1)
    delta = -jnp.sum(jnp.where(pick, wide(att) * wide(d_low), 0.0), axis=1, keepdims=True)
    high = low(delta)
    middle = low(delta - wide(high))
    rest = low(delta - wide(high) - wide(middle))
    zero = jnp.zeros((), jnp.bfloat16)
    extra = jnp.where(lane == 0, high, jnp.where(lane == 1, middle, jnp.where(lane == 2, rest, zero)))
    return jnp.where(pick, d_low, extra)


def attend_back_body(slots, chunks, facts, lengths, gain, q8, inverse, *refs):
    pairs, refs = refs[:chunks], refs[chunks:]
    sources, refs = refs[:6], refs[6:]
    d_query, refs = refs[0], refs[1:]
    d_keys, d_vals, refs = refs[:chunks], refs[chunks : 2 * chunks], refs[2 * chunks :]
    rows, d_resid_hbm, grad_mine, grad_theirs, mark = refs[:5]
    q_mask, refs = refs[5], refs[6:]
    mark[0] = 0
    k_masks, targets, refs = refs[:chunks], refs[chunks : chunks + 6], refs[chunks + 6 :]
    d_own, d_far, resid, cot, w_out, att = targets
    d_att, back, got, put = refs
    span, width = q8.shape[1], resid.shape[1]
    heads = H // 2
    step = pl.program_id(0)
    sequence, place = step // heads, step % heads

    def fetch(number):
        return pltpu.make_async_copy(sources[number], targets[number], got.at[number])

    def send_back():
        return pltpu.make_async_copy(back, d_resid_hbm, put.at[0])

    @pl.when(step == 0)
    def _():
        for number in range(6):
            fetch(number).start()
        for number in range(6):
            fetch(number).wait()
        grads = wide(d_own[...]) + wide(d_far[...])
        unit, scale = row_stats(resid[...])
        rows[0:1, :] = column_sum(grads * unit)
        rows[1:2, :] = column_sum(grads)
        total = wide(cot[...]) + norm_back(unit, scale, grads * vector(gain))
        back[...] = total
        send_back().start()
        branch = low(total)
        rows[2:3, :] = column_sum(wide(branch))
        rows[3:4, :] = column_sum(wide(cot[...]))
        d_att[...] = low(dot(branch, w_out[...], NT))
        product = low(dot(att[...], branch, TN))
        half = width // 2
        for side in range(2):

            @pl.when(facts[CORE] == side)
            def _():
                grad_mine[...] = product[:, side * half : (side + 1) * half]
                grad_theirs[...] = product[:, (1 - side) * half : (2 - side) * half]

    @pl.when(place == 0)
    def _():
        q_mask[...] = query_lanes(span, facts[QUERY_START], lengths, sequence, slots)
        for chunk, mask in enumerate(k_masks):
            mask[...] = key_lanes(mask.shape[0], facts[KEY_START + chunk], lengths, sequence, slots)

    block = (pl.ds(sequence * span, span), pl.ds(pl.multiple_of(place * 128, 128), 128))
    first = low_half(span)
    query = q8[0]
    queries = (jnp.where(first, query, q_mask[...]), jnp.where(first, q_mask[...], query))
    d_low = low(wide(d_att[block]) * wide(inverse[0]))
    held = att[block]
    d_values = [delta_lanes(held, d_low, first), delta_lanes(held, d_low, ~first)]
    grads, key_grads, value_grads = attend_back_pair(query, queries, d_low, d_values, pairs, k_masks)
    d_query[0] = low(grads)
    for chunk in range(chunks):
        d_keys[chunk][0] = key_grads[chunk]
        d_vals[chunk][0] = value_grads[chunk]

    @pl.when(step == pl.num_programs(0) - 1)
    def _():
        send_back().wait()


def pair_block(array, lead, steps, group=1):
    heads = H // 2 // group

    def index(i, *_):
        i = jnp.minimum(i, steps - 1)
        return (i // heads, 0, i % heads)

    shape = (1, array.shape[-2], 2 * HD * group)
    if lead:
        return (array, pl.BlockSpec((2,) + shape, lambda i, *_: (0,) + index(i)))
    return (array, pl.BlockSpec(shape, index))


def attend_back(facts, lengths, gain, q8, inverse, pairs, sources, after):
    count, span, width = q8.shape
    steps = count * H // 2
    tokens = count * span
    anywhere = pl.BlockSpec(memory_space=pl.ANY)

    def shape(sizes, dtype):
        return jax.ShapeDtypeStruct(sizes, dtype)

    ins = [scalars(facts), scalars(lengths), whole(gain)]
    ins += [pair_block(q8, False, steps), pair_block(inverse, False, steps)]
    ins += [pair_block(a, True, steps) for a in pairs] + [(a, anywhere) for a in sources]
    outs = [pair_block(shape((count, span, width), jnp.bfloat16), False, steps)]
    outs += [pair_block(shape(a.shape[1:], jnp.bfloat16), False, steps) for a in pairs + pairs]
    outs += [
        whole_out((8, width), jnp.float32),
        (shape((tokens, width), jnp.float32), anywhere),
        whole_out((width, width // 2), jnp.bfloat16),
        whole_out((width, width // 2), jnp.bfloat16),
        (jax.ShapeDtypeStruct((1,), jnp.int32), pl.BlockSpec(memory_space=pltpu.SMEM)),
    ]
    scratch = [pltpu.VMEM((a.shape[-2], 2 * HD), jnp.bfloat16) for a in [q8] + list(pairs)]
    scratch += [pltpu.VMEM(a.shape, a.dtype) for a in sources]
    scratch += [pltpu.VMEM((tokens, width), d) for d in (jnp.bfloat16, jnp.float32)]
    scratch += [pltpu.SemaphoreType.DMA((6,)), pltpu.SemaphoreType.DMA((1,))]
    body = functools.partial(attend_back_body, lengths.shape[1], len(pairs))
    return call(body, (steps,), ins, outs, scratch, after=after, limit=BIG, name="attend_back")


def gelu_pair(values):
    half = 0.5 + 0.5 * lax.erf(values * math.sqrt(0.5))
    slope = half + values * (math.sqrt(0.5 / math.pi) * jnp.exp(-0.5 * values * values))
    return values * half, slope


def layer_body(resid, own, far, bias, out, mark):
    mark[0] = 0
    out[...] = low(resid[...] + wide(own[...]) + wide(far[...]) + vector(bias))


def layer(resid, own, far, bias, after):
    count, width = resid.shape
    spec = pl.BlockSpec((count // 2, width), lambda i: (i, 0))
    ins = [(resid, spec), (own, spec), (far, spec), whole(bias)]
    outs = [(jax.ShapeDtypeStruct((count, width), jnp.bfloat16), spec)]
    outs.append((jax.ShapeDtypeStruct((1,), jnp.int32), pl.BlockSpec(memory_space=pltpu.SMEM)))
    return call(layer_body, (2,), ins, outs, after=after, name="layer")


def attend_body(slots, chunks, lengths, facts, b_out, gain, bias, q8, *refs):
    pairs, refs = refs[:chunks], refs[chunks:]
    sources, refs = refs[:2], refs[2:]
    att, inverse, resid, act, q_mask = refs[:5]
    k_masks, refs = refs[5 : 5 + chunks], refs[5 + chunks :]
    tok, w_out, held, got = refs
    span = q8.shape[1]
    heads = H // 2 // GROUP
    step = pl.program_id(0)
    last = pl.num_programs(0) - 1
    targets = (tok, w_out)

    def fetch(number):
        return pltpu.make_async_copy(sources[number], targets[number], got.at[number])

    @pl.when(step == 0)
    def _():
        fetch(0).start()
        fetch(1).start()

    @pl.when(step < last)
    def _():
        sequence, place = step // heads, step % heads
        attend_masks(slots, lengths, facts, q_mask, k_masks, sequence, place)
        for member in range(GROUP):
            lanes = slice(member * 128, (member + 1) * 128)
            values, inv = attend_pair(q8, pairs, q_mask, k_masks, lanes)
            att[0, :, lanes] = values
            inverse[0, :, lanes] = low(inv)
            start = pl.multiple_of((place * GROUP + member) * 128, 128)
            held[pl.ds(sequence * span, span), pl.ds(start, 128)] = values

    @pl.when(step == last)
    def _():
        fetch(0).wait()
        fetch(1).wait()
        total = wide(tok[...]) + dot(held[...], w_out[...]) + vector(b_out)
        resid[...] = total
        act[...] = low(row_stats(total)[0] * vector(gain) + vector(bias))


def attend(lengths, facts, b_out, gain, bias, q8, pairs, tok, w_out):
    count, span, width = q8.shape
    steps = count * (H // 2 // GROUP)
    tokens = count * span
    anywhere = pl.BlockSpec(memory_space=pl.ANY)

    def shape(dtype):
        return jax.ShapeDtypeStruct((count, span, width), dtype)

    ins = [scalars(lengths), scalars(facts)] + [whole(a) for a in (b_out, gain, bias)]
    ins += [pair_block(q8, False, steps, GROUP)] + [pair_block(a, True, steps, GROUP) for a in pairs]
    ins += [(tok, anywhere), (w_out, anywhere)]
    outs = [
        pair_block(shape(jnp.bfloat16), False, steps, GROUP),
        pair_block(shape(jnp.bfloat16), False, steps, GROUP),
        whole_out((tokens, width), jnp.float32),
        whole_out((tokens, width), jnp.bfloat16),
    ]
    scratch = [pltpu.VMEM((a.shape[-2], 2 * HD), jnp.bfloat16) for a in [q8] + list(pairs)]
    scratch += [pltpu.VMEM(tok.shape, jnp.bfloat16), pltpu.VMEM(w_out.shape, jnp.bfloat16)]
    scratch += [pltpu.VMEM(tok.shape, jnp.bfloat16), pltpu.SemaphoreType.DMA((2,))]
    body = functools.partial(attend_body, lengths.shape[1], len(pairs))
    return call(body, (steps + 1,), ins, outs, scratch, limit=BIG, name="attend")


def feed_body(
    height, facts, act, act_far, cot, cot_far, w_up, w_down, b_up,
    up_sum, kept_own, kept_far, d_own, d_far, hbm_0, hbm_1, hbm_2, hbm_3,
    own_d, far_d, grads, put,
):
    step = pl.program_id(0)
    width, tile = w_up.shape
    steps = pl.num_programs(0)
    start = (facts[CORE] * steps + step) * tile
    bias = wide(b_up[pl.ds(pl.multiple_of(start, tile), tile)]).reshape(1, -1)
    @pl.when(step == 0)
    def _():
        for ref in (own_d, far_d):
            ref[...] = jnp.zeros_like(ref)

    down_grads = up_grads = sums = None
    for values, upper, kept, d_sum in ((act, cot, kept_own, own_d), (act_far, cot_far, kept_far, far_d)):
        hidden, slope = gelu_pair(dot(values[...], w_up[...]) + bias)
        hidden = low(hidden)
        d_up = low(dot(upper[...], w_down[...], NT) * slope)
        kept[...] = hidden
        d_sum[...] += dot(d_up, w_up[...], NT)
        down_term = dot(hidden, upper[...], TN)
        up_term = dot(values[...], d_up, TN)
        sum_term = column_sum(wide(d_up))
        down_grads = down_term if down_grads is None else down_grads + down_term
        up_grads = up_term if up_grads is None else up_grads + up_term
        sums = sum_term if sums is None else sums + sum_term
    up_sum[...] = sums
    folds = grads.shape[2] // width // 2
    here = tile // (folds * height)
    tall = down_grads.reshape(here // 4, 4, folds, height, width)
    broad = up_grads.reshape(2, width // (8 * height), 4, height, tile)
    spot = facts[SIDES] + 2 * facts[SIDES + 1]
    rows = here // 4 * height
    lines = pl.ds(pl.multiple_of(step * rows, 16), rows)
    for place in range(4):
        which = place ^ spot
        for fold in range(folds):
            columns = slice(fold * width, (fold + 1) * width)
            grads[which, lines, columns] = low(tall[:, place, fold].reshape(rows, width))
        for top in range(2):
            columns = pl.ds(pl.multiple_of(folds * width + (2 * step + top) * tile, tile), tile)
            grads[which, :, columns] = low(broad[top, :, place].reshape(grads.shape[1], tile))

    def copies(at):
        line = pl.ds(pl.multiple_of(at * rows, 16), rows)
        columns = pl.ds(pl.multiple_of((folds + 2 * at) * tile, tile), 2 * tile)
        for place, target in enumerate((hbm_0, hbm_1, hbm_2, hbm_3)):
            left = slice(0, folds * width)
            yield pltpu.make_async_copy(grads.at[place, line, left], target.at[line, left], put.at[at, 2 * place])
            yield pltpu.make_async_copy(
                grads.at[place, :, columns], target.at[:, columns], put.at[at, 2 * place + 1]
            )

    for copy in copies(step):
        copy.start()

    @pl.when(step == steps - 1)
    def _():
        d_far[...] = low(far_d[...])
        d_own[...] = low(own_d[...])
        for at in range(folds // 2):
            for copy in copies(at):
                copy.wait()


def feed(height, facts, act, act_far, cot, cot_far, w_up, w_down, b_up):
    count, width = act.shape
    hidden = w_up.shape[1]
    steps = hidden // width // 2
    ins = [whole(a) for a in (act, act_far, cot, cot_far)]
    ins += [
        (w_up, pl.BlockSpec((width, width), lambda j, facts: (0, facts[CORE] * steps + j))),
        (w_down, pl.BlockSpec((width, width), lambda j, facts: (facts[CORE] * steps + j, 0))),
        whole(b_up),
    ]
    up_sum = (
        jax.ShapeDtypeStruct((1, hidden // 2), jnp.float32),
        pl.BlockSpec((1, width), lambda j, facts: (0, j)),
    )
    half_sum = whole_out((count, width), jnp.bfloat16)
    part = jax.ShapeDtypeStruct((width // 8, 2 * hidden), jnp.bfloat16)
    kept = (
        jax.ShapeDtypeStruct((count, hidden // 2), jnp.bfloat16),
        pl.BlockSpec((count, width), lambda j, facts: (0, j)),
    )
    outs = [up_sum, kept, kept] + [half_sum] * 2 + [(part, pl.BlockSpec(memory_space=pl.ANY))] * 4
    scratch = [pltpu.VMEM((count, width), jnp.float32)] * 2 + [pltpu.VMEM((4,) + part.shape, jnp.bfloat16)]
    scratch += [pltpu.SemaphoreType.DMA((steps, 8))]
    body = functools.partial(feed_body, height)
    return call(body, (steps,), ins, outs, scratch, prefetch=facts, limit=BIG, name="feed")


def result_body(facts, own, far, w_down, out_own, out_far, mark, sum_own, sum_far):
    step = pl.program_id(0)
    mark[0] = 0

    @pl.when(step == 0)
    def _():
        sum_own[...] = jnp.zeros_like(sum_own)
        sum_far[...] = jnp.zeros_like(sum_far)

    sum_own[...] += dot(own[...], w_down[...])
    sum_far[...] += dot(far[...], w_down[...])

    @pl.when(step == pl.num_programs(0) - 1)
    def _():
        out_far[...] = low(sum_far[...])
        out_own[...] = low(sum_own[...])


def result(facts, own, far, w_down, after):
    count, width = own.shape[0], w_down.shape[1]
    steps = own.shape[1] // width
    block = pl.BlockSpec((count, width), lambda j, facts: (0, j))
    ins = [(own, block), (far, block)]
    ins.append((w_down, pl.BlockSpec((width, width), lambda j, facts: (facts[CORE] * steps + j, 0))))
    outs = [whole_out((count, width), jnp.bfloat16)] * 2
    outs.append((jax.ShapeDtypeStruct((1,), jnp.int32), pl.BlockSpec(memory_space=pltpu.SMEM)))
    scratch = [pltpu.VMEM((count, width), jnp.float32)] * 2
    name = "result"
    return call(result_body, (steps,), ins, outs, scratch, prefetch=facts, after=after, limit=BIG, name=name, cost=LONG)


def project_back_body(owners, parts, core, qg, kg, gain, up_sum, row_sums, *refs):
    sources, refs = refs[:parts], refs[parts:]
    grad_hbm, mine_q, mine_k, mine_two, theirs_q, theirs_k, theirs_two, mark = refs[:8]
    targets, refs = refs[8 : 8 + parts], refs[8 + parts :]
    mark[0] = 0
    grad, one, two, got, put = refs
    copies = [pltpu.make_async_copy(a, b, got.at[i]) for i, (a, b) in enumerate(zip(sources, targets))]
    for copy in copies:
        copy.start()
    waited = set()

    def use(*places):
        for place in places:
            if place not in waited:
                copies[place].wait()
                waited.add(place)
        return [targets[place] for place in places]

    def joined(*places):
        return jnp.concatenate([wide(ref[...]) for ref in use(*places)], axis=1)

    act, wv, wk, wq = 0, 3, 7, 10
    half = one.shape[2] // 2

    side_one = core[0] == 0

    def place_pieces(piece, spots):
        left, right = piece[:, :half], piece[:, half:]
        own, far = jnp.where(side_one, left, right), jnp.where(side_one, right, left)
        for target, start, first, last in spots:
            columns = slice(start, start + last - first)
            target[0, :, columns] = own[:, first:last]
            target[1, :, columns] = far[:, first:last]

    d_value = low(joined(1) + joined(2))
    (act_ref,) = use(act)
    place_pieces(low(dot(act_ref[...], d_value, TN)), ((two, 0, 0, half),))
    bv_sum = column_sum(wide(d_value))
    (w_ref,) = use(wv)
    back = dot(d_value, w_ref[...], NT)
    d_key_low = joined(4) + joined(5)
    (pre,) = use(6)
    unit, scale = wide(pre[0]), wide(pre[1])
    kg_sum = column_sum(d_key_low * unit)
    d_key = low(head_norm_back(unit, scale, d_key_low * vector(kg)))
    place_pieces(low(dot(act_ref[...], d_key, TN)), ((one, half, 0, half),))
    sends = []

    def send(source, target):
        copy = pltpu.make_async_copy(source, target, put.at[len(sends)])
        copy.start()
        sends.append(copy)

    send(two.at[0, :, :half], mine_two.at[:, :half])
    two[1, :, half:] = jnp.zeros((two.shape[1], 128), jnp.bfloat16)
    send(two.at[1], theirs_two)
    send(one.at[1, :, half:], theirs_k)
    send(one.at[0, :, half:], mine_k)
    (w_ref,) = use(wk)
    back = back + dot(d_key, w_ref[...], NT)
    d_low = joined(8)
    (pre,) = use(9)
    unit, scale = wide(pre[0]), wide(pre[1])
    qg_sum = column_sum(d_low * unit)
    d_query = low(head_norm_back(unit, scale, d_low * vector(qg)))
    bq_sum = column_sum(wide(d_query))
    place_pieces(low(dot(act_ref[...], d_query, TN)), ((one, 0, 0, half),))
    send(one.at[0, :, :half], mine_q)
    send(one.at[1, :, :half], theirs_q)
    (w_ref,) = use(wq)
    grads = back + dot(d_query, w_ref[...], NT)
    tok, d_resid = use(11, 12)
    unit, scale = row_stats(wide(tok[...]))
    grad[...] = d_resid[...] + norm_back(unit, scale, grads * vector(gain))
    send(grad, grad_hbm)
    full = [row_sums[0:4, :], column_sum(grads * unit), column_sum(grads), bq_sum, bv_sum, qg_sum, kg_sum]
    full = jnp.concatenate(full, axis=0)
    width = full.shape[1]
    full = jnp.concatenate([full, jnp.zeros((128 - full.shape[0], width), jnp.float32)], axis=0)
    columns = full.T
    lane = lax.broadcasted_iota(jnp.int32, columns.shape, 1)
    hidden = 2 * up_sum.shape[1]
    folds = hidden // width
    first = core[0] == 0
    halves = [jnp.where(first, up_sum[...], 0.0), jnp.where(first, 0.0, up_sum[...])]
    tall = jnp.broadcast_to(jnp.concatenate(halves, axis=1), (128, hidden)).T.reshape(owners, folds, width // owners, 128)
    for fold in range(folds):
        piece = tall[:, fold].reshape(width, 128)
        columns = jnp.where(lane == SMALL + fold, piece, columns)
    end = slice(half, half + 128)
    two[0, :, end] = low(columns)
    send(two.at[0, :, end], mine_two.at[:, end])
    for copy in sends:
        copy.wait()


def project_back(owners, core, vectors, sources, after):
    act = sources[0]
    count, width = act.shape
    anywhere = pl.BlockSpec(memory_space=pl.ANY)
    ins = [scalars(core)] + [whole(a) for a in vectors] + [(a, anywhere) for a in sources]
    one = jax.ShapeDtypeStruct((width, width), jnp.bfloat16)
    two = jax.ShapeDtypeStruct((width, width // 2 + 128), jnp.bfloat16)
    total = jax.ShapeDtypeStruct((count, width), jnp.float32)
    piece = jax.ShapeDtypeStruct((width, width // 2), jnp.bfloat16)
    outs = [(a, anywhere) for a in (total, piece, piece, two, piece, piece, two)]
    outs.append((jax.ShapeDtypeStruct((1,), jnp.int32), pl.BlockSpec(memory_space=pltpu.SMEM)))
    scratch = [pltpu.VMEM(a.shape, a.dtype) for a in sources]
    scratch += [pltpu.VMEM(total.shape, total.dtype)] + [pltpu.VMEM((2,) + a.shape, a.dtype) for a in (one, two)]
    scratch += [pltpu.SemaphoreType.DMA((len(sources),)), pltpu.SemaphoreType.DMA((8,))]
    body = functools.partial(project_back_body, owners, len(sources))
    return call(body, (1,), ins, outs, scratch, after=after, limit=BIG, name="project_back", cost=1000)


def swap(values, axis, bit):
    count = lax.axis_size(axis)
    return lax.ppermute(values, axis, [(i, i ^ (1 << bit)) for i in range(count)])


def add_low(one, two):
    return low(wide(one) + wide(two))


def split_body(counts, bits, facts, *refs):
    total = sum(sum(count) for count in counts)
    inputs, outs = refs[:total], refs[total:]
    place = 0
    for group, count in enumerate(counts):
        give, keep = outs[2 * group : 2 * group + 2]
        mine = facts[SIDES + bits[group]]
        start = 0
        for terms in count:
            columns = slice(start, start + inputs[place].shape[3])
            for half, out in ((1 - mine, give), (mine, keep)):
                held = wide(inputs[place][:, half])
                for other in range(place + 1, place + terms):
                    held = held + wide(inputs[other][:, half])
                out[:, :, columns] = low(held)
            start += inputs[place].shape[3]
            place += terms


def merge_body(parts, *refs):
    out = refs[-1]
    start = 0
    for kept, coming in zip(refs[:parts], refs[parts : 2 * parts]):
        columns = slice(start, start + kept.shape[1])
        out[:, columns] = low(wide(kept[...]) + wide(coming[...]))
        start += kept.shape[1]


def merge(parts, after):
    height, width = parts[0][0].shape[0], sum(kept.shape[1] for kept, _ in parts)
    ins = [whole(kept) for kept, _ in parts] + [whole(coming) for _, coming in parts]
    outs = [whole_out((height, width), jnp.bfloat16)]
    held = call(functools.partial(merge_body, len(parts)), (1,), ins, outs, after=after, name="merge")[0]
    for bit in range(1, lax.axis_size("blk").bit_length() - 1):
        held = add_low(held, swap(held, "blk", bit))
    return held, swap(held, "blk", 0)


def top_body(tile, place, facts, *refs):
    terms, (down, give, keep) = refs[:-3], refs[-3:]
    sums = [wide(kept[...]) + wide(coming[...]) for kept, coming in zip(terms[::2], terms[1::2])]
    width = down.shape[1]
    lower, upper = sums if len(sums) == 2 else (sums[0][:, :width], sums[0][:, width:])
    down[...] = low(lower)
    for block in range(give.shape[1] // tile):
        columns = slice(block * tile, (block + 1) * tile)
        for top in range(2):
            start = (2 * block + top) * tile
            piece = low(upper[:, start : start + tile])

            @pl.when(facts[SIDES + place] == top)
            def _():
                keep[:, columns] = piece

            @pl.when(facts[SIDES + place] != top)
            def _():
                give[:, columns] = piece


def send_top(facts, ff, tile, folds, after):
    owners, blocks = lax.axis_size("seq"), lax.axis_size("blk")
    top = owners.bit_length() - 2
    ins = [scalars(facts)] + [whole(a.reshape(ff.height, -1)) for part in ff.parts for a in part]
    outs = [whole_out((ff.height, size), jnp.bfloat16) for size in (folds * tile, folds // 2 * tile, folds // 2 * tile)]
    down, give, keep = call(functools.partial(top_body, tile, top), (1,), ins, outs, after=after, name="top")
    moves = [
        (s * blocks + b, (s ^ (1 << top)) * blocks + b) for s in range(owners) for b in range(blocks) if (s >> top) != b % 2
    ]
    return [(down, lax.ppermute(down, ("seq", "blk"), moves)), (keep, swap(give, "seq", top))], [down, give]


def send_all(facts, sums, bits, after=(), cost=1000, limit=24):
    terms, outs = [], []
    for one, bit in zip(sums, bits):
        axis = one.left.index(bit)
        before, rows = 1 << axis, one.height << (len(one.left) - axis - 1)
        for part in one.parts:
            terms += [whole(a.reshape(before, 2, rows, a.shape[-1])) for a in part]
        width = sum(part[0].shape[-1] for part in one.parts)
        outs += [whole_out((before, rows, width), jnp.bfloat16)] * 2
    body = functools.partial(split_body, [[len(part) for part in one.parts] for one in sums], bits)
    results = call(body, (1,), [scalars(facts)] + terms, outs, after=after, limit=limit, name="split", cost=cost)
    return [one.sent(bit, *results[2 * i : 2 * i + 2]) for i, (one, bit) in enumerate(zip(sums, bits))]


class RowSum:
    def __init__(self, height, left, parts):
        self.height, self.left, self.parts = height, left, parts

    def sent(self, bit, given, kept):
        self.parts = [(kept, swap(given, "seq", bit))]
        self.left = [other for other in self.left if other != bit]
        return given

    def join(self, *others):
        assert all(self.left == other.left for other in others)
        return RowSum(self.height, self.left, sum((other.parts for other in others), self.parts))

    def last(self):
        return [(a.reshape(self.height, -1), b.reshape(self.height, -1)) for a, b in self.parts]


def place_halves(core, held, other, out, rows, start, half):
    columns = slice(start, start + half)
    own, far = wide(held[:, columns]), wide(other[:, columns])
    first = core[0] == 0
    out[rows, :half] = jnp.where(first, own, far)
    out[rows, half:] = jnp.where(first, far, own)


def finish_ff_body(place, core, held, other, grad_down, grad_up):
    height, width = held.shape[0], grad_down.shape[1]
    folds = grad_down.shape[0] // height
    for fold in range(folds):
        columns = slice(fold * width, (fold + 1) * width)
        own, far = wide(held[:, columns]), wide(other[:, columns])
        grad_down[fold * height : (fold + 1) * height, :] = jnp.where(core[SIDES + place] == core[CORE], own, far)
    place_halves(core, held, other, grad_up, slice(0, height), folds * width, folds * width // 2)


def finish_attention_body(core, kept, coming, far_kept, far_coming, *outs):
    half = outs[0].shape[1] // 2
    held = wide(kept[...]) + wide(coming[...])
    other = wide(far_kept[...]) + wide(far_coming[...])
    first = core[CORE] == 0
    left, right = jnp.where(first, held, other), jnp.where(first, other, held)
    starts = (0, half, 2 * half, 3 * half + 128)
    for start, out in zip(starts, outs[:4]):
        out[:, :half] = left[:, start : start + half]
        out[:, half:] = right[:, start : start + half]
    lanes = slice(3 * half, 3 * half + 128)
    sums = (held[:, lanes] + other[:, lanes]).T
    for place, out in enumerate(outs[4:-1]):
        out[...] = sums[place : place + 1]
    height = held.shape[0]
    for fold in range(outs[-1].shape[1] // height):
        outs[-1][:, fold * height : (fold + 1) * height] = sums[SMALL + fold : SMALL + fold + 1]


def finish_body(place, core, held, other, *refs):
    finish_ff_body(place, core, held, other, *refs[4:6])
    finish_attention_body(core, *refs[:4], *refs[6:])


def finish(core, ff, terms, width, folds):
    height = terms[0].shape[0]
    ins = [scalars(core)] + [whole(a) for a in (*ff, *terms)]
    shapes = [(folds * height, width), (height, folds * width)] + [(height, width)] * 4
    shapes += [(1, height)] * SMALL + [(1, folds * height)]
    outs = [whole_out(shape, jnp.float32) for shape in shapes]
    place = lax.axis_size("seq").bit_length() - 2
    return call(functools.partial(finish_body, place), (1,), ins, outs, name="finish")


def local(
    tokens,
    image_lengths,
    cotangent,
    ln1_gain,
    ln1_bias,
    w_query,
    b_query,
    w_key,
    w_value,
    b_value,
    q_gain,
    k_gain,
    w_out,
    b_out,
    ln2_gain,
    ln2_bias,
    w_up,
    b_up,
    w_down,
    b_down,
):
    sequences, span, width = tokens.shape
    owners = lax.axis_size("seq")
    blocks = lax.axis_size("blk")
    place = lax.axis_index("blk")
    me = lax.axis_index("seq")
    first_key, second_key = (place * span, (1 - place) * span) if blocks == 2 else (place * 0, place * 0)
    bits = list(reversed(range(owners.bit_length() - 1)))
    numbers = [place & 1, place * span, first_key, second_key] + [(me >> bit) & 1 for bit in reversed(bits)]
    facts = jnp.stack(numbers).astype(jnp.int32)
    tok = tokens.reshape(-1, width)
    cot = cotangent.reshape(-1, width)

    def split(array):
        return array.reshape(array.shape[:-2] + (sequences, -1, width))

    def flat(array):
        return array.reshape(array.shape[:-3] + (-1, width))

    act_one, pair, key_norm = projections(tok, ln1_gain, ln1_bias, w_key, w_value, b_value, k_gain)
    q8, query_norm = queries(act_one, w_query, b_query, q_gain)
    q8, pair = split(q8), split(pair)
    if blocks == 2:
        pairs = [pair, swap(pair, "blk", 0)]
    else:
        pairs = [lax.all_gather(pair, "blk", axis=2, tiled=True)]
    height = width // owners
    folds = w_up.shape[1] // width
    top = owners.bit_length() - 2
    cot_far = swap(cot, "blk", 0)
    att, inverse, resid, act_two = attend(
        image_lengths, facts, b_out, ln2_gain, ln2_bias, q8, pairs, tok, w_out
    )
    act_far = swap(act_two, "blk", 0)
    up_sum, hidden_own, hidden_far, d_own, d_far, kept, *given = feed(
        height, facts, act_two, act_far, cot, cot_far, w_up, w_down, b_up
    )
    d_far = swap(d_far, "blk", 0)
    moved = [lax.ppermute(a, "seq", [(i, i ^ r) for i in range(owners)]) for r, a in enumerate(given, 1)]
    ff = RowSum(height, list(reversed(range(2, top))), [(kept, *moved)])
    dq, *rest = attend_back(
        facts,
        image_lengths,
        ln2_gain,
        q8,
        inverse,
        pairs,
        (d_own, d_far, resid, cot, w_out, flat(att)),
        given,
    )
    *rest, row_sums, d_resid, out_mine, out_theirs, mark = rest
    if blocks == 2:
        dk, dk_far, dv, dv_far = rest
        dk_far, dv_far = swap(dk_far, "blk", 0), swap(dv_far, "blk", 0)
    else:
        dk, dv = (lax.psum_scatter(a, "blk", scatter_dimension=1, tiled=True) for a in rest)
        dk_far, dv_far = jnp.zeros_like(dk), jnp.zeros_like(dv)
    dq, dk, dk_far, dv, dv_far = (flat(a) for a in (dq, dk, dk_far, dv, dv_far))
    out_own, out_far, ready = result(facts, hidden_own, hidden_far, w_down, [mark])
    out_far = swap(out_far, "blk", 0)
    out_arrived = swap(out_theirs, "blk", 0)
    sources = (act_one, dv, dv_far, w_value, dk, dk_far, key_norm, w_key, dq, query_norm, w_query, tok, d_resid)
    grad_tok, mine_q, mine_k, mine_two, *theirs, mark = project_back(
        owners, facts, (q_gain, k_gain, ln1_gain, up_sum, row_sums), sources, [ready]
    )
    arrived_q, arrived_k, arrived_two = (swap(a, "blk", 0) for a in theirs)
    one = RowSum(height, bits, [(mine_q, arrived_q), (mine_k, arrived_k)])
    two = RowSum(height, bits, [(mine_two, arrived_two), (out_mine, out_arrived)])
    one = RowSum(height, bits, [(mine_q, arrived_q), (mine_k, arrived_k)])
    two = RowSum(height, bits, [(mine_two, arrived_two), (out_mine, out_arrived)])
    given = [mark]
    for bit in range(2, top):
        given = send_all(facts, (ff,), (bit,), given, LONG)
    given = send_all(facts, (one, two), (0, 1), given)
    given = send_all(facts, (one, two), (1, 0), given)
    ff_parts, given = send_top(facts, ff, width, folds, given)
    out, mark = layer(resid, out_own, out_far, b_down, given)
    given = [*given, mark]
    rest = one.join(two)
    given = send_all(facts, (rest,), (2,), given)
    ff_held = merge(ff_parts, given)
    given = [ff_held[0]]
    for bit in range(3, top + 1):
        given = send_all(facts, (rest,), (bit,), given)
    terms = [a.reshape(height, -1) for a in rest.parts[0]]
    for bit in range(1, blocks.bit_length() - 1):
        terms = [add_low(a, swap(a, "blk", bit)) for a in terms]
    terms += [swap(a, "blk", 0) for a in terms]
    grad_down, grad_up, grad_q, grad_k, grad_v, grad_out, *vectors = finish(facts, ff_held, terms, width, folds)
    t_ln2g, t_ln2b, t_bo, t_bd, t_ln1g, t_ln1b, t_bq, t_bv, t_qg, t_kg, t_bu = (v.reshape(-1) for v in vectors)
    return (
        out.reshape(tokens.shape),
        grad_tok.reshape(tokens.shape),
        t_ln1g,
        t_ln1b,
        grad_q,
        t_bq,
        grad_k,
        grad_v,
        t_bv,
        t_qg,
        t_kg,
        grad_out,
        t_bo,
        t_ln2g,
        t_ln2b,
        grad_up,
        t_bu,
        grad_down,
        t_bd,
    )


def solution(mesh):
    return jax.shard_map(
        local,
        mesh=mesh,
        in_specs=(
            P("seq", "blk", None),
            P("seq", None),
            P("seq", "blk", None),
            P(),
            P(),
            P(),
            P(),
            P(),
            P(),
            P(),
            P(),
            P(),
            P(),
            P(),
            P(),
            P(),
            P(),
            P(),
            P(),
            P(),
        ),
        out_specs=(
            P("seq", "blk", None),
            P("seq", "blk", None),
            P("seq"),
            P("seq"),
            P("seq", None),
            P("seq"),
            P("seq", None),
            P("seq", None),
            P("seq"),
            P("seq"),
            P("seq"),
            P("seq", None),
            P("seq"),
            P("seq"),
            P("seq"),
            P("seq", None),
            P("seq"),
            P("seq", None),
            P("seq"),
        ),
        check_vma=False,
    )
```
